512 devices in a mesh: ctx: 32 (over x, y), tp: 16 (over z, core).
Axes of the slice: x: 4, y: 8, z: 8, core: 2. Of those that a mesh axis runs over, the one named last changes fastest.
Arguments:
- prefix_x: bfloat16 [8192, 8192], P('ctx', 'tp'), may hold values from -6 to 6
- prefix_z: bfloat16 [8192, 8192], P('ctx', 'tp'), may hold values from -6 to 6
- prefix_bc: bfloat16 [8192, 256], P(('ctx', 'tp')), may hold values from -6 to 6
- prefix_dt: float32 [128, 8192], P('tp', 'ctx'), may hold values from -6 to 6
- branch_x: bfloat16 [8192, 8192], P('ctx', 'tp'), may hold values from -6 to 6
- branch_z: bfloat16 [8192, 8192], P('ctx', 'tp'), may hold values from -6 to 6
- branch_bc: bfloat16 [8192, 256], P(('ctx', 'tp')), may hold values from -6 to 6
- branch_dt: float32 [128, 8192], P('tp', 'ctx'), may hold values from -6 to 6
- conv_x: bfloat16 [4, 8192], P(None, 'tp'), may hold values from -3 to 3
- conv_bc: bfloat16 [4, 256], replicated, may hold values from -3 to 3
- decay_rate: float32 [128], P('tp'), may hold values from 2.4414063e-05 to 0.03
- skip: float32 [128], P('tp'), may hold values from 0.5 to 1.5
- norm_gain: float32 [8192], P('tp'), may hold values from 0.5 to 1.5
- bound_pos: int32 [8], replicated, may hold values from 0 to 8191
- branch_owner: int32 [64], replicated, may hold values from 0 to 31, as said below
- branch_parent: int32 [64], replicated, may hold values from 0 to 7
- branch_len: int32 [64], replicated, may hold values from 1 to 255, as said below
Outputs:
- prefix_out: bfloat16 [8192, 8192], P('ctx', 'tp')
- branch_out: bfloat16 [8192, 8192], P('ctx', 'tp')
The draws below stay inside these ranges and needn't reach their ends.
Inputs may be any that keep to these rules, and one draw needn't show every extreme that they name: `branch_owner`: every block index 0 to 31 holds exactly 2 branches. `branch_len`: the branches of one block have lengths that sum to at most 256; in every draw some block's sum is exactly 256, and some branch has exactly 255 rows.
All inputs are finite; a program needn't handle non-finite values.
Results may differ from the reference program's by a relative error of at most 0.0034.
Values may be sent and summed in bfloat16 or wider, within the bound.
No kernel may reach another device: no remote copies, remote signals or barrier semaphores. Data moves between devices by JAX's collectives and lax.ppermute only.
A program may use at most 64 MiB of HBM per device.

```python
import math
import jax
import jax.numpy as jnp
from jax import lax

HEADS = 128
P_SIZE = 64
STATE = 128
CONV = 4
NORM_GROUP = 8192
PRE_DEV = 256
BR_PER = 2
NBOUND = 8
BR_DEV = 256
PREFIX = 8192
BRANCH = 8192
NBRANCH = 64
N_CTX = 32


def branch_layout(key):
    owners = NBRANCH // BR_PER
    shuffled = jax.random.permutation(jax.random.fold_in(key, 11), NBRANCH).astype(jnp.int32)
    owner_of = shuffled // BR_PER
    slot_of = shuffled % BR_PER
    levels = jax.random.randint(jax.random.fold_in(key, 12), (owners,), 1, 5)
    totals = BR_DEV * levels // 4
    full_owner = jax.random.randint(jax.random.fold_in(key, 13), (), 0, owners)
    is_full = jnp.arange(owners) == full_owner
    totals = jnp.where(is_full, BR_DEV, totals)
    shares = jax.random.randint(jax.random.fold_in(key, 14), (owners, BR_PER), 1, 5)
    first_only = (jnp.arange(BR_PER) == 0).astype(shares.dtype)
    shares = jnp.where(is_full[:, None], first_only[None, :], shares)
    share_total = jnp.sum(shares, axis=1)
    cut_points = (totals[:, None] - BR_PER) * jnp.cumsum(shares, axis=1) // share_total[:, None]
    previous = jnp.concatenate([jnp.zeros((owners, 1), cut_points.dtype), cut_points[:, :-1]], axis=1)
    lengths = cut_points - previous + 1
    return (owner_of.astype(jnp.int32), lengths[owner_of, slot_of].astype(jnp.int32))


def draw_branch_owner(key, part):
    return branch_layout(key)[0]


def draw_branch_len(key, part):
    return branch_layout(key)[1]


def place_ends(entries, rng, smallest, high):
    index_at = [jax.random.randint(jax.random.fold_in(rng, axis), (), 0, length) for axis, length in enumerate(entries.shape)]
    main_axis = entries.shape.index(max(entries.shape))
    next_to = index_at[:main_axis] + [(index_at[main_axis] + 1) % entries.shape[main_axis]] + index_at[main_axis + 1:]
    return entries.at[tuple(index_at)].set(smallest).at[tuple(next_to)].set(high)


def level_of(rng, extent, split, least, high):
    level = 1.0
    for dim, parts in split:
        steps = jax.random.uniform(jax.random.fold_in(jax.random.fold_in(rng, 6), dim), (parts,), jnp.float32, least / len(split), high / len(split))
        level = level * jnp.repeat(jnp.exp(steps), extent[dim] // parts).reshape((-1,) + (1,) * (len(extent) - 1 - dim))
    return level


def normal_values(own_key, shape, spread, most, cuts=(), kind=jnp.bfloat16):
    drawn = jax.random.normal(own_key, shape, jnp.float32) * spread
    if len(cuts) > 0:
        drawn = level_of(own_key, shape, cuts, -0.22, 0.18) * drawn
    return jnp.clip(drawn, min=-most, max=most).astype(kind)


def setup_inputs(seed: int = 0) -> dict:
    key_of = jax.random.split(jax.random.key(seed), 18)
    prefix_x = normal_values(key_of[0], (PREFIX, HEADS * P_SIZE), 1.0, 6.0, ((0, 32), (1, 16)))
    prefix_z = normal_values(key_of[1], (PREFIX, HEADS * P_SIZE), 1.0, 6.0, ((0, 32), (1, 16)))
    prefix_bc = normal_values(key_of[2], (PREFIX, 2 * STATE), 1.0, 6.0, ((0, 512),))
    prefix_dt = normal_values(key_of[3], (HEADS, PREFIX), 1.0, 6.0, ((0, 16), (1, 32)), jnp.float32)
    branch_x = normal_values(key_of[4], (BRANCH, HEADS * P_SIZE), 1.0, 6.0, ((0, 32), (1, 16)))
    branch_z = normal_values(key_of[5], (BRANCH, HEADS * P_SIZE), 1.0, 6.0, ((0, 32), (1, 16)))
    branch_bc = normal_values(key_of[6], (BRANCH, 2 * STATE), 1.0, 6.0, ((0, 512),))
    branch_dt = normal_values(key_of[7], (HEADS, BRANCH), 1.0, 6.0, ((0, 16), (1, 32)), jnp.float32)
    conv_x = normal_values(key_of[8], (CONV, HEADS * P_SIZE), CONV ** -0.5, 3.0, ((1, 16),))
    conv_bc = normal_values(key_of[9], (CONV, 2 * STATE), CONV ** -0.5, 3.0)
    decay_rate = jnp.clip(jnp.exp(math.log(0.03) - 7.1137933 * jax.random.uniform(key_of[10], (HEADS,), jnp.float32) ** level_of(key_of[10], (HEADS,), ((0, 16),), -0.2, 0.2)), 2.441406286379788e-05, 0.03)
    skip = jnp.clip(0.5 + 1.0 * jax.random.uniform(key_of[11], (HEADS,), jnp.float32) ** level_of(key_of[11], (HEADS,), ((0, 16),), -0.2, 0.2), 0.5, 1.5)
    norm_gain = jnp.clip(1.0 + 0.1 * jax.random.normal(key_of[12], (HEADS * P_SIZE,), jnp.float32), 0.5, 1.5)
    bound_pos = place_ends(jax.random.randint(key_of[13], (NBOUND,), 0, PREFIX), jax.random.fold_in(key_of[13], 1), 0, PREFIX - 1).astype(jnp.int32)
    branch_owner = draw_branch_owner(jax.random.fold_in(key_of[17], 71), 0)
    branch_parent = place_ends(jax.random.randint(key_of[15], (NBRANCH,), 0, NBOUND), jax.random.fold_in(key_of[15], 1), 0, NBOUND - 1).astype(jnp.int32)
    branch_len = draw_branch_len(jax.random.fold_in(key_of[17], 71), 0)
    return dict(prefix_x=prefix_x, prefix_z=prefix_z, prefix_bc=prefix_bc, prefix_dt=prefix_dt, branch_x=branch_x, branch_z=branch_z, branch_bc=branch_bc, branch_dt=branch_dt, conv_x=conv_x, conv_bc=conv_bc, decay_rate=decay_rate, skip=skip, norm_gain=norm_gain, bound_pos=bound_pos, branch_owner=branch_owner, branch_parent=branch_parent, branch_len=branch_len)


EPSILON = 1e-05

def conv_silu(lagged, weights):
    summed = weights[0].astype(jnp.float32)[None, :] * lagged[0].astype(jnp.float32)
    for tap_index in range(1, len(lagged)):
        summed = summed + weights[tap_index].astype(jnp.float32)[None, :] * lagged[tap_index].astype(jnp.float32)
    return jax.nn.silu(summed).astype(jnp.bfloat16)

def split_conv(convolved, channels, head_count):
    length = convolved.shape[0]
    state_size = (convolved.shape[1] - channels) // 2
    values = convolved[:, :channels].reshape(length, head_count, channels // head_count)
    return (values, convolved[:, channels:channels + state_size], convolved[:, channels + state_size:])

def decays(raw_steps, rates):
    step_size = jax.nn.softplus(raw_steps)
    log_decay = -rates[:, None] * step_size
    return (step_size, log_decay, jnp.cumsum(log_decay, axis=1))

def intra_block(values, b_rows, c_rows, step_size, cumulative, causal_mask):
    scores = jnp.dot(c_rows, b_rows.T, preferred_element_type=jnp.float32)
    exponent = jnp.where(causal_mask[None], cumulative[:, :, None] - cumulative[:, None, :], 0.0)
    mixing = jnp.where(causal_mask[None], scores[None] * jnp.exp(exponent) * step_size[:, None, :], 0.0).astype(jnp.bfloat16)
    return jnp.einsum('hts,shp->thp', mixing.astype(jnp.float32), values.astype(jnp.float32))

def local_states(values, b_rows, step_size, cumulative, positions):
    length = cumulative.shape[1]
    clipped = jnp.clip(positions, 0, length - 1).astype(jnp.int32)
    decay_end = jnp.take(cumulative, clipped, axis=1)
    row_index = jnp.arange(length, dtype=jnp.int32)
    inside = row_index[None, :] <= positions[:, None]
    exponent = jnp.where(inside[:, None, :], decay_end.T[:, :, None] - cumulative[None], 0.0)
    weight = jnp.where(inside[:, None, :], jnp.exp(exponent) * step_size[None], 0.0)
    weighted = (jnp.transpose(weight, (0, 2, 1))[:, :, :, None] * values[None].astype(jnp.float32)).astype(jnp.bfloat16)
    return jnp.einsum('jshp,sn->jhpn', weighted.astype(jnp.float32), b_rows.astype(jnp.float32))

def from_state(c_rows, state, weight):
    result = jnp.einsum('tn,hpn->thp', c_rows.astype(jnp.float32), state, precision=lax.Precision.HIGHEST)
    return result * weight.T[:, :, None]

def finish(mixed_out, values, skip, gate_rows, gain):
    length = mixed_out.shape[0]
    mixed_out = mixed_out + skip[None, :, None] * values.astype(jnp.float32)
    gated = mixed_out.reshape(length, -1) * jax.nn.silu(gate_rows.astype(jnp.float32))
    grouped = gated.reshape(length, -1, NORM_GROUP)
    factor = lax.rsqrt(lax.optimization_barrier(jnp.mean(grouped * grouped, axis=2, keepdims=True)) + EPSILON)
    return ((grouped * factor).reshape(length, -1) * gain[None, :]).astype(jnp.bfloat16)

def layout(owner_index, branch_owner, branch_parent, branch_len, length):
    owned = (branch_owner == owner_index).astype(jnp.int32)
    owned_rank = (jnp.cumsum(owned) - 1).astype(jnp.int32)
    owned_lengths = (owned * branch_len).astype(jnp.int32)
    starts = (jnp.cumsum(owned_lengths) - owned_lengths).astype(jnp.int32)
    branch_slot = jnp.arange(BR_PER, dtype=jnp.int32)
    chosen = owned[None, :] * (owned_rank[None, :] == branch_slot[:, None]).astype(jnp.int32)
    segment_length = lax.optimization_barrier(jnp.sum(chosen * branch_len[None, :], axis=1)).astype(jnp.int32)
    segment_start = lax.optimization_barrier(jnp.sum(chosen * starts[None, :], axis=1)).astype(jnp.int32)
    parents = lax.optimization_barrier(jnp.sum(chosen * branch_parent[None, :], axis=1)).astype(jnp.int32)
    row_index = jnp.arange(length, dtype=jnp.int32)
    inside = ((row_index[None, :] >= segment_start[:, None]) & (row_index[None, :] < (segment_start + segment_length)[:, None])).astype(jnp.int32)
    live_count = lax.optimization_barrier(jnp.sum(inside, axis=0)).astype(jnp.int32)
    segment = (lax.optimization_barrier(jnp.sum(inside * branch_slot[:, None], axis=0)) + BR_PER * (1 - live_count)).astype(jnp.int32)
    offset = (row_index - lax.optimization_barrier(jnp.sum(inside * segment_start[:, None], axis=0))).astype(jnp.int32)
    return (segment, offset, live_count > 0, parents)

def branch_block(joined_rows, gate_rows, raw_steps, all_states, all_tails, weights, rates, skip, gain, owner_index, branch_owner, branch_parent, branch_len):
    length, row_width = joined_rows.shape
    channels = gate_rows.shape[1]
    head_count = rates.shape[0]
    tail_count = weights.shape[0] - 1
    segment, offset, live_rows, parents = layout(owner_index, branch_owner, branch_parent, branch_len, length)
    seed_states = jnp.take(all_states, parents, axis=0)
    tail_rows = jnp.take(all_tails, parents, axis=0).reshape(-1, row_width).astype(jnp.bfloat16)
    column = jnp.arange(tail_rows.shape[0], dtype=jnp.int32)
    column_segment = column // tail_count
    column_row = column % tail_count
    lagged = []
    for tap_index in range(tail_count + 1):
        shift_rows = tail_count - tap_index
        if shift_rows == 0:
            lagged.append(joined_rows)
        else:
            shifted = jnp.concatenate([jnp.zeros((shift_rows, row_width), jnp.bfloat16), joined_rows[:length - shift_rows]], axis=0)
            local_rows = jnp.where((offset >= shift_rows)[:, None], shifted, jnp.zeros_like(shifted))
            picker = ((segment[:, None] == column_segment[None, :]) & (offset[:, None] < shift_rows) & (column_row[None, :] == tail_count - shift_rows + offset[:, None])).astype(jnp.bfloat16)
            tail_part = jnp.dot(picker, tail_rows, preferred_element_type=jnp.float32).astype(jnp.bfloat16)
            lagged.append(local_rows + tail_part)
    values, b_rows, c_rows = split_conv(conv_silu(lagged, weights), channels, head_count)
    step_size, log_decay, cumulative = decays(raw_steps, rates)
    row_index = jnp.arange(length, dtype=jnp.int32)
    causal_mask = (segment[:, None] == segment[None, :]) & live_rows[:, None] & (row_index[None, :] <= row_index[:, None])
    mixed_out = intra_block(values, b_rows, c_rows, step_size, cumulative, causal_mask)
    first_rows = jnp.clip(row_index - offset, 0, length - 1).astype(jnp.int32)
    start_log = jnp.take(cumulative - log_decay, first_rows, axis=1)
    seed_weight = jnp.where(live_rows[None, :], jnp.exp(jnp.where(live_rows[None, :], cumulative - start_log, 0.0)), 0.0)
    for branch_slot in range(seed_states.shape[0]):
        portion = from_state(c_rows, seed_states[branch_slot], seed_weight)
        mixed_out = mixed_out + jnp.where((segment == branch_slot)[:, None, None], portion, 0.0)
    result = finish(mixed_out, values, skip, gate_rows, gain)
    return jnp.where(live_rows[:, None], result, jnp.zeros_like(result))

def reference(prefix_x, prefix_z, prefix_bc, prefix_dt, branch_x, branch_z, branch_bc, branch_dt, conv_x, conv_bc, decay_rate, skip, norm_gain, bound_pos, branch_owner, branch_parent, branch_len):
    length = PRE_DEV
    channels = HEADS * P_SIZE
    weights = jnp.concatenate([conv_x, conv_bc], axis=1)
    tail_count = weights.shape[0] - 1
    joined_rows = jnp.concatenate([prefix_x, prefix_bc], axis=1)
    padded = jnp.concatenate([jnp.zeros((tail_count, joined_rows.shape[1]), jnp.bfloat16), joined_rows], axis=0)
    row_index = jnp.arange(length, dtype=jnp.int32)
    causal_mask = row_index[None, :] <= row_index[:, None]
    last_row = jnp.full((1,), length - 1, jnp.int32)

    def prepare(block_index):
        extended = lax.dynamic_slice_in_dim(padded, block_index * length, length + tail_count, 0)
        lagged = [extended[tap_index:tap_index + length] for tap_index in range(tail_count + 1)]
        values, b_rows, c_rows = split_conv(conv_silu(lagged, weights), channels, HEADS)
        step_size, log_decay, cumulative = decays(lax.dynamic_slice_in_dim(prefix_dt, block_index * length, length, 1), decay_rate)
        return (extended, values, b_rows, c_rows, step_size, cumulative)

    def block(state, block_index):
        extended, values, b_rows, c_rows, step_size, cumulative = prepare(block_index)
        mixed_out = intra_block(values, b_rows, c_rows, step_size, cumulative, causal_mask)
        mixed_out = mixed_out + from_state(c_rows, state, jnp.exp(cumulative))
        gate_rows = lax.dynamic_slice_in_dim(prefix_z, block_index * length, length, 0)
        result = finish(mixed_out, values, skip, gate_rows, norm_gain)
        end_state = local_states(values, b_rows, step_size, cumulative, last_row)[0]
        return (jnp.exp(cumulative[:, -1])[:, None, None] * state + end_state, (result, state))
    initial = jnp.zeros((HEADS, P_SIZE, STATE), jnp.float32)
    unused, (outputs, entering) = lax.scan(block, initial, jnp.arange(N_CTX, dtype=jnp.int32))
    prefix_out = outputs.reshape(PREFIX, channels)

    def boundary(which):
        position = bound_pos[which]
        block_index = (position // length).astype(jnp.int32)
        local_at = (position - block_index * length).astype(jnp.int32)
        extended, values, b_rows, unused_rows, step_size, cumulative = prepare(block_index)
        states = local_states(values, b_rows, step_size, cumulative, local_at[None])[0]
        decay_at = jnp.exp(jnp.take(cumulative, local_at[None], axis=1))[:, 0]
        joined = decay_at[:, None, None] * entering[block_index] + states
        tail = lax.dynamic_slice_in_dim(extended, local_at + 1, tail_count, 0).astype(jnp.float32)
        return (joined, tail)
    all_states, all_tails = lax.map(boundary, jnp.arange(NBOUND, dtype=jnp.int32))
    branch_joined = jnp.concatenate([branch_x, branch_bc], axis=1)

    def owner_block(owner_index):
        rows = lax.dynamic_slice_in_dim(branch_joined, owner_index * BR_DEV, BR_DEV, 0)
        gates = lax.dynamic_slice_in_dim(branch_z, owner_index * BR_DEV, BR_DEV, 0)
        raw_steps = lax.dynamic_slice_in_dim(branch_dt, owner_index * BR_DEV, BR_DEV, 1)
        return branch_block(rows, gates, raw_steps, all_states, all_tails, weights, decay_rate, skip, norm_gain, owner_index, branch_owner, branch_parent, branch_len)
    branch_out = lax.map(owner_block, jnp.arange(N_CTX, dtype=jnp.int32)).reshape(BRANCH, channels)
    return (prefix_out, branch_out)
```

```python
import jax
import jax.numpy as jnp
from jax import lax
from jax.sharding import PartitionSpec as P

BR_PER = 2
EPSILON = 1e-05
SLOTS = 8
BF = jnp.bfloat16
F32 = jnp.float32
HIGH = lax.Precision.HIGHEST


def conv_silu(lagged, weights):
    summed = weights[0].astype(F32)[None, :] * lagged[0].astype(F32)
    for tap in range(1, len(lagged)):
        summed = summed + weights[tap].astype(F32)[None, :] * lagged[tap].astype(F32)
    return jax.nn.silu(summed).astype(BF)


def split_conv(convolved, channels, heads):
    length = convolved.shape[0]
    state = (convolved.shape[1] - channels) // 2
    values = convolved[:, :channels].reshape(length, heads, channels // heads)
    return values, convolved[:, channels : channels + state], convolved[:, channels + state :]


def decays(raw_steps, rates):
    length = raw_steps.shape[1]
    step = jax.nn.softplus(raw_steps)
    log_decay = -rates[:, None] * step
    index = jnp.arange(length, dtype=jnp.int32)
    upper = (index[:, None] <= index[None, :]).astype(F32)
    return step, log_decay, jnp.dot(log_decay, upper, precision=HIGH)


def intra(values, b_rows, c_rows, step, cumulative, mask):
    scores = jnp.dot(c_rows, b_rows.T, preferred_element_type=F32)
    exponent = jnp.where(mask[None], cumulative[:, :, None] - cumulative[:, None, :], 0.0)
    mixing = jnp.where(mask[None], scores[None] * jnp.exp(exponent) * step[:, None, :], 0.0)
    return jnp.einsum("hts,shp->thp", mixing.astype(BF), values, preferred_element_type=F32)


def pick(array, positions):
    index = jnp.arange(array.shape[1], dtype=jnp.int32)
    hit = index[None, None, :] == positions[:, None, None]
    return jnp.sum(jnp.where(hit, array[None], 0.0), axis=2)


def local_states(values, b_rows, step, cumulative, positions):
    length = cumulative.shape[1]
    ends = pick(cumulative, positions)
    row = jnp.arange(length, dtype=jnp.int32)
    inside = (row[None, :] <= positions[:, None])[:, None, :]
    exponent = jnp.where(inside, ends[:, :, None] - cumulative[None], 0.0)
    weight = jnp.where(inside, jnp.exp(exponent) * step[None], 0.0)
    weighted = (jnp.transpose(weight, (0, 2, 1))[:, :, :, None] * values[None].astype(F32)).astype(BF)
    states = jnp.einsum("jshp,sn->jhpn", weighted, b_rows, preferred_element_type=F32)
    return states, ends


def from_state(c_rows, state, weight):
    result = jnp.einsum("tn,hpn->thp", c_rows, state, preferred_element_type=F32)
    return result * weight.T[:, :, None]


def parts_of(value, count):
    found = []
    for _ in range(count):
        part = lax.reduce_precision(value, 8, 7)
        found.append(part.astype(BF))
        value = value - part
    return found


def body(
    prefix_x, prefix_z, prefix_bc, prefix_dt, branch_x, branch_z, branch_bc, branch_dt,
    conv_x, conv_bc, decay_rate, skip, norm_gain, bound_pos, branch_owner, branch_parent, branch_len,
):
    n_ctx = lax.axis_size("ctx")
    me = lax.axis_index("ctx")
    length, channels = prefix_x.shape
    heads = decay_rate.shape[0]
    width = prefix_bc.shape[1]
    n_state = width // 2
    bounds = bound_pos.shape[0]
    branches = branch_owner.shape[0]
    weights = jnp.concatenate([conv_x, conv_bc], axis=1)
    taps = weights.shape[0]
    tail = taps - 1
    row_width = channels + width

    gathered = lax.all_gather(jnp.concatenate([prefix_bc, branch_bc], axis=1), "tp", axis=0, tiled=True)
    joined = jnp.concatenate([prefix_x, gathered[:, :width]], axis=1)
    before = lax.ppermute(joined[length - tail :], "ctx", [(i, i + 1) for i in range(n_ctx - 1)])
    extended = jnp.concatenate([before, joined], axis=0)
    lagged = [extended[tap : tap + length] for tap in range(taps)]
    values, b_rows, c_rows = split_conv(conv_silu(lagged, weights), channels, heads)
    step, _, cumulative = decays(prefix_dt, decay_rate)

    block_of = bound_pos // length
    at = bound_pos - block_of * length
    order = jnp.arange(bounds, dtype=jnp.int32)
    slot_of = jnp.sum(
        ((block_of[:, None] == block_of[None, :]) & (order[None, :] < order[:, None])).astype(jnp.int32), axis=1
    )
    border = jnp.arange(branches, dtype=jnp.int32)
    same = branch_owner[:, None] == branch_owner[None, :]
    earlier = same & (border[None, :] < border[:, None])
    rank = jnp.sum(earlier.astype(jnp.int32), axis=1)
    start = jnp.sum(jnp.where(earlier, branch_len[None, :], 0), axis=1)
    place = jnp.arange(n_ctx * BR_PER, dtype=jnp.int32)
    chosen = place[:, None] == (branch_owner * BR_PER + rank)[None, :]
    parent_of = jnp.sum(jnp.where(chosen, branch_parent[None, :], 0), axis=1)
    mine = (me * BR_PER + jnp.arange(BR_PER, dtype=jnp.int32))[:, None] == (branch_owner * BR_PER + rank)[None, :]
    my_len = jnp.sum(jnp.where(mine, branch_len[None, :], 0), axis=1)
    my_start = jnp.sum(jnp.where(mine, start[None, :], 0), axis=1)

    slot_here = (block_of == me)[None, :] & (slot_of[None, :] == jnp.arange(SLOTS, dtype=jnp.int32)[:, None])
    positions = jnp.sum(jnp.where(slot_here, at[None, :] + 1, 0), axis=1) - 1
    positions = jnp.concatenate([jnp.full((1,), length - 1, jnp.int32), positions])
    states, ends = local_states(values, b_rows, step, cumulative, positions)
    slices = states.reshape(SLOTS + 1, n_ctx, -1, n_state)
    rows = slices.shape[2]
    end_hi, end_lo = parts_of(slices[0], 2)
    partial = jnp.transpose(slices[1:].astype(BF), (1, 0, 2, 3)).reshape(n_ctx, SLOTS * rows, n_state)
    per_head = jnp.repeat(jnp.pad(ends.T, ((0, 0), (0, n_state - SLOTS - 1))), n_ctx // heads, axis=0)
    logs = jnp.stack(parts_of(per_head, 3), axis=1)
    parent_hit = parent_of[:, None] == order[None, :]
    parent_at = jnp.sum(jnp.where(parent_hit, at[None, :], 0), axis=1)
    parent_block = jnp.sum(jnp.where(parent_hit, block_of[None, :], 0), axis=1)
    wanted = parent_at[:, None] + 1 + jnp.arange(tail, dtype=jnp.int32)[None, :]
    wanted = jnp.where((parent_block == me)[:, None], wanted, -1).reshape(-1)
    picker = (wanted[:, None] == jnp.arange(length + tail, dtype=jnp.int32)[None, :]).astype(BF)
    tails = jnp.dot(picker, extended, preferred_element_type=F32).astype(BF)
    tails = tails.reshape(n_ctx, BR_PER * tail * row_width // n_state, n_state)
    pieces = [end_hi, end_lo, partial, tails, logs]
    sent = jnp.concatenate(pieces, axis=1)
    sent = jnp.pad(sent, ((0, 0), (0, -sent.shape[1] % 16), (0, 0)))
    got = lax.all_to_all(sent, "ctx", 0, 0, tiled=True)

    edges = [0]
    for piece in pieces:
        edges.append(edges[-1] + piece.shape[1])
    end_hi, end_lo, partial, tails, logs = [
        got[:, first:last].astype(F32) for first, last in zip(edges[:-1], edges[1:], strict=True)
    ]
    ends = jnp.sum(logs, axis=1)[:, : SLOTS + 1]
    block = jnp.arange(n_ctx, dtype=jnp.int32)
    totals = jnp.sum(jnp.where(block[None, :] <= block[:, None], ends[:, 0][None, :], 0.0), axis=1)
    gap = (totals - ends[:, 0])[:, None] - totals[None, :]
    earlier_block = block[None, :] < block[:, None]
    carry = jnp.where(earlier_block, jnp.exp(jnp.where(earlier_block, gap, 0.0)), 0.0)
    entering = jnp.dot(carry, (end_hi + end_lo).reshape(n_ctx, -1), precision=HIGH)
    held = block[None, :] == block_of[:, None]
    bound_end = jnp.sum(
        jnp.where(
            held[:, :, None] & (slot_of[:, None, None] == jnp.arange(SLOTS, dtype=jnp.int32)[None, None, :]),
            ends[None, :, 1:],
            0.0,
        ),
        axis=(1, 2),
    )
    choose = jnp.where(held, jnp.exp(bound_end)[:, None], 0.0)
    slot_pick = (
        held[:, :, None] & (slot_of[:, None, None] == jnp.arange(SLOTS, dtype=jnp.int32)[None, None, :])
    ).reshape(bounds, -1)
    bound_state = jnp.dot(choose, entering, precision=HIGH) + jnp.dot(
        slot_pick.astype(BF), partial.astype(BF).reshape(n_ctx * SLOTS, -1), preferred_element_type=F32
    )
    seeds = jnp.dot(parent_hit.astype(F32), bound_state, precision=HIGH).reshape(n_ctx, BR_PER * rows, n_state)
    back = jnp.concatenate([entering.reshape(n_ctx, rows, n_state), seeds], axis=1).astype(BF)
    back = lax.all_to_all(back, "ctx", 0, 0, tiled=True)

    row = jnp.arange(length, dtype=jnp.int32)
    mixed = intra(values, b_rows, c_rows, step, cumulative, row[None, :] <= row[:, None])

    inside = (row[None, :] >= my_start[:, None]) & (row[None, :] < (my_start + my_len)[:, None])
    live = inside[0] | inside[1]
    segment = jnp.where(inside[0], 0, jnp.where(inside[1], 1, BR_PER))
    offset = row - jnp.sum(jnp.where(inside, my_start[:, None], 0), axis=0)
    tail_rows = jnp.sum(tails, axis=0).astype(BF).reshape(BR_PER * tail, row_width)
    branch_joined = jnp.concatenate([branch_x, gathered[:, width:]], axis=1)
    column = jnp.arange(BR_PER * tail, dtype=jnp.int32)
    lagged = []
    for shift in range(tail, 0, -1):
        shifted = jnp.concatenate(
            [jnp.zeros((shift, row_width), BF), branch_joined[: length - shift]], axis=0
        )
        local = jnp.where((offset >= shift)[:, None], shifted, jnp.zeros_like(shifted))
        picker = (
            (segment[:, None] == (column // tail)[None, :])
            & (offset[:, None] < shift)
            & ((column % tail)[None, :] == tail - shift + offset[:, None])
        ).astype(BF)
        lagged.append(local + jnp.dot(picker, tail_rows, preferred_element_type=F32).astype(BF))
    lagged.append(branch_joined)
    b_values, b_b, b_c = split_conv(conv_silu(lagged, weights), channels, heads)
    b_step, b_log, b_cum = decays(branch_dt, decay_rate)
    mask = (segment[:, None] == segment[None, :]) & live[:, None] & (row[None, :] <= row[:, None])
    b_mixed = intra(b_values, b_b, b_c, b_step, b_cum, mask)
    starts = pick(b_cum - b_log, my_start)
    gap = b_cum - jnp.where(inside[0][None, :], starts[0][:, None], starts[1][:, None])
    seed_weight = jnp.where(live[None, :], jnp.exp(jnp.where(live[None, :], gap, 0.0)), 0.0)

    shape = (heads, channels // heads, n_state)
    mixed = mixed + from_state(c_rows, back[:, :rows].reshape(shape), jnp.exp(cumulative))
    for slot in range(BR_PER):
        seed = back[:, (slot + 1) * rows : (slot + 2) * rows].reshape(shape)
        b_mixed = b_mixed + from_state(b_c, seed, jnp.where(inside[slot][None, :], seed_weight, 0.0))

    def gate(mixed, values, z):
        mixed = mixed + skip[None, :, None] * values.astype(F32)
        gated = mixed.reshape(length, -1) * jax.nn.silu(z.astype(F32))
        return gated, jnp.sum(gated * gated, axis=1)

    gated, squares = gate(mixed, values, prefix_z)
    b_gated, b_squares = gate(b_mixed, b_values, branch_z)
    every = lax.all_gather(jnp.stack([squares, b_squares])[None], "tp", axis=0, tiled=True)
    factor = lax.rsqrt(jnp.sum(every, axis=0) / (channels * lax.axis_size("tp")) + EPSILON)
    prefix_out = (gated * factor[0][:, None] * norm_gain[None, :]).astype(BF)
    branch_out = (b_gated * factor[1][:, None] * norm_gain[None, :]).astype(BF)
    return prefix_out, jnp.where(live[:, None], branch_out, jnp.zeros_like(branch_out))


def solution(mesh):
    both = P(("ctx", "tp"), None)
    in_specs = (
        P("ctx", "tp"), P("ctx", "tp"), both, P("tp", "ctx"),
        P("ctx", "tp"), P("ctx", "tp"), both, P("tp", "ctx"),
        P(None, "tp"), P(), P("tp"), P("tp"), P("tp"), P(), P(), P(), P(),
    )
    out_specs = (P("ctx", "tp"), P("ctx", "tp"))
    return jax.shard_map(body, mesh=mesh, in_specs=in_specs, out_specs=out_specs, check_vma=False)
```

```python
import functools

import jax
import jax.numpy as jnp
from jax import lax
from jax.experimental import pallas as pl
from jax.experimental.pallas import tpu as pltpu
from jax.sharding import PartitionSpec as P

BR_PER = 2
EPSILON = 1e-05
SLOTS = 2
MISC = 48
HALO = 16
BF = jnp.bfloat16
F32 = jnp.float32
I32 = jnp.int32
HIGH = lax.Precision.HIGHEST
FAR = -1e30


def iota(shape, axis):
    return lax.broadcasted_iota(I32, shape, axis)


def log_row(value, part):
    at = 3 * value + part
    return (at // 2) * 8 + 6 + at % 2


def parts_of(value, count):
    found = []
    for _ in range(count):
        part = value.astype(BF)
        found.append(part)
        value = value - part.astype(F32)
    return found


def expand(columns, head_size):
    rows, heads = columns.shape
    low = iota((rows, 2 * head_size), 1) < head_size
    pairs = [
        jnp.where(low, columns[:, h : h + 1], columns[:, h + 1 : h + 2]) for h in range(0, heads, 2)
    ]
    return jnp.concatenate(pairs, axis=1)


def step_and_logs(raw, rates):
    step = jnp.maximum(raw, 0.0) + jnp.log1p(jnp.exp(-jnp.abs(raw)))
    log_decay = -rates * step
    length = raw.shape[1]
    upper = (iota((length, length), 0) <= iota((length, length), 1)).astype(F32)
    cumulative = jnp.dot(log_decay, upper, precision=HIGH, preferred_element_type=F32)
    return step, log_decay, cumulative


def silu(value):
    return value * jax.nn.sigmoid(value)


def mixed_rows(values, scores, step, cumulative, mask, out_ref, extra):
    length, channels = values.shape
    heads = step.shape[0]
    size = channels // heads
    columns = cumulative.T
    half = length // 2
    low = iota((half, 2 * size), 1) < size
    for first, width in ((0, half), (half, length)):
        rows = slice(first, first + half)
        kept = mask[rows, :width]
        score = scores[rows, :width]
        for h in range(0, heads, 2):
            lanes = slice(h * size, (h + 2) * size)
            sums = []
            for one in (h, h + 1):
                gap = columns[rows, one : one + 1] - cumulative[one : one + 1, :width]
                mixing = score * jnp.exp(jnp.where(kept, gap, FAR)) * step[one : one + 1, :width]
                sums.append(jnp.dot(mixing.astype(BF), values[:width, lanes], preferred_element_type=F32))
            out_ref[rows, lanes] = jnp.where(low, sums[0], sums[1]) + extra[rows, lanes]


def prefix_x_kernel(x_ref, halo_ref, dt_ref, rate_ref, taps_ref, xc_ref, cum_ref, step_ref, ext_ref):
    length = x_ref.shape[0]
    ext_ref[:HALO] = halo_ref[...].astype(F32)
    ext_ref[HALO:] = x_ref[...].astype(F32)
    taps = taps_ref[...].astype(F32)
    count = taps.shape[0]
    total = taps[0:1] * ext_ref[HALO - count + 1 : HALO - count + 1 + length]
    for i in range(1, count):
        first = HALO - count + 1 + i
        total = total + taps[i : i + 1] * ext_ref[first : first + length]
    xc_ref[...] = silu(total).astype(BF)
    step, _, cumulative = step_and_logs(dt_ref[...], rate_ref[...])
    cum_ref[...] = cumulative
    step_ref[...] = step


def prefix_state_kernel(
    meta_ref, wanted_ref, x_ref, halo_ref, bc_ref, bchalo_ref, taps_ref, xc_ref, cum_ref, step_ref,
    sent_ref, b_ref, c_ref, ext_ref, all_ref, *, base,
):
    length, channels = x_ref.shape
    width = bchalo_ref.shape[1]
    n_state = width // 2
    n_ctx = sent_ref.shape[0]
    heads = cum_ref.shape[0]
    bc = bc_ref[:, :width]
    ext_ref[:HALO] = bchalo_ref[...].astype(F32)
    ext_ref[HALO:] = bc.astype(F32)
    taps = taps_ref[...].astype(F32)
    count = taps.shape[0]
    total = taps[0:1] * ext_ref[HALO - count + 1 : HALO - count + 1 + length]
    for i in range(1, count):
        first = HALO - count + 1 + i
        total = total + taps[i : i + 1] * ext_ref[first : first + length]
    convolved = silu(total).astype(BF)
    b_rows = convolved[:, :n_state]
    b_ref[...] = b_rows
    c_ref[...] = convolved[:, n_state:]
    cumulative = cum_ref[...]
    step = step_ref[...]
    values = xc_ref[...].astype(F32)
    lane = iota((heads, length), 1)
    size = channels // heads

    def state(weight):
        weighted = (values * expand(weight.T, size)).astype(BF)
        return lax.dot_general(
            weighted, b_rows, (((0,), (0,)), ((), ())), preferred_element_type=F32
        )

    ends = [cumulative[:, length - 1 :]]
    local = state(jnp.exp(ends[0] - cumulative) * step)
    rows = channels // n_ctx
    for i, part in enumerate(parts_of(local, 2)):
        first = MISC + i * rows
        sent_ref[:, first : first + rows, :] = part.reshape(n_ctx, rows, n_state)
    for slot in range(SLOTS):
        position = meta_ref[base + slot]
        first = MISC + (2 + slot) * rows
        end = jnp.sum(jnp.where(lane == position, cumulative, 0.0), axis=1, keepdims=True)
        ends.append(end)

        @pl.when(position >= 0)
        def _():
            weight = jnp.exp(jnp.where(lane <= position, end - cumulative, FAR)) * step
            sent_ref[:, first : first + rows, :] = state(weight).astype(BF).reshape(n_ctx, rows, n_state)

        @pl.when(position < 0)
        def _():
            sent_ref[:, first : first + rows, :] = jnp.zeros((n_ctx, rows, n_state), BF)

    parts = [part for end in ends for part in parts_of(end, 3)]
    blank = jnp.zeros((heads, n_state), BF)
    groups = (channels + width) // n_state
    for g in range(groups):
        for k in range(2):
            at = 2 * g + k
            block = blank
            if at < len(parts):
                block = jnp.broadcast_to(parts[at].astype(F32), (heads, n_state)).astype(BF)
            first = HALO + length + k * heads
            all_ref[first : first + heads, g * n_state : (g + 1) * n_state] = block.astype(F32)
    all_ref[:HALO, :channels] = halo_ref[...].astype(F32)
    all_ref[:HALO, channels:] = bchalo_ref[...].astype(F32)
    all_ref[HALO : HALO + length, :channels] = x_ref[...].astype(F32)
    all_ref[HALO : HALO + length, channels:] = bc.astype(F32)
    depth = all_ref.shape[0]
    column = iota((n_ctx * 8, depth), 1)
    picker = (column == wanted_ref[...]).astype(BF)
    placed = jnp.dot(picker, all_ref[...].astype(BF), preferred_element_type=F32)
    for g in range(0, groups, 2):
        pair = [
            placed[:, (g + k) * n_state : (g + k + 1) * n_state].reshape(n_ctx, 8, n_state) for k in range(2)
        ]
        sent_ref[:, g * 8 : g * 8 + 16, :] = jnp.concatenate(pair, axis=1).astype(BF)


def prefix_mix_kernel(xc_ref, b_ref, c_ref, cum_ref, step_ref, skip_ref, y_ref):
    length = xc_ref.shape[0]
    scores = lax.dot_general(
        c_ref[...], b_ref[...], (((1,), (1,)), ((), ())), preferred_element_type=F32
    )
    mask = iota((length, length), 1) <= iota((length, length), 0)
    values = xc_ref[...]
    extra = values.astype(F32) * skip_ref[...]
    mixed_rows(values, scores, step_ref[...], cum_ref[...], mask, y_ref, extra)


def scan_kernel(meta_ref, got_ref, *rest, n_branch, bounds):
    extra_ref = rest[0] if len(rest) == 4 else None
    back_ref, entering_ref, bound_ref = rest[-3:]
    n_ctx, _, n_state = got_ref.shape
    rows = entering_ref.shape[1]

    def log_of(misc, value):
        found = [misc[r : r + 1] for r in (log_row(value, k) for k in range(3))]
        return found[0] + found[1] + found[2]

    state = jnp.zeros((rows, n_state), F32)
    for i in range(n_ctx):
        entering_ref[i] = state
        back_ref[i, :rows, :] = state.astype(BF)
        if i < n_ctx - 1:
            misc = got_ref[i, :16, :].astype(F32)
            local = got_ref[i, MISC : MISC + rows, :].astype(F32)
            local = local + got_ref[i, MISC + rows : MISC + 2 * rows, :].astype(F32)
            state = jnp.exp(log_of(misc, 0)) * state + local
    for j in range(bounds):
        block = meta_ref[n_branch + j]
        slot = meta_ref[n_branch + bounds + j]
        misc = got_ref[block, :MISC, :].astype(F32)
        log, part = log_of(misc, 1), got_ref[block, MISC + 2 * rows : MISC + 3 * rows, :].astype(F32)
        for other in range(1, SLOTS):
            first = MISC + (2 + other) * rows
            log = jnp.where(slot == other, log_of(misc, 1 + other), log)
            part = jnp.where(slot == other, got_ref[block, first : first + rows, :].astype(F32), part)
        if extra_ref is not None:
            tail = extra_ref[block, (bounds - SLOTS) * rows :, :].astype(F32)
            for more in range(bounds - SLOTS):
                here = slot == SLOTS + more
                three = tail[3 * more : 3 * more + 1] + tail[3 * more + 1 : 3 * more + 2] + tail[3 * more + 2 : 3 * more + 3]
                log = jnp.where(here, three, log)
                part = jnp.where(here, extra_ref[block, more * rows : (more + 1) * rows, :].astype(F32), part)
        bound_ref[j] = jnp.exp(log) * entering_ref[block] + part
    for o in range(n_ctx):
        for k in range(BR_PER):
            first = (1 + k) * rows
            back_ref[o, first : first + rows, :] = bound_ref[meta_ref[o * BR_PER + k]].astype(BF)


def segments(meta_ref, base, shape, axis):
    row = iota(shape, axis)
    segment = jnp.full(shape, BR_PER, I32)
    offset = row
    for k in range(BR_PER):
        start, size = meta_ref[base + k], meta_ref[base + BR_PER + k]
        inside = (row >= start) & (row < start + size)
        segment = jnp.where(inside, k, segment)
        offset = jnp.where(inside, row - start, offset)
    return segment, offset


def branch_kernel(
    meta_ref, x_ref, bc_ref, got_ref, dt_ref, rate_ref, xtaps_ref, taps_ref, skip_ref,
    y_ref, c_ref, seed_ref, ext_ref, *, base,
):
    length, channels = x_ref.shape
    n_ctx, _, n_state = got_ref.shape
    width = taps_ref.shape[1]
    ext_ref[:HALO] = jnp.zeros((HALO, channels + width), F32)
    ext_ref[HALO:, :channels] = x_ref[...].astype(F32)
    ext_ref[HALO:, channels:] = bc_ref[:, width:].astype(F32)
    misc = got_ref[0].astype(F32)
    for i in range(1, n_ctx):
        misc = misc + got_ref[i].astype(F32)
    groups = (channels + width) // n_state
    tails = jnp.concatenate([misc[g * 8 : (g + 1) * 8] for g in range(groups)], axis=1)
    tails = jnp.concatenate([tails, jnp.zeros_like(tails)], axis=0).astype(BF)
    taps = jnp.concatenate([xtaps_ref[...].astype(F32), taps_ref[...].astype(F32)], axis=1)
    count = taps.shape[0]
    tail = count - 1
    segment, offset = segments(meta_ref, base, (length, 1), 0)
    place = iota((length, 16), 1)
    total = None
    for i in range(count):
        shift = tail - i
        rows = ext_ref[HALO - shift : HALO - shift + length]
        if shift:
            ahead = (offset < shift) & (segment < BR_PER)
            picker = ahead & (place == segment * tail + tail - shift + offset)
            early = jnp.dot(picker.astype(BF), tails, preferred_element_type=F32)
            rows = jnp.where(offset >= shift, rows, 0.0) + early
        term = taps[i : i + 1] * rows
        total = term if total is None else total + term
    convolved = silu(total).astype(BF)
    values = convolved[:, :channels]
    b_rows = convolved[:, channels : channels + n_state]
    c_rows = convolved[:, channels + n_state :]
    c_ref[...] = c_rows
    step, log_decay, cumulative = step_and_logs(dt_ref[...], rate_ref[...])
    across, _ = segments(meta_ref, base, (1, length), 1)
    lane = iota(cumulative.shape, 1)
    before = cumulative - log_decay
    seed = jnp.zeros_like(cumulative)
    for k in range(BR_PER):
        first = jnp.sum(jnp.where(lane == meta_ref[base + k], before, 0.0), axis=1, keepdims=True)
        seed = jnp.where(across == k, jnp.exp(jnp.where(across == k, cumulative - first, 0.0)), seed)
    seed_ref[...] = seed
    scores = lax.dot_general(c_rows, b_rows, (((1,), (1,)), ((), ())), preferred_element_type=F32)
    mask = (segment == across) & (segment < BR_PER)
    mask = mask & (iota((length, length), 1) <= iota((length, length), 0))
    extra = values.astype(F32) * skip_ref[...]
    mixed_rows(values, scores, step, cumulative, mask, y_ref, extra)


def gate_kernel(
    meta_ref, y_ref, c_ref, cum_ref, z_ref, by_ref, bc_ref, seed_ref, bz_ref, back_ref,
    g_ref, bg_ref, sq_ref, *, base,
):
    length, channels = y_ref.shape
    heads = cum_ref.shape[0]
    size = channels // heads
    n_ctx, _, n_state = back_ref.shape
    rows = channels // n_ctx

    def from_state(c_rows, which):
        state = back_ref[:, which * rows : (which + 1) * rows, :].reshape(channels, n_state)
        return lax.dot_general(c_rows, state, (((1,), (1,)), ((), ())), preferred_element_type=F32)

    def squares(gated):
        ones = jnp.ones((8, channels), F32)
        return lax.dot_general(
            ones, gated * gated, (((1,), (1,)), ((), ())), precision=HIGH, preferred_element_type=F32
        )

    y = y_ref[...] + expand(jnp.exp(cum_ref[...]).T, size) * from_state(c_ref[...], 0)
    gated = y * silu(z_ref[...].astype(F32))
    g_ref[...] = gated
    sums = squares(gated)
    segment, _ = segments(meta_ref, base, (length, 1), 0)
    c_rows = bc_ref[...]
    seeded = from_state(c_rows, BR_PER)
    for k in range(BR_PER - 1):
        seeded = jnp.where(segment == k, from_state(c_rows, 1 + k), seeded)
    y = by_ref[...] + expand(seed_ref[...].T, size) * seeded
    gated = y * silu(bz_ref[...].astype(F32))
    bg_ref[...] = gated
    more = squares(gated)
    half = length // 2
    row = iota((8, half), 0)
    packed = jnp.where(
        row == 0,
        sums[:, :half],
        jnp.where(row == 1, sums[:, half:], jnp.where(row == 2, more[:, :half], more[:, half:])),
    )
    for i in range(sq_ref.shape[0]):
        sq_ref[i] = packed


def norm_kernel(meta_ref, sq_ref, g_ref, bg_ref, gain_ref, out_ref, bout_ref, *, base):
    length, channels = g_ref.shape
    n_tp = sq_ref.shape[0]
    total = sq_ref[0]
    for i in range(1, n_tp):
        total = total + sq_ref[i]
    factor = lax.rsqrt(total / (channels * n_tp) + EPSILON).T
    gain = gain_ref[...]
    half = length // 2
    segment, _ = segments(meta_ref, base, (length, 1), 0)
    for k in range(2):
        rows = slice(k * half, (k + 1) * half)
        out_ref[rows] = (g_ref[rows] * factor[:, k : k + 1] * gain).astype(BF)
        scaled = bg_ref[rows] * factor[:, 2 + k : 3 + k] * gain
        bout_ref[rows] = jnp.where(segment[rows] < BR_PER, scaled, 0.0).astype(BF)


def call(kernel, outs, scratch, args, smem=0, blocks=None):
    blocks = blocks or {}
    specs = []
    for i in range(len(args)):
        if i < smem:
            specs.append(pl.BlockSpec(memory_space=pltpu.SMEM))
        elif i in blocks:
            specs.append(pl.BlockSpec(blocks[i], lambda _, n=len(blocks[i]): (0,) * n))
        else:
            specs.append(pl.BlockSpec(args[i].shape, lambda _, n=args[i].ndim: (0,) * n))
    return pl.pallas_call(
        kernel,
        grid=(1,),
        in_specs=specs,
        out_specs=[pl.BlockSpec(s, lambda _, n=len(s): (0,) * n) for s, _ in outs],
        out_shape=[jax.ShapeDtypeStruct(s, t) for s, t in outs],
        scratch_shapes=[pltpu.VMEM(s, t) for s, t in scratch],
        compiler_params=pltpu.CompilerParams(vmem_limit_bytes=48 * 2**20),
        cost_estimate=pl.CostEstimate(flops=2 * 10**9, bytes_accessed=4 * 10**6, transcendentals=10**6),
    )(*args)


def more_states(xc, b_rows, step, cumulative, positions, n_ctx):
    length, channels = xc.shape
    heads = step.shape[0]
    n_state = b_rows.shape[1]
    row = jnp.arange(length, dtype=I32)
    hit = row[None, None, :] == positions[:, None, None]
    ends = jnp.sum(jnp.where(hit, cumulative[None], 0.0), axis=2)
    inside = (row[None, :] <= positions[:, None])[:, None, :]
    weight = jnp.exp(jnp.where(inside, ends[:, :, None] - cumulative[None], FAR)) * step[None]
    values = xc.reshape(length, heads, -1).astype(F32)
    weighted = (jnp.transpose(weight, (0, 2, 1))[:, :, :, None] * values[None]).astype(BF)
    states = jnp.einsum("jshp,sn->jhpn", weighted, b_rows, preferred_element_type=F32).astype(BF)
    rows = channels // n_ctx
    count = positions.shape[0]
    states = jnp.transpose(states.reshape(count, n_ctx, rows, n_state), (1, 0, 2, 3))
    parts = []
    rest = ends
    for _ in range(3):
        part = lax.reduce_precision(rest, 8, 7)
        parts.append(part)
        rest = rest - part
    logs = jnp.stack(parts, axis=1).reshape(3 * count, heads).T
    logs = jnp.repeat(logs, n_ctx // heads, axis=0)
    logs = jnp.broadcast_to(logs[:, :, None], (n_ctx, 3 * count, n_state)).astype(BF)
    sent = jnp.concatenate([states.reshape(n_ctx, count * rows, n_state), logs], axis=1)
    return jnp.pad(sent, ((0, 0), (0, -sent.shape[1] % 16), (0, 0)))


def body(
    prefix_x, prefix_z, prefix_bc, prefix_dt, branch_x, branch_z, branch_bc, branch_dt,
    conv_x, conv_bc, decay_rate, skip, norm_gain, bound_pos, branch_owner, branch_parent, branch_len,
):
    n_ctx = lax.axis_size("ctx")
    n_tp = lax.axis_size("tp")
    me = lax.axis_index("ctx")
    length, channels = prefix_x.shape
    heads = decay_rate.shape[0]
    width = prefix_bc.shape[1]
    n_state = width // 2
    rows = channels // n_ctx
    bounds = bound_pos.shape[0]
    branches = branch_owner.shape[0]
    tail = conv_x.shape[0] - 1
    onward = [(i, i + 1) for i in range(n_ctx - 1)]

    own = jnp.concatenate([prefix_bc, branch_bc], axis=1)
    gathered = lax.all_to_all(
        jnp.broadcast_to(own[None], (n_tp, *own.shape)), "tp", 0, 0, tiled=True
    ).reshape(length, 2 * width)
    halo = lax.ppermute(prefix_x[length - HALO :], "ctx", onward)
    bc_halo = lax.ppermute(gathered[length - HALO :, :width], "ctx", onward)
    rates = decay_rate[:, None]
    skips = jnp.repeat(skip, channels // heads)[None]
    gain = norm_gain[None]

    block_of = bound_pos // length
    at = bound_pos - block_of * length
    order = jnp.arange(bounds, dtype=I32)
    slot_of = jnp.sum(
        ((block_of[:, None] == block_of[None, :]) & (order[None, :] < order[:, None])).astype(I32), axis=1
    )
    border = jnp.arange(branches, dtype=I32)
    earlier = (branch_owner[:, None] == branch_owner[None, :]) & (border[None, :] < border[:, None])
    key = branch_owner * BR_PER + jnp.sum(earlier.astype(I32), axis=1)
    start = jnp.sum(jnp.where(earlier, branch_len[None, :], 0), axis=1)
    place = jnp.arange(n_ctx * BR_PER, dtype=I32)
    chosen = place[:, None] == key[None, :]
    parent_of = jnp.sum(jnp.where(chosen, branch_parent[None, :], 0), axis=1)
    mine = (me * BR_PER + jnp.arange(BR_PER, dtype=I32))[:, None] == key[None, :]
    my_len = jnp.sum(jnp.where(mine, branch_len[None, :], 0), axis=1)
    my_start = jnp.sum(jnp.where(mine, start[None, :], 0), axis=1)
    slot_here = (block_of == me)[None, :] & (slot_of[None, :] == order[:, None])
    positions = jnp.sum(jnp.where(slot_here, at[None, :] + 1, 0), axis=1) - 1
    meta = jnp.concatenate([parent_of, block_of, slot_of, positions, my_start, my_len])
    at_positions = branches + 2 * bounds
    at_mine = at_positions + bounds
    local_at = jnp.where(block_of == me, at + HALO - tail + 1, -HALO * length)
    parent_at = jnp.sum(jnp.where(parent_of[:, None] == order[None, :], local_at[None, :], 0), axis=1)
    k = jnp.arange(8, dtype=I32)
    tail_at = jnp.where(k[None, :] < tail, parent_at[0::2, None], parent_at[1::2, None]) + (k % tail)[None, :]
    head_of = jnp.arange(n_ctx, dtype=I32) // (n_ctx // heads)
    log_at = HALO + length + (k[None, :] - 2 * tail) * heads + head_of[:, None]
    wanted = jnp.where(k[None, :] < 2 * tail, tail_at, log_at).reshape(-1, 1)

    xc, cumulative, step = call(
        prefix_x_kernel,
        [((length, channels), BF), ((heads, length), F32), ((heads, length), F32)],
        [((HALO + length, channels), F32)],
        [prefix_x, halo, prefix_dt, rates, conv_x],
    )
    sent, b_rows, c_rows = call(
        functools.partial(prefix_state_kernel, base=at_positions),
        [((n_ctx, MISC + (2 + SLOTS) * rows, n_state), BF), ((length, n_state), BF), ((length, n_state), BF)],
        [((HALO + length, width), F32), ((HALO + length + 2 * heads, channels + width), F32)],
        [meta, wanted, prefix_x, halo, gathered, bc_halo, conv_bc, xc, cumulative, step],
        smem=1,
    )
    got = lax.all_to_all(sent, "ctx", 0, 0, tiled=True)
    [y] = call(
        prefix_mix_kernel,
        [((length, channels), F32)],
        [],
        [xc, b_rows, c_rows, cumulative, step, skips],
    )

    scan = functools.partial(scan_kernel, n_branch=branches, bounds=bounds)
    scan_out = [((n_ctx, (1 + BR_PER) * rows, n_state), BF)]
    scan_scratch = [((n_ctx, rows, n_state), F32), ((bounds, rows, n_state), F32)]

    def usual():
        return call(scan, scan_out, scan_scratch, [meta, got], smem=1)[0]

    def crowded():
        extra = more_states(xc, b_rows, step, cumulative, positions[SLOTS:], n_ctx)
        extra = lax.all_to_all(extra, "ctx", 0, 0, tiled=True)
        return call(scan, scan_out, scan_scratch, [meta, got, extra], smem=1)[0]

    back = lax.cond(jnp.max(slot_of) >= SLOTS, crowded, usual)
    back = lax.all_to_all(back, "ctx", 0, 0, tiled=True)

    branch_y, branch_c, seed = call(
        functools.partial(branch_kernel, base=at_mine),
        [((length, channels), F32), ((length, n_state), BF), ((heads, length), F32)],
        [((HALO + length, channels + width), F32)],
        [meta, branch_x, gathered, got, branch_dt, rates, conv_x, conv_bc, skips],
        smem=1,
        blocks={3: (n_ctx, MISC, n_state)},
    )
    gated, branch_gated, squares = call(
        functools.partial(gate_kernel, base=at_mine),
        [((length, channels), F32), ((length, channels), F32), ((n_tp, 8, length // 2), F32)],
        [],
        [meta, y, c_rows, cumulative, prefix_z, branch_y, branch_c, seed, branch_z, back],
        smem=1,
    )
    squares = lax.all_to_all(squares, "tp", 0, 0, tiled=True)
    return tuple(
        call(
            functools.partial(norm_kernel, base=at_mine),
            [((length, channels), BF), ((length, channels), BF)],
            [],
            [meta, squares, gated, branch_gated, gain],
            smem=1,
        )
    )


def solution(mesh):
    both = P(("ctx", "tp"), None)
    in_specs = (
        P("ctx", "tp"), P("ctx", "tp"), both, P("tp", "ctx"),
        P("ctx", "tp"), P("ctx", "tp"), both, P("tp", "ctx"),
        P(None, "tp"), P(), P("tp"), P("tp"), P("tp"), P(), P(), P(), P(),
    )
    out_specs = (P("ctx", "tp"), P("ctx", "tp"))
    return jax.shard_map(body, mesh=mesh, in_specs=in_specs, out_specs=out_specs, check_vma=False)
```

```python
import functools

import jax
import jax.numpy as jnp
from jax import lax
from jax.experimental import pallas as pl
from jax.experimental.pallas import tpu as pltpu
from jax.sharding import PartitionSpec as P

BR_PER = 2
EPSILON = 1e-05
SLOTS = 2
MISC = 16
LOGS = 3
HALO = 16
EARLY = 2
BF = jnp.bfloat16
F32 = jnp.float32
I32 = jnp.int32
HIGH = lax.Precision.HIGHEST
FAR = -1e30


def iota(shape, axis):
    return lax.broadcasted_iota(I32, shape, axis)


def parts_of(value, count):
    found = []
    for _ in range(count):
        part = value.astype(BF)
        found.append(part)
        value = value - part.astype(F32)
    return found


def expand(columns, head_size):
    rows, heads = columns.shape
    low = iota((rows, 2 * head_size), 1) < head_size
    pairs = [
        jnp.where(low, columns[:, h : h + 1], columns[:, h + 1 : h + 2]) for h in range(0, heads, 2)
    ]
    return jnp.concatenate(pairs, axis=1)


def step_and_logs(raw, rates):
    step = jnp.maximum(raw, 0.0) + jnp.log1p(jnp.exp(-jnp.abs(raw)))
    log_decay = -rates * step
    length = raw.shape[1]
    upper = (iota((length, length), 0) <= iota((length, length), 1)).astype(F32)
    cumulative = jnp.dot(log_decay, upper, precision=HIGH, preferred_element_type=F32)
    return step, log_decay, cumulative


def silu(value):
    return value * jax.nn.sigmoid(value)


def mixed_rows(values, scores, step, cumulative, mask, out_ref, extra):
    length, channels = values.shape
    heads = step.shape[0]
    size = channels // heads
    columns = cumulative.T
    half = length // 2
    low = iota((half, 2 * size), 1) < size
    for first, width in ((0, half), (half, length)):
        rows = slice(first, first + half)
        kept = mask[rows, :width]
        score = scores[rows, :width]
        for h in range(0, heads, 2):
            lanes = slice(h * size, (h + 2) * size)
            sums = []
            for one in (h, h + 1):
                gap = columns[rows, one : one + 1] - cumulative[one : one + 1, :width]
                mixing = score * jnp.exp(jnp.where(kept, gap, FAR)) * step[one : one + 1, :width]
                sums.append(jnp.dot(mixing.astype(BF), values[:width, lanes], preferred_element_type=F32))
            out_ref[rows, lanes] = jnp.where(low, sums[0], sums[1]) + extra[rows, lanes]


def prefix_x_kernel(x_ref, halo_ref, dt_ref, rate_ref, taps_ref, xc_ref, cum_ref, step_ref, ext_ref):
    length = x_ref.shape[0]
    ext_ref[:HALO] = halo_ref[...].astype(F32)
    ext_ref[HALO:] = x_ref[...].astype(F32)
    taps = taps_ref[...].astype(F32)
    count = taps.shape[0]
    total = taps[0:1] * ext_ref[HALO - count + 1 : HALO - count + 1 + length]
    for i in range(1, count):
        first = HALO - count + 1 + i
        total = total + taps[i : i + 1] * ext_ref[first : first + length]
    xc_ref[...] = silu(total).astype(BF)
    step, _, cumulative = step_and_logs(dt_ref[...], rate_ref[...])
    cum_ref[...] = cumulative
    step_ref[...] = step


def tail_tiles(meta_ref, base, bounds, height, rows):
    row = iota((bounds * height, 1), 0)
    wanted = jnp.full(row.shape, -1, I32)
    for j in range(bounds):
        wanted = jnp.where(row // height == j, meta_ref[base + j] + row % 4, wanted)
    wanted = jnp.where(row % 4 < 3, wanted, -1)
    picker = (iota((bounds * height, rows.shape[0]), 1) == wanted).astype(BF)
    return jnp.dot(picker, rows, preferred_element_type=F32)


def index_kernel(
    me_ref, bound_ref, owner_ref, parent_ref, len_ref, x_ref,
    meta_ref, tails_ref, last_ref, count_ref, start_ref, size_ref, *, n_ctx,
):
    me = me_ref[0]
    length = x_ref.shape[0]
    bounds = bound_ref.shape[0]
    branches = owner_ref.shape[0]

    def clear(o, _):
        count_ref[o] = 0
        count_ref[n_ctx + o] = 0
        return 0

    lax.fori_loop(0, n_ctx, clear, 0)

    def place(b, _):
        owner = owner_ref[b]
        rank = count_ref[owner]
        start = count_ref[n_ctx + owner]
        size = len_ref[b]
        count_ref[owner] = rank + 1
        count_ref[n_ctx + owner] = start + size
        at = owner * BR_PER + rank
        meta_ref[at] = parent_ref[b]
        start_ref[at] = start
        size_ref[at] = size
        return 0

    lax.fori_loop(0, branches, place, 0)
    blocks = [lax.div(bound_ref[j], length) for j in range(bounds)]
    at = branches
    for k in range(SLOTS):
        meta_ref[at + 3 * bounds + k] = -1
    for j in range(bounds):
        slot = jnp.int32(0)
        for i in range(j):
            slot = slot + (blocks[i] == blocks[j]).astype(I32)
        meta_ref[at + j] = blocks[j]
        meta_ref[at + bounds + j] = slot
        meta_ref[at + 2 * bounds + j] = bound_ref[j] - me * length - 2

        @pl.when((blocks[j] == me) & (slot < SLOTS))
        def _():
            meta_ref[at + 3 * bounds + slot] = bound_ref[j] - me * length

    for k in range(BR_PER):
        meta_ref[at + 3 * bounds + SLOTS + k] = start_ref[me * BR_PER + k]
        meta_ref[at + 3 * bounds + SLOTS + BR_PER + k] = size_ref[me * BR_PER + k]
        meta_ref[at + 3 * bounds + SLOTS + 2 * BR_PER + k] = meta_ref[me * BR_PER + k]
    last_ref[...] = x_ref[length - HALO :, :]
    tails_ref[...] = tail_tiles(meta_ref, at + 2 * bounds, bounds, 4, x_ref[...]).astype(BF)


def spread_kernel(prefix_ref, branch_ref, out_ref):
    width = prefix_ref.shape[1]
    for i in range(out_ref.shape[0]):
        out_ref[i, :, :width] = prefix_ref[...]
        out_ref[i, :, width:] = branch_ref[...]


def prefix_state_kernel(
    meta_ref, bc_ref, bchalo_ref, taps_ref, xc_ref, cum_ref, step_ref,
    sent_ref, b_ref, c_ref, ext_ref, tile_ref, *, base, tail_base,
):
    length, channels = xc_ref.shape
    width = bchalo_ref.shape[1]
    n_state = width // 2
    n_ctx = sent_ref.shape[0]
    heads = cum_ref.shape[0]
    bc = bc_ref[:, :width]
    ext_ref[:HALO] = bchalo_ref[...].astype(F32)
    ext_ref[HALO:] = bc.astype(F32)
    taps = taps_ref[...].astype(F32)
    count = taps.shape[0]
    total = taps[0:1] * ext_ref[HALO - count + 1 : HALO - count + 1 + length]
    for i in range(1, count):
        first = HALO - count + 1 + i
        total = total + taps[i : i + 1] * ext_ref[first : first + length]
    convolved = silu(total).astype(BF)
    b_rows = convolved[:, :n_state]
    b_ref[...] = b_rows
    c_ref[...] = convolved[:, n_state:]
    cumulative = cum_ref[...]
    step = step_ref[...]
    values = xc_ref[...].astype(F32)
    lane = iota((heads, length), 1)
    size = channels // heads
    rows = channels // n_ctx

    def send(first, weight):
        weighted = (values * expand(weight.T, size)).astype(BF)
        state = lax.dot_general(
            weighted, b_rows, (((0,), (0,)), ((), ())), preferred_element_type=F32
        )
        sent_ref[:, first : first + rows, :] = state.astype(BF).reshape(n_ctx, rows, n_state)

    ends = [cumulative[:, length - 1 :]]
    send(MISC, jnp.exp(ends[0] - cumulative) * step)
    for slot in range(SLOTS):
        position = meta_ref[base + slot]
        first = MISC + (1 + slot) * rows
        end = jnp.sum(jnp.where(lane == position, cumulative, 0.0), axis=1, keepdims=True)
        ends.append(end)

        @pl.when(position >= 0)
        def _():
            send(first, jnp.exp(jnp.where(lane <= position, end - cumulative, FAR)) * step)

        @pl.when(position < 0)
        def _():
            sent_ref[:, first : first + rows, :] = jnp.zeros((n_ctx, rows, n_state), BF)

    spot = iota((heads, n_state), 1)
    logs = jnp.zeros((heads, n_state), F32)
    for at, part in enumerate(part for end in ends for part in parts_of(end, 3)):
        logs = jnp.where(spot == at, part.astype(F32), logs)
    bounds = tile_ref.shape[0]
    tile_ref[...] = tail_tiles(meta_ref, tail_base, bounds, 8, bc).reshape(bounds, 8, width)
    row = iota((8, n_state), 0)
    per_head = n_ctx // heads
    for o in range(n_ctx):
        pair = [tile_ref[meta_ref[o * BR_PER + k]] for k in range(BR_PER)]
        tails = [
            jnp.where(row < 4, pair[0][:, g * n_state : (g + 1) * n_state], pair[1][:, g * n_state : (g + 1) * n_state])
            for g in range(2)
        ]
        h = o // per_head
        tails[0] = jnp.where(row == LOGS, logs[h : h + 1], tails[0])
        sent_ref[o, :MISC, :] = jnp.concatenate(tails, axis=0).astype(BF)


def prefix_mix_kernel(xc_ref, b_ref, c_ref, cum_ref, step_ref, skip_ref, y_ref):
    length = xc_ref.shape[0]
    scores = lax.dot_general(
        c_ref[...], b_ref[...], (((1,), (1,)), ((), ())), preferred_element_type=F32
    )
    mask = iota((length, length), 1) <= iota((length, length), 0)
    values = xc_ref[...]
    extra = values.astype(F32) * skip_ref[...]
    mixed_rows(values, scores, step_ref[...], cum_ref[...], mask, y_ref, extra)


def scan_kernel(meta_ref, got_ref, *rest, n_branch, bounds):
    extra_ref = rest[0] if len(rest) == 5 else None
    back_ref, entering_ref, bound_ref, log_ref = rest[-4:]
    n_ctx, _, n_state = got_ref.shape
    rows = entering_ref.shape[1]
    parts = got_ref[:, :MISC, :].astype(F32)[:, LOGS, :]
    for v in range(1 + SLOTS):
        log = parts[:, 3 * v : 3 * v + 1] + parts[:, 3 * v + 1 : 3 * v + 2] + parts[:, 3 * v + 2 : 3 * v + 3]
        log_ref[v] = jnp.broadcast_to(log, (n_ctx, n_state))
    state = jnp.zeros((rows, n_state), F32)
    for i in range(n_ctx):
        entering_ref[i] = state
        back_ref[i, :rows, :] = state.astype(BF)
        if i < n_ctx - 1:
            local = got_ref[i, MISC : MISC + rows, :].astype(F32)
            state = jnp.exp(log_ref[0, i : i + 1]) * state + local
    for j in range(bounds):
        block = meta_ref[n_branch + j]
        slot = meta_ref[n_branch + bounds + j]
        log = log_ref[1, pl.ds(block, 1)]
        part = got_ref[block, MISC + rows : MISC + 2 * rows, :].astype(F32)
        for other in range(1, SLOTS):
            first = MISC + (1 + other) * rows
            log = jnp.where(slot == other, log_ref[1 + other, pl.ds(block, 1)], log)
            part = jnp.where(slot == other, got_ref[block, first : first + rows, :].astype(F32), part)
        if extra_ref is not None:
            tail = extra_ref[block, (bounds - SLOTS) * rows :, :].astype(F32)
            for more in range(bounds - SLOTS):
                here = slot == SLOTS + more
                three = tail[3 * more : 3 * more + 1] + tail[3 * more + 1 : 3 * more + 2] + tail[3 * more + 2 : 3 * more + 3]
                log = jnp.where(here, three, log)
                part = jnp.where(here, extra_ref[block, more * rows : (more + 1) * rows, :].astype(F32), part)
        bound_ref[j] = jnp.exp(log) * entering_ref[block] + part
    for o in range(n_ctx):
        for k in range(BR_PER):
            first = (1 + k) * rows
            back_ref[o, first : first + rows, :] = bound_ref[meta_ref[o * BR_PER + k]].astype(BF)


def segments(meta_ref, base, shape, axis):
    row = iota(shape, axis)
    segment = jnp.full(shape, BR_PER, I32)
    offset = row
    for k in range(BR_PER):
        start, size = meta_ref[base + k], meta_ref[base + BR_PER + k]
        inside = (row >= start) & (row < start + size)
        segment = jnp.where(inside, k, segment)
        offset = jnp.where(inside, row - start, offset)
    return segment, offset


def branch_kernel(
    meta_ref, x_ref, bc_ref, xtails_ref, got_ref, dt_ref, rate_ref, xtaps_ref, taps_ref, skip_ref,
    y_ref, c_ref, seed_ref, ext_ref, *, base,
):
    length, channels = x_ref.shape
    n_ctx, _, n_state = got_ref.shape
    width = taps_ref.shape[1]
    ext_ref[:HALO] = jnp.zeros((HALO, channels + width), F32)
    ext_ref[HALO:, :channels] = x_ref[...].astype(F32)
    ext_ref[HALO:, channels:] = bc_ref[:, width:].astype(F32)
    misc = got_ref[0].astype(F32)
    for i in range(1, n_ctx):
        misc = misc + got_ref[i].astype(F32)
    row = iota((8, 1), 0)
    parents = [meta_ref[base + 2 * BR_PER + k] for k in range(BR_PER)]
    wanted = jnp.where(row < 4, parents[0], parents[1]) * 4 + row % 4
    picker = (iota((8, xtails_ref.shape[0]), 1) == wanted).astype(BF)
    tails = jnp.dot(picker, xtails_ref[...], preferred_element_type=F32)
    tails = jnp.concatenate([tails, misc[:8], misc[8:]], axis=1)
    tails = jnp.where(iota(tails.shape, 0) % 4 == LOGS, 0.0, tails)
    tails = jnp.concatenate([tails, jnp.zeros_like(tails)], axis=0).astype(BF)
    taps = jnp.concatenate([xtaps_ref[...].astype(F32), taps_ref[...].astype(F32)], axis=1)
    count = taps.shape[0]
    tail = count - 1
    segment, offset = segments(meta_ref, base, (length, 1), 0)
    place = iota((length, 16), 1)
    total = None
    for i in range(count):
        shift = tail - i
        rows = ext_ref[HALO - shift : HALO - shift + length]
        if shift:
            ahead = (offset < shift) & (segment < BR_PER)
            picker = ahead & (place == segment * 4 + tail - shift + offset)
            early = jnp.dot(picker.astype(BF), tails, preferred_element_type=F32)
            rows = jnp.where(offset >= shift, rows, 0.0) + early
        term = taps[i : i + 1] * rows
        total = term if total is None else total + term
    convolved = silu(total).astype(BF)
    values = convolved[:, :channels]
    b_rows = convolved[:, channels : channels + n_state]
    c_rows = convolved[:, channels + n_state :]
    c_ref[...] = c_rows
    step, log_decay, cumulative = step_and_logs(dt_ref[...], rate_ref[...])
    across, _ = segments(meta_ref, base, (1, length), 1)
    lane = iota(cumulative.shape, 1)
    before = cumulative - log_decay
    seed = jnp.zeros_like(cumulative)
    for k in range(BR_PER):
        first = jnp.sum(jnp.where(lane == meta_ref[base + k], before, 0.0), axis=1, keepdims=True)
        seed = jnp.where(across == k, jnp.exp(jnp.where(across == k, cumulative - first, 0.0)), seed)
    seed_ref[...] = seed
    scores = lax.dot_general(c_rows, b_rows, (((1,), (1,)), ((), ())), preferred_element_type=F32)
    mask = (segment == across) & (segment < BR_PER)
    mask = mask & (iota((length, length), 1) <= iota((length, length), 0))
    extra = values.astype(F32) * skip_ref[...]
    mixed_rows(values, scores, step, cumulative, mask, y_ref, extra)


def gate_kernel(
    meta_ref, y_ref, c_ref, cum_ref, z_ref, by_ref, bc_ref, seed_ref, bz_ref, back_ref,
    g_ref, bg_ref, sq_ref, *, base,
):
    length, channels = y_ref.shape
    heads = cum_ref.shape[0]
    size = channels // heads
    n_ctx, _, n_state = back_ref.shape
    rows = channels // n_ctx

    def from_state(c_rows, which):
        state = back_ref[:, which * rows : (which + 1) * rows, :].reshape(channels, n_state)
        return lax.dot_general(c_rows, state, (((1,), (1,)), ((), ())), preferred_element_type=F32)

    def squares(gated):
        ones = jnp.ones((8, channels), F32)
        return lax.dot_general(
            ones, gated * gated, (((1,), (1,)), ((), ())), precision=HIGH, preferred_element_type=F32
        )

    y = y_ref[...] + expand(jnp.exp(cum_ref[...]).T, size) * from_state(c_ref[...], 0)
    gated = y * silu(z_ref[...].astype(F32))
    g_ref[...] = gated
    sums = squares(gated)
    segment, _ = segments(meta_ref, base, (length, 1), 0)
    c_rows = bc_ref[...]
    seeded = from_state(c_rows, BR_PER)
    for k in range(BR_PER - 1):
        seeded = jnp.where(segment == k, from_state(c_rows, 1 + k), seeded)
    y = by_ref[...] + expand(seed_ref[...].T, size) * seeded
    gated = y * silu(bz_ref[...].astype(F32))
    bg_ref[...] = gated
    more = squares(gated)
    half = length // 2
    row = iota((8, half), 0)
    packed = jnp.where(
        row == 0,
        sums[:, :half],
        jnp.where(row == 1, sums[:, half:], jnp.where(row == 2, more[:, :half], more[:, half:])),
    )
    for i in range(sq_ref.shape[0]):
        sq_ref[i] = packed


def norm_kernel(meta_ref, sq_ref, g_ref, bg_ref, gain_ref, out_ref, bout_ref, *, base):
    length, channels = g_ref.shape
    n_tp = sq_ref.shape[0]
    total = sq_ref[0]
    for i in range(1, n_tp):
        total = total + sq_ref[i]
    factor = lax.rsqrt(total / (channels * n_tp) + EPSILON).T
    gain = gain_ref[...]
    half = length // 2
    segment, _ = segments(meta_ref, base, (length, 1), 0)
    for k in range(2):
        rows = slice(k * half, (k + 1) * half)
        out_ref[rows] = (g_ref[rows] * factor[:, k : k + 1] * gain).astype(BF)
        scaled = bg_ref[rows] * factor[:, 2 + k : 3 + k] * gain
        bout_ref[rows] = jnp.where(segment[rows] < BR_PER, scaled, 0.0).astype(BF)


def call(kernel, outs, scratch, args, smem=0, blocks=None, smem_out=False):
    blocks = blocks or {}
    specs = []
    for i in range(len(args)):
        if i < smem:
            specs.append(pl.BlockSpec(memory_space=pltpu.SMEM))
        elif i in blocks:
            specs.append(pl.BlockSpec(blocks[i], lambda _, n=len(blocks[i]): (0,) * n))
        else:
            specs.append(pl.BlockSpec(args[i].shape, lambda _, n=args[i].ndim: (0,) * n))
    return pl.pallas_call(
        kernel,
        grid=(1,),
        in_specs=specs,
        out_specs=[
            pl.BlockSpec(memory_space=pltpu.SMEM)
            if smem_out and i == 0
            else pl.BlockSpec(s, lambda _, n=len(s): (0,) * n)
            for i, (s, _) in enumerate(outs)
        ],
        out_shape=[jax.ShapeDtypeStruct(s, t) for s, t in outs],
        scratch_shapes=[(pltpu.SMEM if len(s) == 1 else pltpu.VMEM)(s, t) for s, t in scratch],
        compiler_params=pltpu.CompilerParams(vmem_limit_bytes=48 * 2**20),
        cost_estimate=pl.CostEstimate(flops=2 * 10**9, bytes_accessed=4 * 10**6, transcendentals=10**6),
    )(*args)


def more_states(xc, b_rows, step, cumulative, positions, n_ctx):
    length, channels = xc.shape
    heads = step.shape[0]
    n_state = b_rows.shape[1]
    row = jnp.arange(length, dtype=I32)
    hit = row[None, None, :] == positions[:, None, None]
    ends = jnp.sum(jnp.where(hit, cumulative[None], 0.0), axis=2)
    inside = (row[None, :] <= positions[:, None])[:, None, :]
    weight = jnp.exp(jnp.where(inside, ends[:, :, None] - cumulative[None], FAR)) * step[None]
    values = xc.reshape(length, heads, -1).astype(F32)
    weighted = (jnp.transpose(weight, (0, 2, 1))[:, :, :, None] * values[None]).astype(BF)
    states = jnp.einsum("jshp,sn->jhpn", weighted, b_rows, preferred_element_type=F32).astype(BF)
    rows = channels // n_ctx
    count = positions.shape[0]
    states = jnp.transpose(states.reshape(count, n_ctx, rows, n_state), (1, 0, 2, 3))
    parts = []
    rest = ends
    for _ in range(3):
        part = lax.reduce_precision(rest, 8, 7)
        parts.append(part)
        rest = rest - part
    logs = jnp.stack(parts, axis=1).reshape(3 * count, heads).T
    logs = jnp.repeat(logs, n_ctx // heads, axis=0)
    logs = jnp.broadcast_to(logs[:, :, None], (n_ctx, 3 * count, n_state)).astype(BF)
    sent = jnp.concatenate([states.reshape(n_ctx, count * rows, n_state), logs], axis=1)
    return jnp.pad(sent, ((0, 0), (0, -sent.shape[1] % 16), (0, 0)))


def body(
    prefix_x, prefix_z, prefix_bc, prefix_dt, branch_x, branch_z, branch_bc, branch_dt,
    conv_x, conv_bc, decay_rate, skip, norm_gain, bound_pos, branch_owner, branch_parent, branch_len,
):
    n_ctx = lax.axis_size("ctx")
    n_tp = lax.axis_size("tp")
    me = lax.axis_index("ctx")
    length, channels = prefix_x.shape
    heads = decay_rate.shape[0]
    width = prefix_bc.shape[1]
    n_state = width // 2
    rows = channels // n_ctx
    bounds = bound_pos.shape[0]
    branches = branch_owner.shape[0]
    tail = conv_x.shape[0] - 1
    onward = [(i, i + 1) for i in range(n_ctx - 1)]

    [spread] = call(spread_kernel, [((n_tp, length // n_tp, 2 * width), BF)], [], [prefix_bc, branch_bc])
    gathered = lax.all_to_all(spread, "tp", 0, 0, tiled=True).reshape(length, 2 * width)
    rates = decay_rate[:, None]
    skips = jnp.repeat(skip, channels // heads)[None]
    gain = norm_gain[None]
    order = jnp.arange(bounds, dtype=I32)
    block_of = bound_pos // length
    slot_of = jnp.sum(
        ((block_of[:, None] == block_of[None, :]) & (order[None, :] < order[:, None])).astype(I32), axis=1
    )

    at_tails = branches + 2 * bounds
    at_positions = at_tails + bounds
    at_mine = at_positions + SLOTS
    meta, tails, last = call(
        functools.partial(index_kernel, n_ctx=n_ctx),
        [((at_mine + 3 * BR_PER,), I32), ((4 * bounds, channels), BF), ((HALO, channels), BF)],
        [((2 * n_ctx,), I32), ((branches,), I32), ((branches,), I32)],
        [jnp.full((1,), me, I32), bound_pos, branch_owner, branch_parent, branch_len, prefix_x],
        smem=5,
        smem_out=True,
    )
    halo = lax.ppermute(last, "ctx", onward)
    distances = [1 << k for k in range((n_ctx - 1).bit_length())]

    def joined(value, some):
        for far in some:
            value = value + lax.ppermute(value, "ctx", [(i, i ^ far) for i in range(n_ctx)])
        return value

    tails = joined(tails, distances[:EARLY])
    gathered, tails, halo = lax.optimization_barrier((gathered, tails, halo))
    bc_halo = lax.ppermute(gathered[length - HALO :, :width], "ctx", onward)
    xc, cumulative, step = call(
        prefix_x_kernel,
        [((length, channels), BF), ((heads, length), F32), ((heads, length), F32)],
        [((HALO + length, channels), F32)],
        [prefix_x, halo, prefix_dt, rates, conv_x],
    )
    sent, b_rows, c_rows = call(
        functools.partial(prefix_state_kernel, base=at_positions, tail_base=at_tails),
        [((n_ctx, MISC + (1 + SLOTS) * rows, n_state), BF), ((length, n_state), BF), ((length, n_state), BF)],
        [((HALO + length, width), F32), ((bounds, 8, width), F32)],
        [meta, gathered, bc_halo, conv_bc, xc, cumulative, step],
        smem=1,
    )
    got = lax.all_to_all(sent, "ctx", 0, 0, tiled=True)
    tails = joined(tails, distances[EARLY:])
    got, tails = lax.optimization_barrier((got, tails))
    [y] = call(
        prefix_mix_kernel,
        [((length, channels), F32)],
        [],
        [xc, b_rows, c_rows, cumulative, step, skips],
    )

    scan = functools.partial(scan_kernel, n_branch=branches, bounds=bounds)
    scan_out = [((n_ctx, (1 + BR_PER) * rows, n_state), BF)]
    scan_scratch = [
        ((n_ctx, rows, n_state), F32),
        ((bounds, rows, n_state), F32),
        ((1 + SLOTS, n_ctx, n_state), F32),
    ]

    def usual():
        return call(scan, scan_out, scan_scratch, [meta, got], smem=1)[0]

    def crowded():
        here = (block_of == me)[None, :] & (slot_of[None, :] == order[SLOTS:, None])
        positions = jnp.sum(jnp.where(here, (bound_pos - block_of * length + 1)[None, :], 0), axis=1) - 1
        extra = more_states(xc, b_rows, step, cumulative, positions, n_ctx)
        extra = lax.all_to_all(extra, "ctx", 0, 0, tiled=True)
        return call(scan, scan_out, scan_scratch, [meta, got, extra], smem=1)[0]

    back = lax.cond(jnp.max(slot_of) >= SLOTS, crowded, usual)
    back = lax.all_to_all(back, "ctx", 0, 0, tiled=True)

    branch_y, branch_c, seed = call(
        functools.partial(branch_kernel, base=at_mine),
        [((length, channels), F32), ((length, n_state), BF), ((heads, length), F32)],
        [((HALO + length, channels + width), F32)],
        [meta, branch_x, gathered, tails, got, branch_dt, rates, conv_x, conv_bc, skips],
        smem=1,
        blocks={4: (n_ctx, MISC, n_state)},
    )
    gated, branch_gated, squares = call(
        functools.partial(gate_kernel, base=at_mine),
        [((length, channels), F32), ((length, channels), F32), ((n_tp, 8, length // 2), F32)],
        [],
        [meta, y, c_rows, cumulative, prefix_z, branch_y, branch_c, seed, branch_z, back],
        smem=1,
    )
    squares = lax.all_to_all(squares, "tp", 0, 0, tiled=True)
    return tuple(
        call(
            functools.partial(norm_kernel, base=at_mine),
            [((length, channels), BF), ((length, channels), BF)],
            [],
            [meta, squares, gated, branch_gated, gain],
            smem=1,
        )
    )


def solution(mesh):
    both = P(("ctx", "tp"), None)
    in_specs = (
        P("ctx", "tp"), P("ctx", "tp"), both, P("tp", "ctx"),
        P("ctx", "tp"), P("ctx", "tp"), both, P("tp", "ctx"),
        P(None, "tp"), P(), P("tp"), P("tp"), P("tp"), P(), P(), P(), P(),
    )
    out_specs = (P("ctx", "tp"), P("ctx", "tp"))
    return jax.shard_map(body, mesh=mesh, in_specs=in_specs, out_specs=out_specs, check_vma=False)
```

```python
import functools

import jax
import jax.numpy as jnp
from jax import lax
from jax.experimental import pallas as pl
from jax.experimental.pallas import tpu as pltpu
from jax.sharding import PartitionSpec as P

BR_PER = 2
EPSILON = 1e-05
SLOTS = 2
LOGS = 3
HALO = 16
BF = jnp.bfloat16
F32 = jnp.float32
I32 = jnp.int32
HIGH = lax.Precision.HIGHEST
FAR = -1e30


def iota(shape, axis):
    return lax.broadcasted_iota(I32, shape, axis)


def parts_of(value, count):
    found = []
    for _ in range(count):
        part = value.astype(BF)
        found.append(part)
        value = value - part.astype(F32)
    return found


def expand(columns, head_size):
    rows, heads = columns.shape
    low = iota((rows, 2 * head_size), 1) < head_size
    pairs = [
        jnp.where(low, columns[:, h : h + 1], columns[:, h + 1 : h + 2]) for h in range(0, heads, 2)
    ]
    return jnp.concatenate(pairs, axis=1)


def step_and_logs(raw, rates):
    step = jnp.maximum(raw, 0.0) + jnp.log1p(jnp.exp(-jnp.abs(raw)))
    log_decay = -rates * step
    length = raw.shape[1]
    upper = (iota((length, length), 0) <= iota((length, length), 1)).astype(F32)
    cumulative = jnp.dot(log_decay, upper, precision=HIGH, preferred_element_type=F32)
    return step, log_decay, cumulative


def silu(value):
    return value * jax.nn.sigmoid(value)


def mixed_rows(values, scores, step, cumulative, mask, out_ref, extra, gate):
    length, channels = values.shape
    heads = step.shape[0]
    size = channels // heads
    columns = cumulative.T
    half = length // 2
    low = iota((half, 2 * size), 1) < size
    for first, width in ((0, half), (half, length)):
        rows = slice(first, first + half)
        kept = mask[rows, :width]
        score = scores[rows, :width]
        for h in range(0, heads, 2):
            lanes = slice(h * size, (h + 2) * size)
            sums = []
            for one in (h, h + 1):
                gap = columns[rows, one : one + 1] - cumulative[one : one + 1, :width]
                mixing = score * jnp.exp(jnp.where(kept, gap, FAR)) * step[one : one + 1, :width]
                sums.append(jnp.dot(mixing.astype(BF), values[:width, lanes], preferred_element_type=F32))
            out_ref[rows, lanes] = (jnp.where(low, sums[0], sums[1]) + extra[rows, lanes]) * gate[rows, lanes]


def prefix_x_kernel(
    meta_ref, x_ref, halo_ref, dt_ref, rate_ref, taps_ref,
    xc_ref, cum_ref, step_ref, weighted_ref, logs_ref, ext_ref, *, base,
):
    length, channels = x_ref.shape
    heads = rate_ref.shape[0]
    ext_ref[:HALO] = halo_ref[...].astype(F32)
    ext_ref[HALO:] = x_ref[...].astype(F32)
    taps = taps_ref[...].astype(F32)
    count = taps.shape[0]
    total = taps[0:1] * ext_ref[HALO - count + 1 : HALO - count + 1 + length]
    for i in range(1, count):
        first = HALO - count + 1 + i
        total = total + taps[i : i + 1] * ext_ref[first : first + length]
    values = silu(total).astype(BF)
    xc_ref[...] = values
    step, _, cumulative = step_and_logs(dt_ref[...], rate_ref[...])
    cum_ref[...] = cumulative
    step_ref[...] = step
    lane = iota((heads, length), 1)

    def weigh(at, weight):
        weighted_ref[at] = (xc_ref[...].astype(F32) * expand(weight.T, channels // heads)).astype(BF)

    ends = [cumulative[:, length - 1 :]]
    weigh(0, jnp.exp(ends[0] - cumulative) * step)
    for slot in range(SLOTS):
        position = meta_ref[base + slot]
        end = jnp.sum(jnp.where(lane == position, cumulative, 0.0), axis=1, keepdims=True)
        ends.append(end)

        @pl.when(position >= 0)
        def _():
            weigh(1 + slot, jnp.exp(jnp.where(lane <= position, end - cumulative, FAR)) * step)

    spot = iota(logs_ref.shape, 1)
    logs = jnp.zeros(logs_ref.shape, F32)
    for at, part in enumerate(part for end in ends for part in parts_of(end, 3)):
        logs = jnp.where(spot == at, part.astype(F32), logs)
    logs_ref[...] = logs


def tail_tiles(meta_ref, base, rows, out_ref):
    bounds, height, width = out_ref.shape
    row = iota((bounds * height, 1), 0)
    wanted = jnp.full(row.shape, -1, I32)
    for j in range(bounds):
        wanted = jnp.where(row // height == j, meta_ref[base + j] + row % 4, wanted)
    wanted = jnp.where(row % 4 < 3, wanted, -1)
    picker = (iota((bounds * height, rows.shape[0]), 1) == wanted).astype(BF)
    picked = jnp.dot(picker, rows, preferred_element_type=F32)
    out_ref[...] = picked.reshape(bounds, height, width)


def index_kernel(
    me_ref, bound_ref, owner_ref, parent_ref, len_ref, x_ref,
    meta_ref, tails_ref, last_ref, count_ref, start_ref, size_ref, tile_ref, *, n_ctx, n_state,
):
    me = me_ref[0]
    length = x_ref.shape[0]
    bounds = bound_ref.shape[0]
    branches = owner_ref.shape[0]

    def clear(o, _):
        count_ref[o] = 0
        count_ref[n_ctx + o] = 0
        return 0

    lax.fori_loop(0, n_ctx, clear, 0)

    def place(b, _):
        owner = owner_ref[b]
        rank = count_ref[owner]
        start = count_ref[n_ctx + owner]
        size = len_ref[b]
        count_ref[owner] = rank + 1
        count_ref[n_ctx + owner] = start + size
        at = owner * BR_PER + rank
        meta_ref[at] = parent_ref[b]
        start_ref[at] = start
        size_ref[at] = size
        return 0

    lax.fori_loop(0, branches, place, 0)
    blocks = [lax.div(bound_ref[j], length) for j in range(bounds)]
    at = branches
    for k in range(SLOTS):
        meta_ref[at + 3 * bounds + k] = -1
    for j in range(bounds):
        slot = jnp.int32(0)
        for i in range(j):
            slot = slot + (blocks[i] == blocks[j]).astype(I32)
        meta_ref[at + j] = blocks[j]
        meta_ref[at + bounds + j] = slot
        meta_ref[at + 2 * bounds + j] = bound_ref[j] - me * length - 2

        @pl.when((blocks[j] == me) & (slot < SLOTS))
        def _():
            meta_ref[at + 3 * bounds + slot] = bound_ref[j] - me * length

    for k in range(BR_PER):
        meta_ref[at + 3 * bounds + SLOTS + k] = start_ref[me * BR_PER + k]
        meta_ref[at + 3 * bounds + SLOTS + BR_PER + k] = size_ref[me * BR_PER + k]
    last_ref[...] = x_ref[length - HALO :, :]
    tail_tiles(meta_ref, at + 2 * bounds, x_ref[...], tile_ref)
    upper = iota((8, n_state), 0) < 4
    groups = x_ref.shape[1] // n_state
    for o in range(n_ctx):
        first, second = (meta_ref[o * BR_PER + k] for k in range(BR_PER))
        tiles = []
        for g in range(groups):
            lanes = slice(g * n_state, (g + 1) * n_state)
            tiles.append(jnp.where(upper, tile_ref[first, :, lanes], tile_ref[second, :, lanes]))
        tails_ref[o] = jnp.concatenate(tiles, axis=0).astype(BF)


def spread_kernel(prefix_ref, branch_ref, out_ref):
    width = prefix_ref.shape[1]
    for i in range(out_ref.shape[0]):
        out_ref[i, :, :width] = prefix_ref[...]
        out_ref[i, :, width:] = branch_ref[...]


def prefix_state_kernel(
    meta_ref, bc_ref, bchalo_ref, taps_ref, weighted_ref, logs_ref, xtails_ref,
    sent_ref, b_ref, c_ref, ext_ref, tile_ref, *, base, tail_base,
):
    _, length, channels = weighted_ref.shape
    width = bchalo_ref.shape[1]
    n_state = width // 2
    n_ctx, xrows, _ = xtails_ref.shape
    heads = logs_ref.shape[0]
    bc = bc_ref[:, :width]
    ext_ref[:HALO] = bchalo_ref[...].astype(F32)
    ext_ref[HALO:] = bc.astype(F32)
    taps = taps_ref[...].astype(F32)
    count = taps.shape[0]
    total = taps[0:1] * ext_ref[HALO - count + 1 : HALO - count + 1 + length]
    for i in range(1, count):
        first = HALO - count + 1 + i
        total = total + taps[i : i + 1] * ext_ref[first : first + length]
    convolved = silu(total).astype(BF)
    b_rows = convolved[:, :n_state]
    b_ref[...] = b_rows
    c_ref[...] = convolved[:, n_state:]
    rows = channels // n_ctx
    misc = xrows + 16

    def send(at):
        state = lax.dot_general(
            weighted_ref[at], b_rows, (((0,), (0,)), ((), ())), preferred_element_type=F32
        )
        first = misc + at * rows
        sent_ref[:, first : first + rows, :] = state.astype(BF).reshape(n_ctx, rows, n_state)

    send(0)
    for slot in range(SLOTS):
        position = meta_ref[base + slot]
        first = misc + (1 + slot) * rows

        @pl.when(position >= 0)
        def _():
            send(1 + slot)

        @pl.when(position < 0)
        def _():
            sent_ref[:, first : first + rows, :] = jnp.zeros((n_ctx, rows, n_state), BF)

    sent_ref[:, :xrows, :] = xtails_ref[...]
    bounds = tile_ref.shape[0]
    tail_tiles(meta_ref, tail_base, bc, tile_ref)
    row = iota((8, n_state), 0)
    per_head = n_ctx // heads
    for o in range(n_ctx):
        first, second = (meta_ref[o * BR_PER + k] for k in range(BR_PER))
        tails = []
        for g in range(2):
            lanes = slice(g * n_state, (g + 1) * n_state)
            tails.append(jnp.where(row < 4, tile_ref[first, :, lanes], tile_ref[second, :, lanes]))
        h = o // per_head
        tails[0] = jnp.where(row == LOGS, logs_ref[h : h + 1], tails[0])
        sent_ref[o, xrows:misc, :] = jnp.concatenate(tails, axis=0).astype(BF)


def prefix_mix_kernel(xc_ref, b_ref, c_ref, cum_ref, step_ref, skip_ref, z_ref, y_ref, scale_ref):
    length, channels = xc_ref.shape
    scores = lax.dot_general(
        c_ref[...], b_ref[...], (((1,), (1,)), ((), ())), preferred_element_type=F32
    )
    mask = iota((length, length), 1) <= iota((length, length), 0)
    values = xc_ref[...]
    cumulative = cum_ref[...]
    gate = silu(z_ref[...].astype(F32))
    scale_ref[...] = expand(jnp.exp(cumulative).T, channels // cumulative.shape[0]) * gate
    extra = values.astype(F32) * skip_ref[...]
    mixed_rows(values, scores, step_ref[...], cumulative, mask, y_ref, extra, gate)


def scan_kernel(meta_ref, got_ref, *rest, n_branch, bounds):
    extra_ref = rest[0] if len(rest) == 5 else None
    back_ref, entering_ref, bound_ref, log_ref = rest[-4:]
    n_ctx, sent_rows, n_state = got_ref.shape
    rows = entering_ref.shape[1]
    misc = sent_rows - (1 + SLOTS) * rows
    parts = got_ref[:, misc - 16 : misc, :].astype(F32)[:, LOGS, :]
    for v in range(1 + SLOTS):
        log = parts[:, 3 * v : 3 * v + 1] + parts[:, 3 * v + 1 : 3 * v + 2] + parts[:, 3 * v + 2 : 3 * v + 3]
        log_ref[v] = jnp.broadcast_to(log, (n_ctx, n_state))
    state = jnp.zeros((rows, n_state), F32)
    for i in range(n_ctx):
        entering_ref[i] = state
        back_ref[i, :rows, :] = state.astype(BF)
        if i < n_ctx - 1:
            local = got_ref[i, misc : misc + rows, :].astype(F32)
            state = jnp.exp(log_ref[0, i : i + 1]) * state + local
    for j in range(bounds):
        block = meta_ref[n_branch + j]
        slot = meta_ref[n_branch + bounds + j]
        log = log_ref[1, pl.ds(block, 1)]
        part = got_ref[block, misc + rows : misc + 2 * rows, :].astype(F32)
        for other in range(1, SLOTS):
            first = misc + (1 + other) * rows
            log = jnp.where(slot == other, log_ref[1 + other, pl.ds(block, 1)], log)
            part = jnp.where(slot == other, got_ref[block, first : first + rows, :].astype(F32), part)
        if extra_ref is not None:
            tail = extra_ref[block, (bounds - SLOTS) * rows :, :].astype(F32)
            for more in range(bounds - SLOTS):
                here = slot == SLOTS + more
                three = tail[3 * more : 3 * more + 1] + tail[3 * more + 1 : 3 * more + 2] + tail[3 * more + 2 : 3 * more + 3]
                log = jnp.where(here, three, log)
                part = jnp.where(here, extra_ref[block, more * rows : (more + 1) * rows, :].astype(F32), part)
        bound_ref[j] = jnp.exp(log) * entering_ref[block] + part
    for o in range(n_ctx):
        for k in range(BR_PER):
            first = (1 + k) * rows
            back_ref[o, first : first + rows, :] = bound_ref[meta_ref[o * BR_PER + k]].astype(BF)


def segments(meta_ref, base, shape, axis):
    row = iota(shape, axis)
    segment = jnp.full(shape, BR_PER, I32)
    offset = row
    for k in range(BR_PER):
        start, size = meta_ref[base + k], meta_ref[base + BR_PER + k]
        inside = (row >= start) & (row < start + size)
        segment = jnp.where(inside, k, segment)
        offset = jnp.where(inside, row - start, offset)
    return segment, offset


def branch_kernel(
    meta_ref, x_ref, bc_ref, got_ref, dt_ref, rate_ref, xtaps_ref, taps_ref, skip_ref, z_ref,
    y_ref, c_ref, scale_ref, ext_ref, *, base,
):
    length, channels = x_ref.shape
    n_ctx, _, n_state = got_ref.shape
    width = taps_ref.shape[1]
    ext_ref[:HALO] = jnp.zeros((HALO, channels + width), F32)
    ext_ref[HALO:, :channels] = x_ref[...].astype(F32)
    ext_ref[HALO:, channels:] = bc_ref[:, width:].astype(F32)
    groups = (channels + width) // n_state
    misc = got_ref[0, : 8 * groups, :].astype(F32)
    for i in range(1, n_ctx):
        misc = misc + got_ref[i, : 8 * groups, :].astype(F32)
    tails = jnp.concatenate([misc[8 * g : 8 * (g + 1)] for g in range(groups)], axis=1)
    unused = iota(tails.shape, 0) % 4 == LOGS
    tails = jnp.where(unused, 0.0, tails)
    tails = jnp.concatenate([tails, jnp.zeros_like(tails)], axis=0).astype(BF)
    taps = jnp.concatenate([xtaps_ref[...].astype(F32), taps_ref[...].astype(F32)], axis=1)
    count = taps.shape[0]
    tail = count - 1
    segment, offset = segments(meta_ref, base, (length, 1), 0)
    place = iota((length, 16), 1)
    total = None
    for i in range(count):
        shift = tail - i
        rows = ext_ref[HALO - shift : HALO - shift + length]
        if shift:
            ahead = (offset < shift) & (segment < BR_PER)
            picker = ahead & (place == segment * 4 + tail - shift + offset)
            early = jnp.dot(picker.astype(BF), tails, preferred_element_type=F32)
            rows = jnp.where(offset >= shift, rows, 0.0) + early
        term = taps[i : i + 1] * rows
        total = term if total is None else total + term
    convolved = silu(total).astype(BF)
    values = convolved[:, :channels]
    b_rows = convolved[:, channels : channels + n_state]
    c_rows = convolved[:, channels + n_state :]
    c_ref[...] = c_rows
    step, log_decay, cumulative = step_and_logs(dt_ref[...], rate_ref[...])
    across, _ = segments(meta_ref, base, (1, length), 1)
    lane = iota(cumulative.shape, 1)
    before = cumulative - log_decay
    seed = jnp.zeros_like(cumulative)
    for k in range(BR_PER):
        first = jnp.sum(jnp.where(lane == meta_ref[base + k], before, 0.0), axis=1, keepdims=True)
        seed = jnp.where(across == k, jnp.exp(jnp.where(across == k, cumulative - first, 0.0)), seed)
    gate = silu(z_ref[...].astype(F32))
    scale_ref[...] = expand(seed.T, channels // seed.shape[0]) * gate
    scores = lax.dot_general(c_rows, b_rows, (((1,), (1,)), ((), ())), preferred_element_type=F32)
    mask = (segment == across) & (segment < BR_PER)
    mask = mask & (iota((length, length), 1) <= iota((length, length), 0))
    extra = values.astype(F32) * skip_ref[...]
    mixed_rows(values, scores, step, cumulative, mask, y_ref, extra, gate)


def gate_kernel(
    meta_ref, y_ref, scale_ref, c_ref, by_ref, bscale_ref, bc_ref, back_ref,
    g_ref, bg_ref, sq_ref, *, base,
):
    length, channels = y_ref.shape
    n_ctx, _, n_state = back_ref.shape
    rows = channels // n_ctx

    def from_state(c_rows, which):
        state = back_ref[:, which * rows : (which + 1) * rows, :].reshape(channels, n_state)
        return lax.dot_general(c_rows, state, (((1,), (1,)), ((), ())), preferred_element_type=F32)

    def squares(gated):
        ones = jnp.ones((8, channels), F32)
        return lax.dot_general(
            ones, gated * gated, (((1,), (1,)), ((), ())), precision=HIGH, preferred_element_type=F32
        )

    gated = y_ref[...] + scale_ref[...] * from_state(c_ref[...], 0)
    g_ref[...] = gated
    sums = squares(gated)
    segment, _ = segments(meta_ref, base, (length, 1), 0)
    c_rows = bc_ref[...]
    seeded = from_state(c_rows, BR_PER)
    for k in range(BR_PER - 1):
        seeded = jnp.where(segment == k, from_state(c_rows, 1 + k), seeded)
    gated = by_ref[...] + bscale_ref[...] * seeded
    bg_ref[...] = gated
    more = squares(gated)
    half = length // 2
    row = iota((8, half), 0)
    packed = jnp.where(
        row == 0,
        sums[:, :half],
        jnp.where(row == 1, sums[:, half:], jnp.where(row == 2, more[:, :half], more[:, half:])),
    )
    for i in range(sq_ref.shape[0]):
        sq_ref[i] = packed


def norm_kernel(meta_ref, sq_ref, g_ref, bg_ref, gain_ref, out_ref, bout_ref, *, base):
    length, channels = g_ref.shape
    n_tp = sq_ref.shape[0]
    total = sq_ref[0]
    for i in range(1, n_tp):
        total = total + sq_ref[i]
    factor = lax.rsqrt(total / (channels * n_tp) + EPSILON).T
    gain = gain_ref[...]
    half = length // 2
    segment, _ = segments(meta_ref, base, (length, 1), 0)
    for k in range(2):
        rows = slice(k * half, (k + 1) * half)
        out_ref[rows] = (g_ref[rows] * factor[:, k : k + 1] * gain).astype(BF)
        scaled = bg_ref[rows] * factor[:, 2 + k : 3 + k] * gain
        bout_ref[rows] = jnp.where(segment[rows] < BR_PER, scaled, 0.0).astype(BF)


def call(kernel, outs, scratch, args, smem=0, smem_out=False):
    def where(scalar):
        return pl.BlockSpec(memory_space=pltpu.SMEM if scalar else pltpu.VMEM)

    return pl.pallas_call(
        kernel,
        in_specs=[where(i < smem) for i in range(len(args))],
        out_specs=[where(smem_out and i == 0) for i in range(len(outs))],
        out_shape=[jax.ShapeDtypeStruct(s, t) for s, t in outs],
        scratch_shapes=[(pltpu.SMEM if len(s) == 1 else pltpu.VMEM)(s, t) for s, t in scratch],
        compiler_params=pltpu.CompilerParams(vmem_limit_bytes=24 * 2**20),
        cost_estimate=pl.CostEstimate(flops=2 * 10**9, bytes_accessed=4 * 10**6, transcendentals=10**6),
    )(*args)


def more_states(xc, b_rows, step, cumulative, positions, n_ctx):
    length, channels = xc.shape
    heads = step.shape[0]
    n_state = b_rows.shape[1]
    row = jnp.arange(length, dtype=I32)
    hit = row[None, None, :] == positions[:, None, None]
    ends = jnp.sum(jnp.where(hit, cumulative[None], 0.0), axis=2)
    inside = (row[None, :] <= positions[:, None])[:, None, :]
    weight = jnp.exp(jnp.where(inside, ends[:, :, None] - cumulative[None], FAR)) * step[None]
    values = xc.reshape(length, heads, -1).astype(F32)
    weighted = (jnp.transpose(weight, (0, 2, 1))[:, :, :, None] * values[None]).astype(BF)
    states = jnp.einsum("jshp,sn->jhpn", weighted, b_rows, preferred_element_type=F32).astype(BF)
    rows = channels // n_ctx
    count = positions.shape[0]
    states = jnp.transpose(states.reshape(count, n_ctx, rows, n_state), (1, 0, 2, 3))
    parts = []
    rest = ends
    for _ in range(3):
        part = lax.reduce_precision(rest, 8, 7)
        parts.append(part)
        rest = rest - part
    logs = jnp.stack(parts, axis=1).reshape(3 * count, heads).T
    logs = jnp.repeat(logs, n_ctx // heads, axis=0)
    logs = jnp.broadcast_to(logs[:, :, None], (n_ctx, 3 * count, n_state)).astype(BF)
    sent = jnp.concatenate([states.reshape(n_ctx, count * rows, n_state), logs], axis=1)
    return jnp.pad(sent, ((0, 0), (0, -sent.shape[1] % 16), (0, 0)))


def body(
    prefix_x, prefix_z, prefix_bc, prefix_dt, branch_x, branch_z, branch_bc, branch_dt,
    conv_x, conv_bc, decay_rate, skip, norm_gain, bound_pos, branch_owner, branch_parent, branch_len,
):
    n_ctx = lax.axis_size("ctx")
    n_tp = lax.axis_size("tp")
    me = lax.axis_index("ctx")
    length, channels = prefix_x.shape
    heads = decay_rate.shape[0]
    width = prefix_bc.shape[1]
    n_state = width // 2
    rows = channels // n_ctx
    bounds = bound_pos.shape[0]
    branches = branch_owner.shape[0]
    tail = conv_x.shape[0] - 1
    onward = [(i, i + 1) for i in range(n_ctx - 1)]

    [spread] = call(spread_kernel, [((n_tp, length // n_tp, 2 * width), BF)], [], [prefix_bc, branch_bc])
    gathered = lax.all_to_all(spread, "tp", 0, 0, tiled=True).reshape(length, 2 * width)
    rates = decay_rate[:, None]
    skips = jnp.repeat(skip, channels // heads)[None]
    gain = norm_gain[None]
    order = jnp.arange(bounds, dtype=I32)
    block_of = bound_pos // length
    slot_of = jnp.sum(
        ((block_of[:, None] == block_of[None, :]) & (order[None, :] < order[:, None])).astype(I32), axis=1
    )

    at_tails = branches + 2 * bounds
    at_positions = at_tails + bounds
    at_mine = at_positions + SLOTS
    xrows = 8 * channels // n_state
    meta, xtails, last = call(
        functools.partial(index_kernel, n_ctx=n_ctx, n_state=n_state),
        [((at_mine + 2 * BR_PER,), I32), ((n_ctx, xrows, n_state), BF), ((HALO, channels), BF)],
        [((2 * n_ctx,), I32), ((branches,), I32), ((branches,), I32), ((bounds, 8, channels), F32)],
        [jnp.full((1,), me, I32), bound_pos, branch_owner, branch_parent, branch_len, prefix_x],
        smem=5,
        smem_out=True,
    )
    halo = lax.ppermute(last, "ctx", onward)
    xc, cumulative, step, weighted, logs = call(
        functools.partial(prefix_x_kernel, base=at_positions),
        [
            ((length, channels), BF),
            ((heads, length), F32),
            ((heads, length), F32),
            ((1 + SLOTS, length, channels), BF),
            ((heads, n_state), F32),
        ],
        [((HALO + length, channels), F32)],
        [meta, prefix_x, halo, prefix_dt, rates, conv_x],
        smem=1,
    )
    gathered, weighted = lax.optimization_barrier((gathered, weighted))
    bc_halo = lax.ppermute(gathered[length - HALO :, :width], "ctx", onward)
    sent, b_rows, c_rows = call(
        functools.partial(prefix_state_kernel, base=at_positions, tail_base=at_tails),
        [((n_ctx, xrows + 16 + (1 + SLOTS) * rows, n_state), BF), ((length, n_state), BF), ((length, n_state), BF)],
        [((HALO + length, width), F32), ((bounds, 8, width), F32)],
        [meta, gathered, bc_halo, conv_bc, weighted, logs, xtails],
        smem=1,
    )
    got = lax.all_to_all(sent, "ctx", 0, 0, tiled=True)
    y, scale = call(
        prefix_mix_kernel,
        [((length, channels), F32), ((length, channels), F32)],
        [],
        [xc, b_rows, c_rows, cumulative, step, skips, prefix_z],
    )
    got, y, scale = lax.optimization_barrier((got, y, scale))

    scan = functools.partial(scan_kernel, n_branch=branches, bounds=bounds)
    scan_out = [((n_ctx, (1 + BR_PER) * rows, n_state), BF)]
    scan_scratch = [
        ((n_ctx, rows, n_state), F32),
        ((bounds, rows, n_state), F32),
        ((1 + SLOTS, n_ctx, n_state), F32),
    ]

    def usual():
        return call(scan, scan_out, scan_scratch, [meta, got], smem=1)[0]

    def crowded():
        here = (block_of == me)[None, :] & (slot_of[None, :] == order[SLOTS:, None])
        positions = jnp.sum(jnp.where(here, (bound_pos - block_of * length + 1)[None, :], 0), axis=1) - 1
        extra = more_states(xc, b_rows, step, cumulative, positions, n_ctx)
        extra = lax.all_to_all(extra, "ctx", 0, 0, tiled=True)
        return call(scan, scan_out, scan_scratch, [meta, got, extra], smem=1)[0]

    back = lax.cond(jnp.max(slot_of) >= SLOTS, crowded, usual)
    back = lax.all_to_all(back, "ctx", 0, 0, tiled=True)

    branch_y, branch_c, branch_scale = call(
        functools.partial(branch_kernel, base=at_mine),
        [((length, channels), F32), ((length, n_state), BF), ((length, channels), F32)],
        [((HALO + length, channels + width), F32)],
        [meta, branch_x, gathered, got, branch_dt, rates, conv_x, conv_bc, skips, branch_z],
        smem=1,
    )
    gated, branch_gated, squares = call(
        functools.partial(gate_kernel, base=at_mine),
        [((length, channels), F32), ((length, channels), F32), ((n_tp, 8, length // 2), F32)],
        [],
        [meta, y, scale, c_rows, branch_y, branch_scale, branch_c, back],
        smem=1,
    )
    squares = lax.all_to_all(squares, "tp", 0, 0, tiled=True)
    return tuple(
        call(
            functools.partial(norm_kernel, base=at_mine),
            [((length, channels), BF), ((length, channels), BF)],
            [],
            [meta, squares, gated, branch_gated, gain],
            smem=1,
        )
    )


def solution(mesh):
    both = P(("ctx", "tp"), None)
    in_specs = (
        P("ctx", "tp"), P("ctx", "tp"), both, P("tp", "ctx"),
        P("ctx", "tp"), P("ctx", "tp"), both, P("tp", "ctx"),
        P(None, "tp"), P(), P("tp"), P("tp"), P("tp"), P(), P(), P(), P(),
    )
    out_specs = (P("ctx", "tp"), P("ctx", "tp"))
    return jax.shard_map(body, mesh=mesh, in_specs=in_specs, out_specs=out_specs, check_vma=False)
```

```python
import functools

import jax
import jax.numpy as jnp
from jax import lax
from jax.experimental import pallas as pl
from jax.experimental.pallas import tpu as pltpu
from jax.sharding import PartitionSpec as P

BR_PER = 2
EPSILON = 1e-05
SLOTS = 2
LOGS = 3
HALO = 16
BF = jnp.bfloat16
F32 = jnp.float32
I32 = jnp.int32
HIGH = lax.Precision.HIGHEST
FAR = -1e30


def iota(shape, axis):
    return lax.broadcasted_iota(I32, shape, axis)


def parts_of(value, count):
    found = []
    for _ in range(count):
        part = value.astype(BF)
        found.append(part)
        value = value - part.astype(F32)
    return found


def expand(columns, head_size):
    rows, heads = columns.shape
    low = iota((rows, 2 * head_size), 1) < head_size
    pairs = [
        jnp.where(low, columns[:, h : h + 1], columns[:, h + 1 : h + 2]) for h in range(0, heads, 2)
    ]
    return jnp.concatenate(pairs, axis=1)


def step_and_logs(raw, rates):
    step = jnp.maximum(raw, 0.0) + jnp.log1p(jnp.exp(-jnp.abs(raw)))
    log_decay = -rates * step
    length = raw.shape[1]
    upper = (iota((length, length), 0) <= iota((length, length), 1)).astype(F32)
    cumulative = jnp.dot(log_decay, upper, precision=HIGH, preferred_element_type=F32)
    return step, log_decay, cumulative


def silu(value):
    return value * jax.nn.sigmoid(value)


def mixed_rows(values, scores, step, cumulative, mask, out_ref, extra, gate):
    length, channels = values.shape
    heads = step.shape[0]
    size = channels // heads
    columns = cumulative.T
    half = length // 2
    low = iota((half, 2 * size), 1) < size
    for first, width in ((0, half), (half, length)):
        rows = slice(first, first + half)
        kept = mask[rows, :width]
        score = scores[rows, :width]
        for h in range(0, heads, 2):
            lanes = slice(h * size, (h + 2) * size)
            sums = []
            for one in (h, h + 1):
                gap = columns[rows, one : one + 1] - cumulative[one : one + 1, :width]
                mixing = score * jnp.exp(jnp.where(kept, gap, FAR)) * step[one : one + 1, :width]
                sums.append(jnp.dot(mixing.astype(BF), values[:width, lanes], preferred_element_type=F32))
            out_ref[rows, lanes] = (jnp.where(low, sums[0], sums[1]) + extra[rows, lanes]) * gate[rows, lanes]


def prefix_x_kernel(
    meta_ref, x_ref, halo_ref, dt_ref, rate_ref, taps_ref,
    xc_ref, cum_ref, step_ref, weighted_ref, logs_ref, ext_ref, *, base,
):
    length, channels = x_ref.shape
    heads = rate_ref.shape[0]
    ext_ref[:HALO] = halo_ref[...].astype(F32)
    ext_ref[HALO:] = x_ref[...].astype(F32)
    taps = taps_ref[...].astype(F32)
    count = taps.shape[0]
    total = taps[0:1] * ext_ref[HALO - count + 1 : HALO - count + 1 + length]
    for i in range(1, count):
        first = HALO - count + 1 + i
        total = total + taps[i : i + 1] * ext_ref[first : first + length]
    values = silu(total).astype(BF)
    xc_ref[...] = values
    step, _, cumulative = step_and_logs(dt_ref[...], rate_ref[...])
    cum_ref[...] = cumulative
    step_ref[...] = step
    lane = iota((heads, length), 1)

    def weigh(at, weight):
        weighted_ref[at] = (xc_ref[...].astype(F32) * expand(weight.T, channels // heads)).astype(BF)

    ends = [cumulative[:, length - 1 :]]
    weigh(0, jnp.exp(ends[0] - cumulative) * step)
    for slot in range(SLOTS):
        position = meta_ref[base + slot]
        end = jnp.sum(jnp.where(lane == position, cumulative, 0.0), axis=1, keepdims=True)
        ends.append(end)

        @pl.when(position >= 0)
        def _():
            weigh(1 + slot, jnp.exp(jnp.where(lane <= position, end - cumulative, FAR)) * step)

    spot = iota(logs_ref.shape, 1)
    logs = jnp.zeros(logs_ref.shape, F32)
    for at, part in enumerate(part for end in ends for part in parts_of(end, 3)):
        logs = jnp.where(spot == at, part.astype(F32), logs)
    logs_ref[...] = logs


def tail_tiles(meta_ref, base, rows, out_ref):
    bounds, height, width = out_ref.shape
    row = iota((bounds * height, 1), 0)
    wanted = jnp.full(row.shape, -1, I32)
    for j in range(bounds):
        wanted = jnp.where(row // height == j, meta_ref[base + j] + row % 4, wanted)
    wanted = jnp.where(row % 4 < 3, wanted, -1)
    picker = (iota((bounds * height, rows.shape[0]), 1) == wanted).astype(BF)
    picked = jnp.dot(picker, rows, preferred_element_type=F32)
    out_ref[...] = picked.reshape(bounds, height, width)


def index_kernel(
    me_ref, bound_ref, owner_ref, parent_ref, len_ref, x_ref,
    meta_ref, tails_ref, last_ref, count_ref, start_ref, size_ref, tile_ref, *, n_ctx, n_state,
):
    me = me_ref[0]
    length = x_ref.shape[0]
    bounds = bound_ref.shape[0]
    branches = owner_ref.shape[0]

    def clear(o, _):
        count_ref[o] = 0
        count_ref[n_ctx + o] = 0
        return 0

    lax.fori_loop(0, n_ctx, clear, 0)

    def place(b, _):
        owner = owner_ref[b]
        rank = count_ref[owner]
        start = count_ref[n_ctx + owner]
        size = len_ref[b]
        count_ref[owner] = rank + 1
        count_ref[n_ctx + owner] = start + size
        at = owner * BR_PER + rank
        meta_ref[at] = parent_ref[b]
        start_ref[at] = start
        size_ref[at] = size
        return 0

    lax.fori_loop(0, branches, place, 0)
    blocks = [lax.div(bound_ref[j], length) for j in range(bounds)]
    at = branches
    for k in range(SLOTS):
        meta_ref[at + 3 * bounds + k] = -1
    for j in range(bounds):
        slot = jnp.int32(0)
        for i in range(j):
            slot = slot + (blocks[i] == blocks[j]).astype(I32)
        meta_ref[at + j] = blocks[j]
        meta_ref[at + bounds + j] = slot
        meta_ref[at + 2 * bounds + j] = bound_ref[j] - me * length - 2

        @pl.when((blocks[j] == me) & (slot < SLOTS))
        def _():
            meta_ref[at + 3 * bounds + slot] = bound_ref[j] - me * length

    for k in range(BR_PER):
        meta_ref[at + 3 * bounds + SLOTS + k] = start_ref[me * BR_PER + k]
        meta_ref[at + 3 * bounds + SLOTS + BR_PER + k] = size_ref[me * BR_PER + k]
    last_ref[...] = x_ref[length - HALO :, :]
    tail_tiles(meta_ref, at + 2 * bounds, x_ref[...], tile_ref)
    upper = iota((8, n_state), 0) < 4
    groups = x_ref.shape[1] // n_state
    for o in range(n_ctx):
        first, second = (meta_ref[o * BR_PER + k] for k in range(BR_PER))
        tiles = []
        for g in range(groups):
            lanes = slice(g * n_state, (g + 1) * n_state)
            tiles.append(jnp.where(upper, tile_ref[first, :, lanes], tile_ref[second, :, lanes]))
        tails_ref[o] = jnp.concatenate(tiles, axis=0).astype(BF)


def spread_kernel(prefix_ref, branch_ref, halo_ref, out_ref):
    height, width = prefix_ref.shape
    n_state = width // 2
    halo = halo_ref[...].astype(F32)
    tile = jnp.concatenate([halo[8:, n_state:], halo[8:, :n_state]], axis=0).astype(BF)
    for i in range(out_ref.shape[0]):
        out_ref[i, :, :width] = prefix_ref[...]
        out_ref[i, :, width : 2 * width] = branch_ref[...]
        out_ref[i, height - HALO :, 2 * width :] = tile


def prefix_state_kernel(
    meta_ref, bc_ref, taps_ref, weighted_ref, logs_ref, xtails_ref,
    sent_ref, b_ref, c_ref, ext_ref, tile_ref, *, base, tail_base,
):
    _, length, channels = weighted_ref.shape
    width = taps_ref.shape[1]
    n_state = width // 2
    n_ctx, xrows, _ = xtails_ref.shape
    heads = logs_ref.shape[0]
    bc = bc_ref[:, :width]
    halo = bc_ref[length - HALO :, 2 * width :].astype(F32)
    ext_ref[HALO - 8 : HALO, :n_state] = halo[8:]
    ext_ref[HALO - 8 : HALO, n_state:] = halo[:8]
    ext_ref[HALO:] = bc.astype(F32)
    taps = taps_ref[...].astype(F32)
    count = taps.shape[0]
    total = taps[0:1] * ext_ref[HALO - count + 1 : HALO - count + 1 + length]
    for i in range(1, count):
        first = HALO - count + 1 + i
        total = total + taps[i : i + 1] * ext_ref[first : first + length]
    convolved = silu(total).astype(BF)
    b_rows = convolved[:, :n_state]
    b_ref[...] = b_rows
    c_ref[...] = convolved[:, n_state:]
    rows = channels // n_ctx
    misc = xrows + 16

    def send(at):
        state = lax.dot_general(
            weighted_ref[at], b_rows, (((0,), (0,)), ((), ())), preferred_element_type=F32
        )
        first = misc + at * rows
        sent_ref[:, first : first + rows, :] = state.astype(BF).reshape(n_ctx, rows, n_state)

    send(0)
    for slot in range(SLOTS):
        position = meta_ref[base + slot]
        first = misc + (1 + slot) * rows

        @pl.when(position >= 0)
        def _():
            send(1 + slot)

        @pl.when(position < 0)
        def _():
            sent_ref[:, first : first + rows, :] = jnp.zeros((n_ctx, rows, n_state), BF)

    sent_ref[:, :xrows, :] = xtails_ref[...]
    bounds = tile_ref.shape[0]
    tail_tiles(meta_ref, tail_base, bc, tile_ref)
    row = iota((8, n_state), 0)
    per_head = n_ctx // heads
    for o in range(n_ctx):
        first, second = (meta_ref[o * BR_PER + k] for k in range(BR_PER))
        tails = []
        for g in range(2):
            lanes = slice(g * n_state, (g + 1) * n_state)
            tails.append(jnp.where(row < 4, tile_ref[first, :, lanes], tile_ref[second, :, lanes]))
        h = o // per_head
        tails[0] = jnp.where(row == LOGS, logs_ref[h : h + 1], tails[0])
        sent_ref[o, xrows:misc, :] = jnp.concatenate(tails, axis=0).astype(BF)


def prefix_mix_kernel(xc_ref, b_ref, c_ref, cum_ref, step_ref, skip_ref, z_ref, y_ref, scale_ref):
    length, channels = xc_ref.shape
    scores = lax.dot_general(
        c_ref[...], b_ref[...], (((1,), (1,)), ((), ())), preferred_element_type=F32
    )
    mask = iota((length, length), 1) <= iota((length, length), 0)
    values = xc_ref[...]
    cumulative = cum_ref[...]
    gate = silu(z_ref[...].astype(F32))
    scale_ref[...] = expand(jnp.exp(cumulative).T, channels // cumulative.shape[0]) * gate
    extra = values.astype(F32) * skip_ref[...]
    mixed_rows(values, scores, step_ref[...], cumulative, mask, y_ref, extra, gate)


def scan_kernel(meta_ref, got_ref, *rest, n_branch, bounds):
    extra_ref = rest[0] if len(rest) == 5 else None
    back_ref, entering_ref, bound_ref, log_ref = rest[-4:]
    n_ctx, sent_rows, n_state = got_ref.shape
    rows = entering_ref.shape[1]
    misc = sent_rows - (1 + SLOTS) * rows
    parts = got_ref[:, misc - 16 : misc, :].astype(F32)[:, LOGS, :]
    for v in range(1 + SLOTS):
        log = parts[:, 3 * v : 3 * v + 1] + parts[:, 3 * v + 1 : 3 * v + 2] + parts[:, 3 * v + 2 : 3 * v + 3]
        log_ref[v] = jnp.broadcast_to(log, (n_ctx, n_state))
    state = jnp.zeros((rows, n_state), F32)
    for i in range(n_ctx):
        entering_ref[i] = state
        back_ref[i, :rows, :] = state.astype(BF)
        if i < n_ctx - 1:
            local = got_ref[i, misc : misc + rows, :].astype(F32)
            state = jnp.exp(log_ref[0, i : i + 1]) * state + local
    for j in range(bounds):
        block = meta_ref[n_branch + j]
        slot = meta_ref[n_branch + bounds + j]
        log = log_ref[1, pl.ds(block, 1)]
        part = got_ref[block, misc + rows : misc + 2 * rows, :].astype(F32)
        for other in range(1, SLOTS):
            first = misc + (1 + other) * rows
            log = jnp.where(slot == other, log_ref[1 + other, pl.ds(block, 1)], log)
            part = jnp.where(slot == other, got_ref[block, first : first + rows, :].astype(F32), part)
        if extra_ref is not None:
            tail = extra_ref[block, (bounds - SLOTS) * rows :, :].astype(F32)
            for more in range(bounds - SLOTS):
                here = slot == SLOTS + more
                three = tail[3 * more : 3 * more + 1] + tail[3 * more + 1 : 3 * more + 2] + tail[3 * more + 2 : 3 * more + 3]
                log = jnp.where(here, three, log)
                part = jnp.where(here, extra_ref[block, more * rows : (more + 1) * rows, :].astype(F32), part)
        bound_ref[j] = jnp.exp(log) * entering_ref[block] + part
    for o in range(n_ctx):
        for k in range(BR_PER):
            first = (1 + k) * rows
            back_ref[o, first : first + rows, :] = bound_ref[meta_ref[o * BR_PER + k]].astype(BF)


def segments(meta_ref, base, shape, axis):
    row = iota(shape, axis)
    segment = jnp.full(shape, BR_PER, I32)
    offset = row
    for k in range(BR_PER):
        start, size = meta_ref[base + k], meta_ref[base + BR_PER + k]
        inside = (row >= start) & (row < start + size)
        segment = jnp.where(inside, k, segment)
        offset = jnp.where(inside, row - start, offset)
    return segment, offset


def branch_kernel(
    meta_ref, x_ref, bc_ref, got_ref, dt_ref, rate_ref, xtaps_ref, taps_ref, skip_ref, z_ref,
    y_ref, c_ref, scale_ref, ext_ref, *, base,
):
    length, channels = x_ref.shape
    n_ctx, _, n_state = got_ref.shape
    width = taps_ref.shape[1]
    ext_ref[:HALO] = jnp.zeros((HALO, channels + width), F32)
    ext_ref[HALO:, :channels] = x_ref[...].astype(F32)
    ext_ref[HALO:, channels:] = bc_ref[:, width : 2 * width].astype(F32)
    groups = (channels + width) // n_state
    misc = got_ref[0, : 8 * groups, :].astype(F32)
    for i in range(1, n_ctx):
        misc = misc + got_ref[i, : 8 * groups, :].astype(F32)
    tails = jnp.concatenate([misc[8 * g : 8 * (g + 1)] for g in range(groups)], axis=1)
    unused = iota(tails.shape, 0) % 4 == LOGS
    tails = jnp.where(unused, 0.0, tails)
    tails = jnp.concatenate([tails, jnp.zeros_like(tails)], axis=0).astype(BF)
    taps = jnp.concatenate([xtaps_ref[...].astype(F32), taps_ref[...].astype(F32)], axis=1)
    count = taps.shape[0]
    tail = count - 1
    segment, offset = segments(meta_ref, base, (length, 1), 0)
    place = iota((length, 16), 1)
    total = None
    for i in range(count):
        shift = tail - i
        rows = ext_ref[HALO - shift : HALO - shift + length]
        if shift:
            ahead = (offset < shift) & (segment < BR_PER)
            picker = ahead & (place == segment * 4 + tail - shift + offset)
            early = jnp.dot(picker.astype(BF), tails, preferred_element_type=F32)
            rows = jnp.where(offset >= shift, rows, 0.0) + early
        term = taps[i : i + 1] * rows
        total = term if total is None else total + term
    convolved = silu(total).astype(BF)
    values = convolved[:, :channels]
    b_rows = convolved[:, channels : channels + n_state]
    c_rows = convolved[:, channels + n_state :]
    c_ref[...] = c_rows
    step, log_decay, cumulative = step_and_logs(dt_ref[...], rate_ref[...])
    across, _ = segments(meta_ref, base, (1, length), 1)
    lane = iota(cumulative.shape, 1)
    before = cumulative - log_decay
    seed = jnp.zeros_like(cumulative)
    for k in range(BR_PER):
        first = jnp.sum(jnp.where(lane == meta_ref[base + k], before, 0.0), axis=1, keepdims=True)
        seed = jnp.where(across == k, jnp.exp(jnp.where(across == k, cumulative - first, 0.0)), seed)
    gate = silu(z_ref[...].astype(F32))
    scale_ref[...] = expand(seed.T, channels // seed.shape[0]) * gate
    scores = lax.dot_general(c_rows, b_rows, (((1,), (1,)), ((), ())), preferred_element_type=F32)
    mask = (segment == across) & (segment < BR_PER)
    mask = mask & (iota((length, length), 1) <= iota((length, length), 0))
    extra = values.astype(F32) * skip_ref[...]
    mixed_rows(values, scores, step, cumulative, mask, y_ref, extra, gate)


def gate_kernel(
    meta_ref, y_ref, scale_ref, c_ref, by_ref, bscale_ref, bc_ref, back_ref,
    g_ref, bg_ref, sq_ref, *, base,
):
    length, channels = y_ref.shape
    n_ctx, _, n_state = back_ref.shape
    rows = channels // n_ctx

    def from_state(c_rows, which):
        state = back_ref[:, which * rows : (which + 1) * rows, :].reshape(channels, n_state)
        return lax.dot_general(c_rows, state, (((1,), (1,)), ((), ())), preferred_element_type=F32)

    def squares(gated):
        ones = jnp.ones((8, channels), F32)
        return lax.dot_general(
            ones, gated * gated, (((1,), (1,)), ((), ())), precision=HIGH, preferred_element_type=F32
        )

    gated = y_ref[...] + scale_ref[...] * from_state(c_ref[...], 0)
    g_ref[...] = gated
    sums = squares(gated)
    segment, _ = segments(meta_ref, base, (length, 1), 0)
    c_rows = bc_ref[...]
    seeded = from_state(c_rows, BR_PER)
    for k in range(BR_PER - 1):
        seeded = jnp.where(segment == k, from_state(c_rows, 1 + k), seeded)
    gated = by_ref[...] + bscale_ref[...] * seeded
    bg_ref[...] = gated
    more = squares(gated)
    half = length // 2
    row = iota((8, half), 0)
    packed = jnp.where(
        row == 0,
        sums[:, :half],
        jnp.where(row == 1, sums[:, half:], jnp.where(row == 2, more[:, :half], more[:, half:])),
    )
    for i in range(sq_ref.shape[0]):
        sq_ref[i] = packed


def norm_kernel(meta_ref, sq_ref, g_ref, bg_ref, gain_ref, out_ref, bout_ref, *, base):
    length, channels = g_ref.shape
    n_tp = sq_ref.shape[0]
    total = sq_ref[0]
    for i in range(1, n_tp):
        total = total + sq_ref[i]
    factor = lax.rsqrt(total / (channels * n_tp) + EPSILON).T
    gain = gain_ref[...]
    half = length // 2
    segment, _ = segments(meta_ref, base, (length, 1), 0)
    for k in range(2):
        rows = slice(k * half, (k + 1) * half)
        out_ref[rows] = (g_ref[rows] * factor[:, k : k + 1] * gain).astype(BF)
        scaled = bg_ref[rows] * factor[:, 2 + k : 3 + k] * gain
        bout_ref[rows] = jnp.where(segment[rows] < BR_PER, scaled, 0.0).astype(BF)


def call(kernel, outs, scratch, args, smem=0, smem_out=False):
    def where(scalar):
        return pl.BlockSpec(memory_space=pltpu.SMEM if scalar else pltpu.VMEM)

    return pl.pallas_call(
        kernel,
        in_specs=[where(i < smem) for i in range(len(args))],
        out_specs=[where(smem_out and i == 0) for i in range(len(outs))],
        out_shape=[jax.ShapeDtypeStruct(s, t) for s, t in outs],
        scratch_shapes=[(pltpu.SMEM if len(s) == 1 else pltpu.VMEM)(s, t) for s, t in scratch],
        compiler_params=pltpu.CompilerParams(vmem_limit_bytes=24 * 2**20),
        cost_estimate=pl.CostEstimate(flops=2 * 10**9, bytes_accessed=4 * 10**6, transcendentals=10**6),
    )(*args)


def more_states(xc, b_rows, step, cumulative, positions, n_ctx):
    length, channels = xc.shape
    heads = step.shape[0]
    n_state = b_rows.shape[1]
    row = jnp.arange(length, dtype=I32)
    hit = row[None, None, :] == positions[:, None, None]
    ends = jnp.sum(jnp.where(hit, cumulative[None], 0.0), axis=2)
    inside = (row[None, :] <= positions[:, None])[:, None, :]
    weight = jnp.exp(jnp.where(inside, ends[:, :, None] - cumulative[None], FAR)) * step[None]
    values = xc.reshape(length, heads, -1).astype(F32)
    weighted = (jnp.transpose(weight, (0, 2, 1))[:, :, :, None] * values[None]).astype(BF)
    states = jnp.einsum("jshp,sn->jhpn", weighted, b_rows, preferred_element_type=F32).astype(BF)
    rows = channels // n_ctx
    count = positions.shape[0]
    states = jnp.transpose(states.reshape(count, n_ctx, rows, n_state), (1, 0, 2, 3))
    parts = []
    rest = ends
    for _ in range(3):
        part = lax.reduce_precision(rest, 8, 7)
        parts.append(part)
        rest = rest - part
    logs = jnp.stack(parts, axis=1).reshape(3 * count, heads).T
    logs = jnp.repeat(logs, n_ctx // heads, axis=0)
    logs = jnp.broadcast_to(logs[:, :, None], (n_ctx, 3 * count, n_state)).astype(BF)
    sent = jnp.concatenate([states.reshape(n_ctx, count * rows, n_state), logs], axis=1)
    return jnp.pad(sent, ((0, 0), (0, -sent.shape[1] % 16), (0, 0)))


def body(
    prefix_x, prefix_z, prefix_bc, prefix_dt, branch_x, branch_z, branch_bc, branch_dt,
    conv_x, conv_bc, decay_rate, skip, norm_gain, bound_pos, branch_owner, branch_parent, branch_len,
):
    n_ctx = lax.axis_size("ctx")
    n_tp = lax.axis_size("tp")
    me = lax.axis_index("ctx")
    length, channels = prefix_x.shape
    heads = decay_rate.shape[0]
    width = prefix_bc.shape[1]
    n_state = width // 2
    rows = channels // n_ctx
    bounds = bound_pos.shape[0]
    branches = branch_owner.shape[0]
    tail = conv_x.shape[0] - 1
    onward = [(i, i + 1) for i in range(n_ctx - 1)]

    height = prefix_bc.shape[0]
    bc_halo = lax.ppermute(prefix_bc[height - HALO :], "ctx", onward)
    [spread] = call(
        spread_kernel, [((n_tp, height, 2 * width + n_state), BF)], [], [prefix_bc, branch_bc, bc_halo]
    )
    gathered = lax.all_to_all(spread, "tp", 0, 0, tiled=True).reshape(length, 2 * width + n_state)
    rates = decay_rate[:, None]
    skips = jnp.repeat(skip, channels // heads)[None]
    gain = norm_gain[None]
    order = jnp.arange(bounds, dtype=I32)
    block_of = bound_pos // length
    slot_of = jnp.sum(
        ((block_of[:, None] == block_of[None, :]) & (order[None, :] < order[:, None])).astype(I32), axis=1
    )

    at_tails = branches + 2 * bounds
    at_positions = at_tails + bounds
    at_mine = at_positions + SLOTS
    xrows = 8 * channels // n_state
    meta, xtails, last = call(
        functools.partial(index_kernel, n_ctx=n_ctx, n_state=n_state),
        [((at_mine + 2 * BR_PER,), I32), ((n_ctx, xrows, n_state), BF), ((HALO, channels), BF)],
        [((2 * n_ctx,), I32), ((branches,), I32), ((branches,), I32), ((bounds, 8, channels), F32)],
        [jnp.full((1,), me, I32), bound_pos, branch_owner, branch_parent, branch_len, prefix_x],
        smem=5,
        smem_out=True,
    )
    halo = lax.ppermute(last, "ctx", onward)
    xc, cumulative, step, weighted, logs = call(
        functools.partial(prefix_x_kernel, base=at_positions),
        [
            ((length, channels), BF),
            ((heads, length), F32),
            ((heads, length), F32),
            ((1 + SLOTS, length, channels), BF),
            ((heads, n_state), F32),
        ],
        [((HALO + length, channels), F32)],
        [meta, prefix_x, halo, prefix_dt, rates, conv_x],
        smem=1,
    )
    gathered, weighted = lax.optimization_barrier((gathered, weighted))
    sent, b_rows, c_rows = call(
        functools.partial(prefix_state_kernel, base=at_positions, tail_base=at_tails),
        [((n_ctx, xrows + 16 + (1 + SLOTS) * rows, n_state), BF), ((length, n_state), BF), ((length, n_state), BF)],
        [((HALO + length, width), F32), ((bounds, 8, width), F32)],
        [meta, gathered, conv_bc, weighted, logs, xtails],
        smem=1,
    )
    got = lax.all_to_all(sent, "ctx", 0, 0, tiled=True)
    y, scale = call(
        prefix_mix_kernel,
        [((length, channels), F32), ((length, channels), F32)],
        [],
        [xc, b_rows, c_rows, cumulative, step, skips, prefix_z],
    )
    got, y, scale = lax.optimization_barrier((got, y, scale))

    scan = functools.partial(scan_kernel, n_branch=branches, bounds=bounds)
    scan_out = [((n_ctx, (1 + BR_PER) * rows, n_state), BF)]
    scan_scratch = [
        ((n_ctx, rows, n_state), F32),
        ((bounds, rows, n_state), F32),
        ((1 + SLOTS, n_ctx, n_state), F32),
    ]

    def usual():
        return call(scan, scan_out, scan_scratch, [meta, got], smem=1)[0]

    def crowded():
        here = (block_of == me)[None, :] & (slot_of[None, :] == order[SLOTS:, None])
        positions = jnp.sum(jnp.where(here, (bound_pos - block_of * length + 1)[None, :], 0), axis=1) - 1
        extra = more_states(xc, b_rows, step, cumulative, positions, n_ctx)
        extra = lax.all_to_all(extra, "ctx", 0, 0, tiled=True)
        return call(scan, scan_out, scan_scratch, [meta, got, extra], smem=1)[0]

    back = lax.cond(jnp.max(slot_of) >= SLOTS, crowded, usual)
    back = lax.all_to_all(back, "ctx", 0, 0, tiled=True)

    branch_y, branch_c, branch_scale = call(
        functools.partial(branch_kernel, base=at_mine),
        [((length, channels), F32), ((length, n_state), BF), ((length, channels), F32)],
        [((HALO + length, channels + width), F32)],
        [meta, branch_x, gathered, got, branch_dt, rates, conv_x, conv_bc, skips, branch_z],
        smem=1,
    )
    gated, branch_gated, squares = call(
        functools.partial(gate_kernel, base=at_mine),
        [((length, channels), F32), ((length, channels), F32), ((n_tp, 8, length // 2), F32)],
        [],
        [meta, y, scale, c_rows, branch_y, branch_scale, branch_c, back],
        smem=1,
    )
    squares = lax.all_to_all(squares, "tp", 0, 0, tiled=True)
    return tuple(
        call(
            functools.partial(norm_kernel, base=at_mine),
            [((length, channels), BF), ((length, channels), BF)],
            [],
            [meta, squares, gated, branch_gated, gain],
            smem=1,
        )
    )


def solution(mesh):
    both = P(("ctx", "tp"), None)
    in_specs = (
        P("ctx", "tp"), P("ctx", "tp"), both, P("tp", "ctx"),
        P("ctx", "tp"), P("ctx", "tp"), both, P("tp", "ctx"),
        P(None, "tp"), P(), P("tp"), P("tp"), P("tp"), P(), P(), P(), P(),
    )
    out_specs = (P("ctx", "tp"), P("ctx", "tp"))
    return jax.shard_map(body, mesh=mesh, in_specs=in_specs, out_specs=out_specs, check_vma=False)
```

```python
import functools

import jax
import jax.numpy as jnp
from jax import lax
from jax.experimental import pallas as pl
from jax.experimental.pallas import tpu as pltpu
from jax.sharding import PartitionSpec as P

BR_PER = 2
EPSILON = 1e-05
SLOTS = 2
LOGS = 3
HALO = 16
BF = jnp.bfloat16
F32 = jnp.float32
I32 = jnp.int32
HIGH = lax.Precision.HIGHEST
FAR = -1e30


def iota(shape, axis):
    return lax.broadcasted_iota(I32, shape, axis)


def parts_of(value, count):
    found = []
    for _ in range(count):
        part = value.astype(BF)
        found.append(part)
        value = value - part.astype(F32)
    return found


def expand(columns, head_size):
    rows, heads = columns.shape
    low = iota((rows, 2 * head_size), 1) < head_size
    pairs = [
        jnp.where(low, columns[:, h : h + 1], columns[:, h + 1 : h + 2]) for h in range(0, heads, 2)
    ]
    return jnp.concatenate(pairs, axis=1)


def step_and_logs(raw, rates):
    step = jnp.maximum(raw, 0.0) + jnp.log1p(jnp.exp(-jnp.abs(raw)))
    log_decay = -rates * step
    length = raw.shape[1]
    upper = (iota((length, length), 0) <= iota((length, length), 1)).astype(F32)
    cumulative = jnp.dot(log_decay, upper, precision=HIGH, preferred_element_type=F32)
    return step, log_decay, cumulative


def silu(value):
    return value * jax.nn.sigmoid(value)


def mixed_rows(values, scores, step, cumulative, mask, out_ref, extra, gate):
    length, channels = values.shape
    heads = step.shape[0]
    size = channels // heads
    columns = cumulative.T
    half = length // 2
    low = iota((half, 2 * size), 1) < size
    for first, width in ((0, half), (half, length)):
        rows = slice(first, first + half)
        kept = mask[rows, :width]
        score = scores[rows, :width]
        for h in range(0, heads, 2):
            lanes = slice(h * size, (h + 2) * size)
            sums = []
            for one in (h, h + 1):
                gap = columns[rows, one : one + 1] - cumulative[one : one + 1, :width]
                mixing = score * jnp.exp(jnp.where(kept, gap, FAR)) * step[one : one + 1, :width]
                sums.append(jnp.dot(mixing.astype(BF), values[:width, lanes], preferred_element_type=F32))
            out_ref[rows, lanes] = (jnp.where(low, sums[0], sums[1]) + extra[rows, lanes]) * gate[rows, lanes]


def prefix_x_kernel(
    meta_ref, x_ref, dt_ref, rate_ref, taps_ref,
    xc_ref, cum_ref, step_ref, weighted_ref, first_ref, logs_ref, ext_ref, *, base,
):
    length, channels = x_ref.shape
    heads = rate_ref.shape[0]
    ext_ref[:HALO] = jnp.zeros((HALO, channels), F32)
    ext_ref[HALO:] = x_ref[...].astype(F32)
    taps = taps_ref[...].astype(F32)
    count = taps.shape[0]
    total = taps[0:1] * ext_ref[HALO - count + 1 : HALO - count + 1 + length]
    for i in range(1, count):
        first = HALO - count + 1 + i
        total = total + taps[i : i + 1] * ext_ref[first : first + length]
    values = silu(total).astype(BF)
    xc_ref[...] = values
    step, _, cumulative = step_and_logs(dt_ref[...], rate_ref[...])
    cum_ref[...] = cumulative
    step_ref[...] = step
    lane = iota((heads, length), 1)

    def weigh(at, weight):
        wide = expand(weight.T, channels // heads)
        first_ref[at] = wide[:HALO]
        weighted_ref[at] = (xc_ref[...].astype(F32) * wide).astype(BF)

    ends = [cumulative[:, length - 1 :]]
    weigh(0, jnp.exp(ends[0] - cumulative) * step)
    for slot in range(SLOTS):
        position = meta_ref[base + slot]
        end = jnp.sum(jnp.where(lane == position, cumulative, 0.0), axis=1, keepdims=True)
        ends.append(end)

        @pl.when(position >= 0)
        def _():
            weigh(1 + slot, jnp.exp(jnp.where(lane <= position, end - cumulative, FAR)) * step)

    spot = iota(logs_ref.shape, 1)
    logs = jnp.zeros(logs_ref.shape, F32)
    for at, part in enumerate(part for end in ends for part in parts_of(end, 3)):
        logs = jnp.where(spot == at, part.astype(F32), logs)
    logs_ref[...] = logs


def tail_tiles(meta_ref, base, rows, out_ref):
    bounds, height, width = out_ref.shape
    row = iota((bounds * height, 1), 0)
    wanted = jnp.full(row.shape, -1, I32)
    for j in range(bounds):
        wanted = jnp.where(row // height == j, meta_ref[base + j] + row % 4, wanted)
    wanted = jnp.where(row % 4 < 3, wanted, -1)
    picker = (iota((bounds * height, rows.shape[0]), 1) == wanted).astype(BF)
    picked = jnp.dot(picker, rows, preferred_element_type=F32)
    out_ref[...] = picked.reshape(bounds, height, width)


def index_kernel(
    me_ref, bound_ref, owner_ref, parent_ref, len_ref, x_ref,
    meta_ref, tails_ref, last_ref, count_ref, start_ref, size_ref, tile_ref, *, n_ctx, n_state,
):
    me = me_ref[0]
    length = x_ref.shape[0]
    bounds = bound_ref.shape[0]
    branches = owner_ref.shape[0]

    def clear(o, _):
        count_ref[o] = 0
        count_ref[n_ctx + o] = 0
        return 0

    lax.fori_loop(0, n_ctx, clear, 0)

    def place(b, _):
        owner = owner_ref[b]
        rank = count_ref[owner]
        start = count_ref[n_ctx + owner]
        size = len_ref[b]
        count_ref[owner] = rank + 1
        count_ref[n_ctx + owner] = start + size
        at = owner * BR_PER + rank
        meta_ref[at] = parent_ref[b]
        start_ref[at] = start
        size_ref[at] = size
        return 0

    lax.fori_loop(0, branches, place, 0)
    blocks = [lax.div(bound_ref[j], length) for j in range(bounds)]
    at = branches
    for k in range(SLOTS):
        meta_ref[at + 3 * bounds + k] = -1
    for j in range(bounds):
        slot = jnp.int32(0)
        for i in range(j):
            slot = slot + (blocks[i] == blocks[j]).astype(I32)
        meta_ref[at + j] = blocks[j]
        meta_ref[at + bounds + j] = slot
        meta_ref[at + 2 * bounds + j] = bound_ref[j] - me * length - 2

        @pl.when((blocks[j] == me) & (slot < SLOTS))
        def _():
            meta_ref[at + 3 * bounds + slot] = bound_ref[j] - me * length

    for k in range(BR_PER):
        meta_ref[at + 3 * bounds + SLOTS + k] = start_ref[me * BR_PER + k]
        meta_ref[at + 3 * bounds + SLOTS + BR_PER + k] = size_ref[me * BR_PER + k]
    last_ref[...] = x_ref[length - HALO :, :]
    tail_tiles(meta_ref, at + 2 * bounds, x_ref[...], tile_ref)
    upper = iota((8, n_state), 0) < 4
    groups = x_ref.shape[1] // n_state
    for o in range(n_ctx):
        first, second = (meta_ref[o * BR_PER + k] for k in range(BR_PER))
        tiles = []
        for g in range(groups):
            lanes = slice(g * n_state, (g + 1) * n_state)
            tiles.append(jnp.where(upper, tile_ref[first, :, lanes], tile_ref[second, :, lanes]))
        tails_ref[o] = jnp.concatenate(tiles, axis=0).astype(BF)


def spread_kernel(prefix_ref, branch_ref, out_ref):
    width = prefix_ref.shape[1]
    for i in range(out_ref.shape[0]):
        out_ref[i, :, :width] = prefix_ref[...]
        out_ref[i, :, width:] = branch_ref[...]


def prefix_state_kernel(
    meta_ref, x_ref, halo_ref, xtaps_ref, bc_ref, bchalo_ref, taps_ref, weighted_ref, first_ref, logs_ref, xtails_ref,
    sent_ref, b_ref, c_ref, xfirst_ref, ext_ref, tile_ref, edge_ref, *, base, tail_base,
):
    _, length, channels = weighted_ref.shape
    width = bchalo_ref.shape[1]
    n_state = width // 2
    n_ctx, xrows, _ = xtails_ref.shape
    heads = logs_ref.shape[0]
    bc = bc_ref[:, :width]
    ext_ref[:HALO] = bchalo_ref[...].astype(F32)
    ext_ref[HALO:] = bc.astype(F32)
    taps = taps_ref[...].astype(F32)
    count = taps.shape[0]
    total = taps[0:1] * ext_ref[HALO - count + 1 : HALO - count + 1 + length]
    for i in range(1, count):
        first = HALO - count + 1 + i
        total = total + taps[i : i + 1] * ext_ref[first : first + length]
    convolved = silu(total).astype(BF)
    b_rows = convolved[:, :n_state]
    b_ref[...] = b_rows
    c_ref[...] = convolved[:, n_state:]
    rows = channels // n_ctx
    misc = xrows + 16
    edge_ref[:HALO] = halo_ref[...].astype(F32)
    edge_ref[HALO:] = x_ref[:HALO].astype(F32)
    taps = xtaps_ref[...].astype(F32)
    total = taps[0:1] * edge_ref[HALO - count + 1 : 2 * HALO - count + 1]
    for i in range(1, count):
        first = HALO - count + 1 + i
        total = total + taps[i : i + 1] * edge_ref[first : first + HALO]
    xfirst = silu(total).astype(BF)
    xfirst_ref[...] = xfirst

    def send(at):
        edge = (xfirst.astype(F32) * first_ref[at]).astype(BF)
        weighted = jnp.concatenate([edge, weighted_ref[at, HALO:, :]], axis=0)
        state = lax.dot_general(
            weighted, b_rows, (((0,), (0,)), ((), ())), preferred_element_type=F32
        )
        first = misc + at * rows
        sent_ref[:, first : first + rows, :] = state.astype(BF).reshape(n_ctx, rows, n_state)

    send(0)
    for slot in range(SLOTS):
        position = meta_ref[base + slot]
        first = misc + (1 + slot) * rows

        @pl.when(position >= 0)
        def _():
            send(1 + slot)

        @pl.when(position < 0)
        def _():
            sent_ref[:, first : first + rows, :] = jnp.zeros((n_ctx, rows, n_state), BF)

    sent_ref[:, :xrows, :] = xtails_ref[...]
    bounds = tile_ref.shape[0]
    tail_tiles(meta_ref, tail_base, bc, tile_ref)
    row = iota((8, n_state), 0)
    per_head = n_ctx // heads
    for o in range(n_ctx):
        first, second = (meta_ref[o * BR_PER + k] for k in range(BR_PER))
        tails = []
        for g in range(2):
            lanes = slice(g * n_state, (g + 1) * n_state)
            tails.append(jnp.where(row < 4, tile_ref[first, :, lanes], tile_ref[second, :, lanes]))
        h = o // per_head
        tails[0] = jnp.where(row == LOGS, logs_ref[h : h + 1], tails[0])
        sent_ref[o, xrows:misc, :] = jnp.concatenate(tails, axis=0).astype(BF)


def prefix_mix_kernel(xc_ref, xfirst_ref, b_ref, c_ref, cum_ref, step_ref, skip_ref, z_ref, y_ref, scale_ref):
    length, channels = xc_ref.shape
    scores = lax.dot_general(
        c_ref[...], b_ref[...], (((1,), (1,)), ((), ())), preferred_element_type=F32
    )
    mask = iota((length, length), 1) <= iota((length, length), 0)
    values = jnp.concatenate([xfirst_ref[...], xc_ref[HALO:]], axis=0)
    cumulative = cum_ref[...]
    gate = silu(z_ref[...].astype(F32))
    scale_ref[...] = expand(jnp.exp(cumulative).T, channels // cumulative.shape[0]) * gate
    extra = values.astype(F32) * skip_ref[...]
    mixed_rows(values, scores, step_ref[...], cumulative, mask, y_ref, extra, gate)


def scan_kernel(meta_ref, got_ref, *rest, n_branch, bounds):
    extra_ref = rest[0] if len(rest) == 5 else None
    back_ref, entering_ref, bound_ref, log_ref = rest[-4:]
    n_ctx, sent_rows, n_state = got_ref.shape
    rows = entering_ref.shape[1]
    misc = sent_rows - (1 + SLOTS) * rows
    parts = got_ref[:, misc - 16 : misc, :].astype(F32)[:, LOGS, :]
    for v in range(1 + SLOTS):
        log = parts[:, 3 * v : 3 * v + 1] + parts[:, 3 * v + 1 : 3 * v + 2] + parts[:, 3 * v + 2 : 3 * v + 3]
        log_ref[v] = jnp.broadcast_to(log, (n_ctx, n_state))
    state = jnp.zeros((rows, n_state), F32)
    for i in range(n_ctx):
        entering_ref[i] = state
        back_ref[i, :rows, :] = state.astype(BF)
        if i < n_ctx - 1:
            local = got_ref[i, misc : misc + rows, :].astype(F32)
            state = jnp.exp(log_ref[0, i : i + 1]) * state + local
    for j in range(bounds):
        block = meta_ref[n_branch + j]
        slot = meta_ref[n_branch + bounds + j]
        log = log_ref[1, pl.ds(block, 1)]
        part = got_ref[block, misc + rows : misc + 2 * rows, :].astype(F32)
        for other in range(1, SLOTS):
            first = misc + (1 + other) * rows
            log = jnp.where(slot == other, log_ref[1 + other, pl.ds(block, 1)], log)
            part = jnp.where(slot == other, got_ref[block, first : first + rows, :].astype(F32), part)
        if extra_ref is not None:
            tail = extra_ref[block, (bounds - SLOTS) * rows :, :].astype(F32)
            for more in range(bounds - SLOTS):
                here = slot == SLOTS + more
                three = tail[3 * more : 3 * more + 1] + tail[3 * more + 1 : 3 * more + 2] + tail[3 * more + 2 : 3 * more + 3]
                log = jnp.where(here, three, log)
                part = jnp.where(here, extra_ref[block, more * rows : (more + 1) * rows, :].astype(F32), part)
        bound_ref[j] = jnp.exp(log) * entering_ref[block] + part
    for o in range(n_ctx):
        for k in range(BR_PER):
            first = (1 + k) * rows
            back_ref[o, first : first + rows, :] = bound_ref[meta_ref[o * BR_PER + k]].astype(BF)


def segments(meta_ref, base, shape, axis):
    row = iota(shape, axis)
    segment = jnp.full(shape, BR_PER, I32)
    offset = row
    for k in range(BR_PER):
        start, size = meta_ref[base + k], meta_ref[base + BR_PER + k]
        inside = (row >= start) & (row < start + size)
        segment = jnp.where(inside, k, segment)
        offset = jnp.where(inside, row - start, offset)
    return segment, offset


def branch_kernel(
    meta_ref, x_ref, bc_ref, got_ref, dt_ref, rate_ref, xtaps_ref, taps_ref, skip_ref, z_ref,
    y_ref, c_ref, scale_ref, ext_ref, *, base,
):
    length, channels = x_ref.shape
    n_ctx, _, n_state = got_ref.shape
    width = taps_ref.shape[1]
    ext_ref[:HALO] = jnp.zeros((HALO, channels + width), F32)
    ext_ref[HALO:, :channels] = x_ref[...].astype(F32)
    ext_ref[HALO:, channels:] = bc_ref[:, width:].astype(F32)
    groups = (channels + width) // n_state
    misc = got_ref[0, : 8 * groups, :].astype(F32)
    for i in range(1, n_ctx):
        misc = misc + got_ref[i, : 8 * groups, :].astype(F32)
    tails = jnp.concatenate([misc[8 * g : 8 * (g + 1)] for g in range(groups)], axis=1)
    unused = iota(tails.shape, 0) % 4 == LOGS
    tails = jnp.where(unused, 0.0, tails)
    tails = jnp.concatenate([tails, jnp.zeros_like(tails)], axis=0).astype(BF)
    taps = jnp.concatenate([xtaps_ref[...].astype(F32), taps_ref[...].astype(F32)], axis=1)
    count = taps.shape[0]
    tail = count - 1
    segment, offset = segments(meta_ref, base, (length, 1), 0)
    place = iota((length, 16), 1)
    total = None
    for i in range(count):
        shift = tail - i
        rows = ext_ref[HALO - shift : HALO - shift + length]
        if shift:
            ahead = (offset < shift) & (segment < BR_PER)
            picker = ahead & (place == segment * 4 + tail - shift + offset)
            early = jnp.dot(picker.astype(BF), tails, preferred_element_type=F32)
            rows = jnp.where(offset >= shift, rows, 0.0) + early
        term = taps[i : i + 1] * rows
        total = term if total is None else total + term
    convolved = silu(total).astype(BF)
    values = convolved[:, :channels]
    b_rows = convolved[:, channels : channels + n_state]
    c_rows = convolved[:, channels + n_state :]
    c_ref[...] = c_rows
    step, log_decay, cumulative = step_and_logs(dt_ref[...], rate_ref[...])
    across, _ = segments(meta_ref, base, (1, length), 1)
    lane = iota(cumulative.shape, 1)
    before = cumulative - log_decay
    seed = jnp.zeros_like(cumulative)
    for k in range(BR_PER):
        first = jnp.sum(jnp.where(lane == meta_ref[base + k], before, 0.0), axis=1, keepdims=True)
        seed = jnp.where(across == k, jnp.exp(jnp.where(across == k, cumulative - first, 0.0)), seed)
    gate = silu(z_ref[...].astype(F32))
    scale_ref[...] = expand(seed.T, channels // seed.shape[0]) * gate
    scores = lax.dot_general(c_rows, b_rows, (((1,), (1,)), ((), ())), preferred_element_type=F32)
    mask = (segment == across) & (segment < BR_PER)
    mask = mask & (iota((length, length), 1) <= iota((length, length), 0))
    extra = values.astype(F32) * skip_ref[...]
    mixed_rows(values, scores, step, cumulative, mask, y_ref, extra, gate)


def gate_kernel(
    meta_ref, y_ref, scale_ref, c_ref, by_ref, bscale_ref, bc_ref, back_ref,
    g_ref, bg_ref, sq_ref, *, base,
):
    length, channels = y_ref.shape
    n_ctx, _, n_state = back_ref.shape
    rows = channels // n_ctx

    def from_state(c_rows, which):
        state = back_ref[:, which * rows : (which + 1) * rows, :].reshape(channels, n_state)
        return lax.dot_general(c_rows, state, (((1,), (1,)), ((), ())), preferred_element_type=F32)

    def squares(gated):
        ones = jnp.ones((8, channels), F32)
        return lax.dot_general(
            ones, gated * gated, (((1,), (1,)), ((), ())), precision=HIGH, preferred_element_type=F32
        )

    gated = y_ref[...] + scale_ref[...] * from_state(c_ref[...], 0)
    g_ref[...] = gated
    sums = squares(gated)
    segment, _ = segments(meta_ref, base, (length, 1), 0)
    c_rows = bc_ref[...]
    seeded = from_state(c_rows, BR_PER)
    for k in range(BR_PER - 1):
        seeded = jnp.where(segment == k, from_state(c_rows, 1 + k), seeded)
    gated = by_ref[...] + bscale_ref[...] * seeded
    bg_ref[...] = gated
    more = squares(gated)
    half = length // 2
    row = iota((8, half), 0)
    packed = jnp.where(
        row == 0,
        sums[:, :half],
        jnp.where(row == 1, sums[:, half:], jnp.where(row == 2, more[:, :half], more[:, half:])),
    )
    for i in range(sq_ref.shape[0]):
        sq_ref[i] = packed


def norm_kernel(meta_ref, sq_ref, g_ref, bg_ref, gain_ref, out_ref, bout_ref, *, base):
    length, channels = g_ref.shape
    n_tp = sq_ref.shape[0]
    total = sq_ref[0]
    for i in range(1, n_tp):
        total = total + sq_ref[i]
    factor = lax.rsqrt(total / (channels * n_tp) + EPSILON).T
    gain = gain_ref[...]
    half = length // 2
    segment, _ = segments(meta_ref, base, (length, 1), 0)
    for k in range(2):
        rows = slice(k * half, (k + 1) * half)
        out_ref[rows] = (g_ref[rows] * factor[:, k : k + 1] * gain).astype(BF)
        scaled = bg_ref[rows] * factor[:, 2 + k : 3 + k] * gain
        bout_ref[rows] = jnp.where(segment[rows] < BR_PER, scaled, 0.0).astype(BF)


def call(kernel, outs, scratch, args, smem=0, smem_out=False, grid=False):
    def where(scalar, shape):
        if grid and not scalar:
            return pl.BlockSpec(shape, lambda _, n=len(shape): (0,) * n)
        return pl.BlockSpec(memory_space=pltpu.SMEM if scalar else pltpu.VMEM)

    return pl.pallas_call(
        kernel,
        grid=(1,) if grid else (),
        in_specs=[where(i < smem, a.shape) for i, a in enumerate(args)],
        out_specs=[where(smem_out and i == 0, s) for i, (s, _) in enumerate(outs)],
        out_shape=[jax.ShapeDtypeStruct(s, t) for s, t in outs],
        scratch_shapes=[(pltpu.SMEM if len(s) == 1 else pltpu.VMEM)(s, t) for s, t in scratch],
        compiler_params=pltpu.CompilerParams(vmem_limit_bytes=24 * 2**20),
        cost_estimate=pl.CostEstimate(flops=2 * 10**9, bytes_accessed=4 * 10**6, transcendentals=10**6),
    )(*args)


def more_states(xc, b_rows, step, cumulative, positions, n_ctx):
    length, channels = xc.shape
    heads = step.shape[0]
    n_state = b_rows.shape[1]
    row = jnp.arange(length, dtype=I32)
    hit = row[None, None, :] == positions[:, None, None]
    ends = jnp.sum(jnp.where(hit, cumulative[None], 0.0), axis=2)
    inside = (row[None, :] <= positions[:, None])[:, None, :]
    weight = jnp.exp(jnp.where(inside, ends[:, :, None] - cumulative[None], FAR)) * step[None]
    values = xc.reshape(length, heads, -1).astype(F32)
    weighted = (jnp.transpose(weight, (0, 2, 1))[:, :, :, None] * values[None]).astype(BF)
    states = jnp.einsum("jshp,sn->jhpn", weighted, b_rows, preferred_element_type=F32).astype(BF)
    rows = channels // n_ctx
    count = positions.shape[0]
    states = jnp.transpose(states.reshape(count, n_ctx, rows, n_state), (1, 0, 2, 3))
    parts = []
    rest = ends
    for _ in range(3):
        part = lax.reduce_precision(rest, 8, 7)
        parts.append(part)
        rest = rest - part
    logs = jnp.stack(parts, axis=1).reshape(3 * count, heads).T
    logs = jnp.repeat(logs, n_ctx // heads, axis=0)
    logs = jnp.broadcast_to(logs[:, :, None], (n_ctx, 3 * count, n_state)).astype(BF)
    sent = jnp.concatenate([states.reshape(n_ctx, count * rows, n_state), logs], axis=1)
    return jnp.pad(sent, ((0, 0), (0, -sent.shape[1] % 16), (0, 0)))


def body(
    prefix_x, prefix_z, prefix_bc, prefix_dt, branch_x, branch_z, branch_bc, branch_dt,
    conv_x, conv_bc, decay_rate, skip, norm_gain, bound_pos, branch_owner, branch_parent, branch_len,
):
    n_ctx = lax.axis_size("ctx")
    n_tp = lax.axis_size("tp")
    me = lax.axis_index("ctx")
    length, channels = prefix_x.shape
    heads = decay_rate.shape[0]
    width = prefix_bc.shape[1]
    n_state = width // 2
    rows = channels // n_ctx
    bounds = bound_pos.shape[0]
    branches = branch_owner.shape[0]
    tail = conv_x.shape[0] - 1
    onward = [(i, i + 1) for i in range(n_ctx - 1)]

    [spread] = call(spread_kernel, [((n_tp, length // n_tp, 2 * width), BF)], [], [prefix_bc, branch_bc], grid=True)
    gathered = lax.all_to_all(spread, "tp", 0, 0, tiled=True).reshape(length, 2 * width)
    rates = decay_rate[:, None]
    skips = jnp.repeat(skip, channels // heads)[None]
    gain = norm_gain[None]
    order = jnp.arange(bounds, dtype=I32)
    block_of = bound_pos // length
    slot_of = jnp.sum(
        ((block_of[:, None] == block_of[None, :]) & (order[None, :] < order[:, None])).astype(I32), axis=1
    )

    at_tails = branches + 2 * bounds
    at_positions = at_tails + bounds
    at_mine = at_positions + SLOTS
    xrows = 8 * channels // n_state
    meta, xtails, last = call(
        functools.partial(index_kernel, n_ctx=n_ctx, n_state=n_state),
        [((at_mine + 2 * BR_PER,), I32), ((n_ctx, xrows, n_state), BF), ((HALO, channels), BF)],
        [((2 * n_ctx,), I32), ((branches,), I32), ((branches,), I32), ((bounds, 8, channels), F32)],
        [jnp.full((1,), me, I32), bound_pos, branch_owner, branch_parent, branch_len, prefix_x],
        smem=5,
        smem_out=True,
    )
    halo = lax.ppermute(last, "ctx", onward)
    xc, cumulative, step, weighted, first, logs = call(
        functools.partial(prefix_x_kernel, base=at_positions),
        [
            ((length, channels), BF),
            ((heads, length), F32),
            ((heads, length), F32),
            ((1 + SLOTS, length, channels), BF),
            ((1 + SLOTS, HALO, channels), F32),
            ((heads, n_state), F32),
        ],
        [((HALO + length, channels), F32)],
        [meta, prefix_x, prefix_dt, rates, conv_x],
        smem=1,
    )
    gathered, weighted = lax.optimization_barrier((gathered, weighted))
    bc_halo = lax.ppermute(gathered[length - HALO :, :width], "ctx", onward)
    sent, b_rows, c_rows, xfirst = call(
        functools.partial(prefix_state_kernel, base=at_positions, tail_base=at_tails),
        [((n_ctx, xrows + 16 + (1 + SLOTS) * rows, n_state), BF), ((length, n_state), BF), ((length, n_state), BF), ((HALO, channels), BF)],
        [((HALO + length, width), F32), ((bounds, 8, width), F32), ((2 * HALO, channels), F32)],
        [meta, prefix_x, halo, conv_x, gathered, bc_halo, conv_bc, weighted, first, logs, xtails],
        smem=1,
    )
    got = lax.all_to_all(sent, "ctx", 0, 0, tiled=True)
    y, scale = call(
        prefix_mix_kernel,
        [((length, channels), F32), ((length, channels), F32)],
        [],
        [xc, xfirst, b_rows, c_rows, cumulative, step, skips, prefix_z],
    )
    got, y, scale = lax.optimization_barrier((got, y, scale))

    scan = functools.partial(scan_kernel, n_branch=branches, bounds=bounds)
    scan_out = [((n_ctx, (1 + BR_PER) * rows, n_state), BF)]
    scan_scratch = [
        ((n_ctx, rows, n_state), F32),
        ((bounds, rows, n_state), F32),
        ((1 + SLOTS, n_ctx, n_state), F32),
    ]

    def usual():
        return call(scan, scan_out, scan_scratch, [meta, got], smem=1, grid=True)[0]

    def crowded():
        here = (block_of == me)[None, :] & (slot_of[None, :] == order[SLOTS:, None])
        positions = jnp.sum(jnp.where(here, (bound_pos - block_of * length + 1)[None, :], 0), axis=1) - 1
        whole = jnp.concatenate([xfirst, xc[HALO:]], axis=0)
        extra = more_states(whole, b_rows, step, cumulative, positions, n_ctx)
        extra = lax.all_to_all(extra, "ctx", 0, 0, tiled=True)
        return call(scan, scan_out, scan_scratch, [meta, got, extra], smem=1)[0]

    back = lax.cond(jnp.max(slot_of) >= SLOTS, crowded, usual)
    back = lax.all_to_all(back, "ctx", 0, 0, tiled=True)

    branch_y, branch_c, branch_scale = call(
        functools.partial(branch_kernel, base=at_mine),
        [((length, channels), F32), ((length, n_state), BF), ((length, channels), F32)],
        [((HALO + length, channels + width), F32)],
        [meta, branch_x, gathered, got, branch_dt, rates, conv_x, conv_bc, skips, branch_z],
        smem=1,
    )
    gated, branch_gated, squares = call(
        functools.partial(gate_kernel, base=at_mine),
        [((length, channels), F32), ((length, channels), F32), ((n_tp, 8, length // 2), F32)],
        [],
        [meta, y, scale, c_rows, branch_y, branch_scale, branch_c, back],
        smem=1,
    )
    squares = lax.all_to_all(squares, "tp", 0, 0, tiled=True)
    return tuple(
        call(
            functools.partial(norm_kernel, base=at_mine),
            [((length, channels), BF), ((length, channels), BF)],
            [],
            [meta, squares, gated, branch_gated, gain],
            smem=1,
            grid=True,
        )
    )


def solution(mesh):
    both = P(("ctx", "tp"), None)
    in_specs = (
        P("ctx", "tp"), P("ctx", "tp"), both, P("tp", "ctx"),
        P("ctx", "tp"), P("ctx", "tp"), both, P("tp", "ctx"),
        P(None, "tp"), P(), P("tp"), P("tp"), P("tp"), P(), P(), P(), P(),
    )
    out_specs = (P("ctx", "tp"), P("ctx", "tp"))
    return jax.shard_map(body, mesh=mesh, in_specs=in_specs, out_specs=out_specs, check_vma=False)
```

```python
import functools

import jax
import jax.numpy as jnp
from jax import lax
from jax.experimental import pallas as pl
from jax.experimental.pallas import tpu as pltpu
from jax.sharding import PartitionSpec as P

BR_PER = 2
EPSILON = 1e-05
SLOTS = 2
LOGS = 3
HALO = 16
BF = jnp.bfloat16
F32 = jnp.float32
I32 = jnp.int32
HIGH = lax.Precision.HIGHEST
FAR = -1e30


def iota(shape, axis):
    return lax.broadcasted_iota(I32, shape, axis)


def parts_of(value, count):
    found = []
    for _ in range(count):
        part = value.astype(BF)
        found.append(part)
        value = value - part.astype(F32)
    return found


def expand(columns, head_size):
    rows, heads = columns.shape
    low = iota((rows, 2 * head_size), 1) < head_size
    pairs = [
        jnp.where(low, columns[:, h : h + 1], columns[:, h + 1 : h + 2]) for h in range(0, heads, 2)
    ]
    return jnp.concatenate(pairs, axis=1)


def step_and_logs(raw, rates):
    step = jnp.maximum(raw, 0.0) + jnp.log1p(jnp.exp(-jnp.abs(raw)))
    log_decay = -rates * step
    length = raw.shape[1]
    upper = (iota((length, length), 0) <= iota((length, length), 1)).astype(F32)
    cumulative = jnp.dot(log_decay, upper, precision=HIGH, preferred_element_type=F32)
    return step, log_decay, cumulative


def silu(value):
    return value * jax.nn.sigmoid(value)


def mixed_rows(values, scores, step, cumulative, mask, out_ref, extra, gate):
    length, channels = values.shape
    heads = step.shape[0]
    size = channels // heads
    columns = cumulative.T
    half = length // 2
    low = iota((half, 2 * size), 1) < size
    for first, width in ((0, half), (half, length)):
        rows = slice(first, first + half)
        kept = mask[rows, :width]
        score = scores[rows, :width]
        for h in range(0, heads, 2):
            lanes = slice(h * size, (h + 2) * size)
            sums = []
            for one in (h, h + 1):
                gap = columns[rows, one : one + 1] - cumulative[one : one + 1, :width]
                mixing = score * jnp.exp(jnp.where(kept, gap, FAR)) * step[one : one + 1, :width]
                sums.append(jnp.dot(mixing.astype(BF), values[:width, lanes], preferred_element_type=F32))
            out_ref[rows, lanes] = (jnp.where(low, sums[0], sums[1]) + extra[rows, lanes]) * gate[rows, lanes]


def prefix_x_kernel(
    meta_ref, x_ref, dt_ref, rate_ref, taps_ref,
    xc_ref, cum_ref, step_ref, weighted_ref, first_ref, logs_ref, ext_ref, *, base,
):
    length, channels = x_ref.shape
    heads = rate_ref.shape[0]
    ext_ref[:HALO] = jnp.zeros((HALO, channels), F32)
    ext_ref[HALO:] = x_ref[...].astype(F32)
    taps = taps_ref[...].astype(F32)
    count = taps.shape[0]
    total = taps[0:1] * ext_ref[HALO - count + 1 : HALO - count + 1 + length]
    for i in range(1, count):
        first = HALO - count + 1 + i
        total = total + taps[i : i + 1] * ext_ref[first : first + length]
    values = silu(total).astype(BF)
    xc_ref[...] = values
    step, _, cumulative = step_and_logs(dt_ref[...], rate_ref[...])
    cum_ref[...] = cumulative
    step_ref[...] = step
    lane = iota((heads, length), 1)

    def weigh(at, weight):
        wide = expand(weight.T, channels // heads)
        first_ref[at] = wide[:HALO]
        weighted_ref[at] = (xc_ref[...].astype(F32) * wide).astype(BF)

    ends = [cumulative[:, length - 1 :]]
    weigh(0, jnp.exp(ends[0] - cumulative) * step)
    for slot in range(SLOTS):
        position = meta_ref[base + slot]
        end = jnp.sum(jnp.where(lane == position, cumulative, 0.0), axis=1, keepdims=True)
        ends.append(end)

        @pl.when(position >= 0)
        def _():
            weigh(1 + slot, jnp.exp(jnp.where(lane <= position, end - cumulative, FAR)) * step)

    spot = iota(logs_ref.shape, 1)
    logs = jnp.zeros(logs_ref.shape, F32)
    for at, part in enumerate(part for end in ends for part in parts_of(end, 3)):
        logs = jnp.where(spot == at, part.astype(F32), logs)
    logs_ref[...] = logs


def tail_tiles(meta_ref, base, rows, out_ref):
    bounds, height, width = out_ref.shape
    row = iota((bounds * height, 1), 0)
    wanted = jnp.full(row.shape, -1, I32)
    for j in range(bounds):
        wanted = jnp.where(row // height == j, meta_ref[base + j] + row % 4, wanted)
    wanted = jnp.where(row % 4 < 3, wanted, -1)
    picker = (iota((bounds * height, rows.shape[0]), 1) == wanted).astype(BF)
    picked = jnp.dot(picker, rows, preferred_element_type=F32)
    out_ref[...] = picked.reshape(bounds, height, width)


def index_kernel(
    me_ref, bound_ref, owner_ref, parent_ref, len_ref, x_ref,
    meta_ref, tails_ref, last_ref, count_ref, start_ref, size_ref, tile_ref, *, n_ctx, n_state,
):
    me = me_ref[0]
    length = x_ref.shape[0]
    bounds = bound_ref.shape[0]
    branches = owner_ref.shape[0]

    def clear(o, _):
        count_ref[o] = 0
        count_ref[n_ctx + o] = 0
        return 0

    lax.fori_loop(0, n_ctx, clear, 0)

    def place(b, _):
        owner = owner_ref[b]
        rank = count_ref[owner]
        start = count_ref[n_ctx + owner]
        size = len_ref[b]
        count_ref[owner] = rank + 1
        count_ref[n_ctx + owner] = start + size
        at = owner * BR_PER + rank
        meta_ref[at] = parent_ref[b]
        start_ref[at] = start
        size_ref[at] = size
        return 0

    lax.fori_loop(0, branches, place, 0)
    blocks = [lax.div(bound_ref[j], length) for j in range(bounds)]
    at = branches
    for k in range(SLOTS):
        meta_ref[at + 3 * bounds + k] = -1
    for j in range(bounds):
        slot = jnp.int32(0)
        for i in range(j):
            slot = slot + (blocks[i] == blocks[j]).astype(I32)
        meta_ref[at + j] = blocks[j]
        meta_ref[at + bounds + j] = slot
        meta_ref[at + 2 * bounds + j] = bound_ref[j] - me * length - 2

        @pl.when((blocks[j] == me) & (slot < SLOTS))
        def _():
            meta_ref[at + 3 * bounds + slot] = bound_ref[j] - me * length

    for k in range(BR_PER):
        meta_ref[at + 3 * bounds + SLOTS + k] = start_ref[me * BR_PER + k]
        meta_ref[at + 3 * bounds + SLOTS + BR_PER + k] = size_ref[me * BR_PER + k]
    last_ref[...] = x_ref[length - HALO :, :]
    tail_tiles(meta_ref, at + 2 * bounds, x_ref[...], tile_ref)
    upper = iota((8, n_state), 0) < 4
    groups = x_ref.shape[1] // n_state
    for o in range(n_ctx):
        first, second = (meta_ref[o * BR_PER + k] for k in range(BR_PER))
        tiles = []
        for g in range(groups):
            lanes = slice(g * n_state, (g + 1) * n_state)
            tiles.append(jnp.where(upper, tile_ref[first, :, lanes], tile_ref[second, :, lanes]))
        tails_ref[o] = jnp.concatenate(tiles, axis=0).astype(BF)


def convolve(ext_ref, taps_ref, first, height):
    taps = taps_ref[...].astype(F32)
    count = taps.shape[0]
    total = taps[0:1] * ext_ref[first - count + 1 : first - count + 1 + height]
    for i in range(1, count):
        start = first - count + 1 + i
        total = total + taps[i : i + 1] * ext_ref[start : start + height]
    return silu(total).astype(BF)


def over_rows(weighted, b_rows):
    return lax.dot_general(weighted, b_rows, (((0,), (0,)), ((), ())), preferred_element_type=F32)


def prefix_later_kernel(
    meta_ref, bc_ref, taps_ref, weighted_ref, logs_ref, xtails_ref,
    part_ref, misc_ref, conv_ref, ext_ref, tile_ref, *, base, tail_base,
):
    _, length, channels = weighted_ref.shape
    width = taps_ref.shape[1]
    n_state = width // 2
    n_ctx, xrows, _ = xtails_ref.shape
    heads = logs_ref.shape[0]
    bc = bc_ref[:, :width]
    ext_ref[...] = bc.astype(F32)
    convolved = convolve(ext_ref, taps_ref, HALO, length - HALO)
    conv_ref[HALO:] = convolved
    part_ref[0] = over_rows(weighted_ref[0, HALO:, :], convolved[:, :n_state])
    for slot in range(SLOTS):

        @pl.when(meta_ref[base + slot] >= 0)
        def _():
            part_ref[1 + slot] = over_rows(weighted_ref[1 + slot, HALO:, :], convolved[:, :n_state])

    misc_ref[:, :xrows, :] = xtails_ref[...]
    tail_tiles(meta_ref, tail_base, bc, tile_ref)
    row = iota((8, n_state), 0)
    per_head = n_ctx // heads
    for o in range(n_ctx):
        first, second = (meta_ref[o * BR_PER + k] for k in range(BR_PER))
        tails = []
        for g in range(2):
            lanes = slice(g * n_state, (g + 1) * n_state)
            tails.append(jnp.where(row < 4, tile_ref[first, :, lanes], tile_ref[second, :, lanes]))
        h = o // per_head
        tails[0] = jnp.where(row == LOGS, logs_ref[h : h + 1], tails[0])
        misc_ref[o, xrows:, :] = jnp.concatenate(tails, axis=0).astype(BF)


def prefix_state_kernel(
    meta_ref, x_ref, halo_ref, xtaps_ref, bc_ref, bchalo_ref, taps_ref, first_ref, part_ref, misc_ref, conv_ref,
    sent_ref, b_ref, c_ref, xfirst_ref, ext_ref, edge_ref, *, base,
):
    channels = x_ref.shape[1]
    width = taps_ref.shape[1]
    n_state = width // 2
    n_ctx, misc, _ = misc_ref.shape
    rows = channels // n_ctx
    ext_ref[:HALO] = bchalo_ref[...].astype(F32)
    ext_ref[HALO:] = bc_ref[:HALO, :width].astype(F32)
    convolved = convolve(ext_ref, taps_ref, HALO, HALO)
    b_rows = convolved[:, :n_state]
    b_ref[:HALO] = b_rows
    b_ref[HALO:] = conv_ref[HALO:, :n_state]
    c_ref[:HALO] = convolved[:, n_state:]
    c_ref[HALO:] = conv_ref[HALO:, n_state:]
    edge_ref[:HALO] = halo_ref[...].astype(F32)
    edge_ref[HALO:] = x_ref[:HALO].astype(F32)
    xfirst = convolve(edge_ref, xtaps_ref, HALO, HALO)
    xfirst_ref[...] = xfirst

    def send(at):
        weighted = (xfirst.astype(F32) * first_ref[at]).astype(BF)
        state = part_ref[at] + over_rows(weighted, b_rows)
        start = misc + at * rows
        sent_ref[:, start : start + rows, :] = state.astype(BF).reshape(n_ctx, rows, n_state)

    sent_ref[:, :misc, :] = misc_ref[...]
    send(0)
    for slot in range(SLOTS):
        position = meta_ref[base + slot]
        start = misc + (1 + slot) * rows

        @pl.when(position >= 0)
        def _():
            send(1 + slot)

        @pl.when(position < 0)
        def _():
            sent_ref[:, start : start + rows, :] = jnp.zeros((n_ctx, rows, n_state), BF)


def prefix_mix_kernel(xc_ref, xfirst_ref, b_ref, c_ref, cum_ref, step_ref, skip_ref, z_ref, y_ref, scale_ref):
    length, channels = xc_ref.shape
    scores = lax.dot_general(
        c_ref[...], b_ref[...], (((1,), (1,)), ((), ())), preferred_element_type=F32
    )
    mask = iota((length, length), 1) <= iota((length, length), 0)
    values = jnp.concatenate([xfirst_ref[...], xc_ref[HALO:]], axis=0)
    cumulative = cum_ref[...]
    gate = silu(z_ref[...].astype(F32))
    scale_ref[...] = expand(jnp.exp(cumulative).T, channels // cumulative.shape[0]) * gate
    extra = values.astype(F32) * skip_ref[...]
    mixed_rows(values, scores, step_ref[...], cumulative, mask, y_ref, extra, gate)


def scan_kernel(meta_ref, got_ref, *rest, n_branch, bounds):
    extra_ref = rest[0] if len(rest) == 5 else None
    back_ref, entering_ref, bound_ref, log_ref = rest[-4:]
    n_ctx, sent_rows, n_state = got_ref.shape
    rows = entering_ref.shape[1]
    misc = sent_rows - (1 + SLOTS) * rows
    parts = got_ref[:, misc - 16 : misc, :].astype(F32)[:, LOGS, :]
    for v in range(1 + SLOTS):
        log = parts[:, 3 * v : 3 * v + 1] + parts[:, 3 * v + 1 : 3 * v + 2] + parts[:, 3 * v + 2 : 3 * v + 3]
        log_ref[v] = jnp.broadcast_to(log, (n_ctx, n_state))
    state = jnp.zeros((rows, n_state), F32)
    for i in range(n_ctx):
        entering_ref[i] = state
        back_ref[i, :rows, :] = state.astype(BF)
        if i < n_ctx - 1:
            local = got_ref[i, misc : misc + rows, :].astype(F32)
            state = jnp.exp(log_ref[0, i : i + 1]) * state + local
    for j in range(bounds):
        block = meta_ref[n_branch + j]
        slot = meta_ref[n_branch + bounds + j]
        log = log_ref[1, pl.ds(block, 1)]
        part = got_ref[block, misc + rows : misc + 2 * rows, :].astype(F32)
        for other in range(1, SLOTS):
            first = misc + (1 + other) * rows
            log = jnp.where(slot == other, log_ref[1 + other, pl.ds(block, 1)], log)
            part = jnp.where(slot == other, got_ref[block, first : first + rows, :].astype(F32), part)
        if extra_ref is not None:
            tail = extra_ref[block, (bounds - SLOTS) * rows :, :].astype(F32)
            for more in range(bounds - SLOTS):
                here = slot == SLOTS + more
                three = tail[3 * more : 3 * more + 1] + tail[3 * more + 1 : 3 * more + 2] + tail[3 * more + 2 : 3 * more + 3]
                log = jnp.where(here, three, log)
                part = jnp.where(here, extra_ref[block, more * rows : (more + 1) * rows, :].astype(F32), part)
        bound_ref[j] = jnp.exp(log) * entering_ref[block] + part
    for o in range(n_ctx):
        for k in range(BR_PER):
            first = (1 + k) * rows
            back_ref[o, first : first + rows, :] = bound_ref[meta_ref[o * BR_PER + k]].astype(BF)


def segments(meta_ref, base, shape, axis):
    row = iota(shape, axis)
    segment = jnp.full(shape, BR_PER, I32)
    offset = row
    for k in range(BR_PER):
        start, size = meta_ref[base + k], meta_ref[base + BR_PER + k]
        inside = (row >= start) & (row < start + size)
        segment = jnp.where(inside, k, segment)
        offset = jnp.where(inside, row - start, offset)
    return segment, offset


def branch_kernel(
    meta_ref, x_ref, bc_ref, got_ref, dt_ref, rate_ref, xtaps_ref, taps_ref, skip_ref, z_ref,
    y_ref, c_ref, scale_ref, ext_ref, *, base,
):
    length, channels = x_ref.shape
    n_ctx, _, n_state = got_ref.shape
    width = taps_ref.shape[1]
    ext_ref[:HALO] = jnp.zeros((HALO, channels + width), F32)
    ext_ref[HALO:, :channels] = x_ref[...].astype(F32)
    ext_ref[HALO:, channels:] = bc_ref[:, width:].astype(F32)
    groups = (channels + width) // n_state
    misc = got_ref[0, : 8 * groups, :].astype(F32)
    for i in range(1, n_ctx):
        misc = misc + got_ref[i, : 8 * groups, :].astype(F32)
    tails = jnp.concatenate([misc[8 * g : 8 * (g + 1)] for g in range(groups)], axis=1)
    unused = iota(tails.shape, 0) % 4 == LOGS
    tails = jnp.where(unused, 0.0, tails)
    tails = jnp.concatenate([tails, jnp.zeros_like(tails)], axis=0).astype(BF)
    taps = jnp.concatenate([xtaps_ref[...].astype(F32), taps_ref[...].astype(F32)], axis=1)
    count = taps.shape[0]
    tail = count - 1
    segment, offset = segments(meta_ref, base, (length, 1), 0)
    place = iota((length, 16), 1)
    total = None
    for i in range(count):
        shift = tail - i
        rows = ext_ref[HALO - shift : HALO - shift + length]
        if shift:
            ahead = (offset < shift) & (segment < BR_PER)
            picker = ahead & (place == segment * 4 + tail - shift + offset)
            early = jnp.dot(picker.astype(BF), tails, preferred_element_type=F32)
            rows = jnp.where(offset >= shift, rows, 0.0) + early
        term = taps[i : i + 1] * rows
        total = term if total is None else total + term
    convolved = silu(total).astype(BF)
    values = convolved[:, :channels]
    b_rows = convolved[:, channels : channels + n_state]
    c_rows = convolved[:, channels + n_state :]
    c_ref[...] = c_rows
    step, log_decay, cumulative = step_and_logs(dt_ref[...], rate_ref[...])
    across, _ = segments(meta_ref, base, (1, length), 1)
    lane = iota(cumulative.shape, 1)
    before = cumulative - log_decay
    seed = jnp.zeros_like(cumulative)
    for k in range(BR_PER):
        first = jnp.sum(jnp.where(lane == meta_ref[base + k], before, 0.0), axis=1, keepdims=True)
        seed = jnp.where(across == k, jnp.exp(jnp.where(across == k, cumulative - first, 0.0)), seed)
    gate = silu(z_ref[...].astype(F32))
    scale_ref[...] = expand(seed.T, channels // seed.shape[0]) * gate
    scores = lax.dot_general(c_rows, b_rows, (((1,), (1,)), ((), ())), preferred_element_type=F32)
    mask = (segment == across) & (segment < BR_PER)
    mask = mask & (iota((length, length), 1) <= iota((length, length), 0))
    extra = values.astype(F32) * skip_ref[...]
    mixed_rows(values, scores, step, cumulative, mask, y_ref, extra, gate)


def gate_kernel(
    meta_ref, y_ref, scale_ref, c_ref, by_ref, bscale_ref, bc_ref, back_ref,
    g_ref, bg_ref, sq_ref, *, base,
):
    length, channels = y_ref.shape
    n_ctx, _, n_state = back_ref.shape
    rows = channels // n_ctx

    def from_state(c_rows, which):
        state = back_ref[:, which * rows : (which + 1) * rows, :].reshape(channels, n_state)
        return lax.dot_general(c_rows, state, (((1,), (1,)), ((), ())), preferred_element_type=F32)

    def squares(gated):
        square = gated * gated
        total = square[:, :n_state]
        for at in range(n_state, channels, n_state):
            total = total + square[:, at : at + n_state]
        ones = jnp.ones((8, n_state), F32)
        return lax.dot_general(
            ones, total, (((1,), (1,)), ((), ())), precision=HIGH, preferred_element_type=F32
        )

    gated = y_ref[...] + scale_ref[...] * from_state(c_ref[...], 0)
    g_ref[...] = gated
    sums = squares(gated)
    segment, _ = segments(meta_ref, base, (length, 1), 0)
    c_rows = bc_ref[...]
    seeded = from_state(c_rows, BR_PER)
    for k in range(BR_PER - 1):
        seeded = jnp.where(segment == k, from_state(c_rows, 1 + k), seeded)
    gated = by_ref[...] + bscale_ref[...] * seeded
    bg_ref[...] = gated
    more = squares(gated)
    half = length // 2
    row = iota((8, half), 0)
    packed = jnp.where(
        row == 0,
        sums[:, :half],
        jnp.where(row == 1, sums[:, half:], jnp.where(row == 2, more[:, :half], more[:, half:])),
    )
    for i in range(sq_ref.shape[0]):
        sq_ref[i] = packed


def norm_kernel(meta_ref, sq_ref, g_ref, bg_ref, gain_ref, out_ref, bout_ref, *, base):
    length, channels = g_ref.shape
    n_tp = sq_ref.shape[0]
    total = sq_ref[0]
    for i in range(1, n_tp):
        total = total + sq_ref[i]
    factor = lax.rsqrt(total / (channels * n_tp) + EPSILON).T
    gain = gain_ref[...]
    half = length // 2
    segment, _ = segments(meta_ref, base, (length, 1), 0)
    for k in range(2):
        rows = slice(k * half, (k + 1) * half)
        out_ref[rows] = (g_ref[rows] * factor[:, k : k + 1] * gain).astype(BF)
        scaled = bg_ref[rows] * factor[:, 2 + k : 3 + k] * gain
        bout_ref[rows] = jnp.where(segment[rows] < BR_PER, scaled, 0.0).astype(BF)


def call(kernel, outs, scratch, args, smem=0, smem_out=False, grid=False):
    def where(scalar, shape):
        if grid and not scalar:
            return pl.BlockSpec(shape, lambda _, n=len(shape): (0,) * n)
        return pl.BlockSpec(memory_space=pltpu.SMEM if scalar else pltpu.VMEM)

    return pl.pallas_call(
        kernel,
        grid=(1,) if grid else (),
        in_specs=[where(i < smem, a.shape) for i, a in enumerate(args)],
        out_specs=[where(smem_out and i == 0, s) for i, (s, _) in enumerate(outs)],
        out_shape=[jax.ShapeDtypeStruct(s, t) for s, t in outs],
        scratch_shapes=[(pltpu.SMEM if len(s) == 1 else pltpu.VMEM)(s, t) for s, t in scratch],
        compiler_params=pltpu.CompilerParams(vmem_limit_bytes=24 * 2**20),
        cost_estimate=pl.CostEstimate(flops=2 * 10**9, bytes_accessed=4 * 10**6, transcendentals=10**6),
    )(*args)


def more_states(xc, b_rows, step, cumulative, positions, n_ctx):
    length, channels = xc.shape
    heads = step.shape[0]
    n_state = b_rows.shape[1]
    row = jnp.arange(length, dtype=I32)
    hit = row[None, None, :] == positions[:, None, None]
    ends = jnp.sum(jnp.where(hit, cumulative[None], 0.0), axis=2)
    inside = (row[None, :] <= positions[:, None])[:, None, :]
    weight = jnp.exp(jnp.where(inside, ends[:, :, None] - cumulative[None], FAR)) * step[None]
    values = xc.reshape(length, heads, -1).astype(F32)
    weighted = (jnp.transpose(weight, (0, 2, 1))[:, :, :, None] * values[None]).astype(BF)
    states = jnp.einsum("jshp,sn->jhpn", weighted, b_rows, preferred_element_type=F32).astype(BF)
    rows = channels // n_ctx
    count = positions.shape[0]
    states = jnp.transpose(states.reshape(count, n_ctx, rows, n_state), (1, 0, 2, 3))
    parts = []
    rest = ends
    for _ in range(3):
        part = lax.reduce_precision(rest, 8, 7)
        parts.append(part)
        rest = rest - part
    logs = jnp.stack(parts, axis=1).reshape(3 * count, heads).T
    logs = jnp.repeat(logs, n_ctx // heads, axis=0)
    logs = jnp.broadcast_to(logs[:, :, None], (n_ctx, 3 * count, n_state)).astype(BF)
    sent = jnp.concatenate([states.reshape(n_ctx, count * rows, n_state), logs], axis=1)
    return jnp.pad(sent, ((0, 0), (0, -sent.shape[1] % 16), (0, 0)))


def body(
    prefix_x, prefix_z, prefix_bc, prefix_dt, branch_x, branch_z, branch_bc, branch_dt,
    conv_x, conv_bc, decay_rate, skip, norm_gain, bound_pos, branch_owner, branch_parent, branch_len,
):
    n_ctx = lax.axis_size("ctx")
    n_tp = lax.axis_size("tp")
    me = lax.axis_index("ctx")
    length, channels = prefix_x.shape
    heads = decay_rate.shape[0]
    width = prefix_bc.shape[1]
    n_state = width // 2
    rows = channels // n_ctx
    bounds = bound_pos.shape[0]
    branches = branch_owner.shape[0]
    tail = conv_x.shape[0] - 1
    onward = [(i, i + 1) for i in range(n_ctx - 1)]

    own = jnp.concatenate([prefix_bc, branch_bc], axis=1)
    spread = jnp.broadcast_to(own[None], (n_tp, *own.shape))
    gathered = lax.all_to_all(spread, "tp", 0, 0, tiled=True).reshape(length, 2 * width)
    rates = decay_rate[:, None]
    skips = jnp.repeat(skip, channels // heads)[None]
    gain = norm_gain[None]
    order = jnp.arange(bounds, dtype=I32)
    block_of = bound_pos // length
    slot_of = jnp.sum(
        ((block_of[:, None] == block_of[None, :]) & (order[None, :] < order[:, None])).astype(I32), axis=1
    )

    at_tails = branches + 2 * bounds
    at_positions = at_tails + bounds
    at_mine = at_positions + SLOTS
    xrows = 8 * channels // n_state
    meta, xtails, last = call(
        functools.partial(index_kernel, n_ctx=n_ctx, n_state=n_state),
        [((at_mine + 2 * BR_PER,), I32), ((n_ctx, xrows, n_state), BF), ((HALO, channels), BF)],
        [((2 * n_ctx,), I32), ((branches,), I32), ((branches,), I32), ((bounds, 8, channels), F32)],
        [jnp.full((1,), me, I32), bound_pos, branch_owner, branch_parent, branch_len, prefix_x],
        smem=5,
        smem_out=True,
    )
    halo = lax.ppermute(last, "ctx", onward)
    xc, cumulative, step, weighted, first, logs = call(
        functools.partial(prefix_x_kernel, base=at_positions),
        [
            ((length, channels), BF),
            ((heads, length), F32),
            ((heads, length), F32),
            ((1 + SLOTS, length, channels), BF),
            ((1 + SLOTS, HALO, channels), F32),
            ((heads, n_state), F32),
        ],
        [((HALO + length, channels), F32)],
        [meta, prefix_x, prefix_dt, rates, conv_x],
        smem=1,
    )
    gathered, weighted = lax.optimization_barrier((gathered, weighted))
    bc_halo = lax.ppermute(gathered[length - HALO :, :width], "ctx", onward)
    part, misc, convolved = call(
        functools.partial(prefix_later_kernel, base=at_positions, tail_base=at_tails),
        [
            ((1 + SLOTS, channels, n_state), F32),
            ((n_ctx, xrows + 16, n_state), BF),
            ((length, width), BF),
        ],
        [((length, width), F32), ((bounds, 8, width), F32)],
        [meta, gathered, conv_bc, weighted, logs, xtails],
        smem=1,
    )
    sent, b_rows, c_rows, xfirst = call(
        functools.partial(prefix_state_kernel, base=at_positions),
        [
            ((n_ctx, xrows + 16 + (1 + SLOTS) * rows, n_state), BF),
            ((length, n_state), BF),
            ((length, n_state), BF),
            ((HALO, channels), BF),
        ],
        [((2 * HALO, width), F32), ((2 * HALO, channels), F32)],
        [meta, prefix_x, halo, conv_x, gathered, bc_halo, conv_bc, first, part, misc, convolved],
        smem=1,
    )
    got = lax.all_to_all(sent, "ctx", 0, 0, tiled=True)
    y, scale = call(
        prefix_mix_kernel,
        [((length, channels), F32), ((length, channels), F32)],
        [],
        [xc, xfirst, b_rows, c_rows, cumulative, step, skips, prefix_z],
    )

    scan = functools.partial(scan_kernel, n_branch=branches, bounds=bounds)
    scan_out = [((n_ctx, (1 + BR_PER) * rows, n_state), BF)]
    scan_scratch = [
        ((n_ctx, rows, n_state), F32),
        ((bounds, rows, n_state), F32),
        ((1 + SLOTS, n_ctx, n_state), F32),
    ]

    def usual():
        return call(scan, scan_out, scan_scratch, [meta, got], smem=1, grid=True)[0]

    def crowded():
        here = (block_of == me)[None, :] & (slot_of[None, :] == order[SLOTS:, None])
        positions = jnp.sum(jnp.where(here, (bound_pos - block_of * length + 1)[None, :], 0), axis=1) - 1
        whole = jnp.concatenate([xfirst, xc[HALO:]], axis=0)
        extra = more_states(whole, b_rows, step, cumulative, positions, n_ctx)
        extra = lax.all_to_all(extra, "ctx", 0, 0, tiled=True)
        return call(scan, scan_out, scan_scratch, [meta, got, extra], smem=1)[0]

    back = lax.cond(jnp.max(slot_of) >= SLOTS, crowded, usual)
    back = lax.all_to_all(back, "ctx", 0, 0, tiled=True)

    branch_y, branch_c, branch_scale = call(
        functools.partial(branch_kernel, base=at_mine),
        [((length, channels), F32), ((length, n_state), BF), ((length, channels), F32)],
        [((HALO + length, channels + width), F32)],
        [meta, branch_x, gathered, got, branch_dt, rates, conv_x, conv_bc, skips, branch_z],
        smem=1,
    )
    gated, branch_gated, squares = call(
        functools.partial(gate_kernel, base=at_mine),
        [((length, channels), F32), ((length, channels), F32), ((n_tp, 8, length // 2), F32)],
        [],
        [meta, y, scale, c_rows, branch_y, branch_scale, branch_c, back],
        smem=1,
    )
    squares = lax.all_to_all(squares, "tp", 0, 0, tiled=True)
    return tuple(
        call(
            functools.partial(norm_kernel, base=at_mine),
            [((length, channels), BF), ((length, channels), BF)],
            [],
            [meta, squares, gated, branch_gated, gain],
            smem=1,
            grid=True,
        )
    )


def solution(mesh):
    both = P(("ctx", "tp"), None)
    in_specs = (
        P("ctx", "tp"), P("ctx", "tp"), both, P("tp", "ctx"),
        P("ctx", "tp"), P("ctx", "tp"), both, P("tp", "ctx"),
        P(None, "tp"), P(), P("tp"), P("tp"), P("tp"), P(), P(), P(), P(),
    )
    out_specs = (P("ctx", "tp"), P("ctx", "tp"))
    return jax.shard_map(body, mesh=mesh, in_specs=in_specs, out_specs=out_specs, check_vma=False)
```

```python
import functools

import jax
import jax.numpy as jnp
from jax import lax
from jax.experimental import pallas as pl
from jax.experimental.pallas import tpu as pltpu
from jax.sharding import PartitionSpec as P

BR_PER = 2
EPSILON = 1e-05
SLOTS = 2
LOGS = 3
HALO = 16
BF = jnp.bfloat16
F32 = jnp.float32
I32 = jnp.int32
HIGH = lax.Precision.HIGHEST
FAR = -1e30


def iota(shape, axis):
    return lax.broadcasted_iota(I32, shape, axis)


def parts_of(value, count):
    found = []
    for _ in range(count):
        part = value.astype(BF)
        found.append(part)
        value = value - part.astype(F32)
    return found


def expand(columns, head_size):
    rows, heads = columns.shape
    low = iota((rows, 2 * head_size), 1) < head_size
    pairs = [
        jnp.where(low, columns[:, h : h + 1], columns[:, h + 1 : h + 2]) for h in range(0, heads, 2)
    ]
    return jnp.concatenate(pairs, axis=1)


def step_and_logs(raw, rates):
    step = jnp.maximum(raw, 0.0) + jnp.log1p(jnp.exp(-jnp.abs(raw)))
    log_decay = -rates * step
    length = raw.shape[1]
    upper = (iota((length, length), 0) <= iota((length, length), 1)).astype(F32)
    cumulative = jnp.dot(log_decay, upper, precision=HIGH, preferred_element_type=F32)
    return step, log_decay, cumulative


def silu(value):
    return value * jax.nn.sigmoid(value)


def mixed_rows(values, scores, step, cumulative, mask, out_ref, extra, gate):
    length, channels = values.shape
    heads = step.shape[0]
    size = channels // heads
    columns = cumulative.T
    half = length // 2
    low = iota((half, 2 * size), 1) < size
    for first, width in ((0, half), (half, length)):
        rows = slice(first, first + half)
        kept = mask[rows, :width]
        score = scores[rows, :width]
        for h in range(0, heads, 2):
            lanes = slice(h * size, (h + 2) * size)
            sums = []
            for one in (h, h + 1):
                gap = columns[rows, one : one + 1] - cumulative[one : one + 1, :width]
                mixing = score * jnp.exp(jnp.where(kept, gap, FAR)) * step[one : one + 1, :width]
                sums.append(jnp.dot(mixing.astype(BF), values[:width, lanes], preferred_element_type=F32))
            out_ref[rows, lanes] = (jnp.where(low, sums[0], sums[1]) + extra[rows, lanes]) * gate[rows, lanes]


def prefix_x_kernel(
    meta_ref, x_ref, dt_ref, rate_ref, taps_ref,
    xc_ref, cum_ref, step_ref, weighted_ref, first_ref, logs_ref, ext_ref, *, base,
):
    length, channels = x_ref.shape
    heads = rate_ref.shape[0]
    ext_ref[:HALO] = jnp.zeros((HALO, channels), F32)
    ext_ref[HALO:] = x_ref[...].astype(F32)
    taps = taps_ref[...].astype(F32)
    count = taps.shape[0]
    total = taps[0:1] * ext_ref[HALO - count + 1 : HALO - count + 1 + length]
    for i in range(1, count):
        first = HALO - count + 1 + i
        total = total + taps[i : i + 1] * ext_ref[first : first + length]
    values = silu(total).astype(BF)
    xc_ref[...] = values
    step, _, cumulative = step_and_logs(dt_ref[...], rate_ref[...])
    cum_ref[...] = cumulative
    step_ref[...] = step
    lane = iota((heads, length), 1)

    def weigh(at, weight):
        wide = expand(weight.T, channels // heads)
        first_ref[at] = wide[:HALO]
        weighted_ref[at] = (xc_ref[...].astype(F32) * wide).astype(BF)

    ends = [cumulative[:, length - 1 :]]
    weigh(0, jnp.exp(ends[0] - cumulative) * step)
    for slot in range(SLOTS):
        position = meta_ref[base + slot]
        end = jnp.sum(jnp.where(lane == position, cumulative, 0.0), axis=1, keepdims=True)
        ends.append(end)

        @pl.when(position >= 0)
        def _():
            weigh(1 + slot, jnp.exp(jnp.where(lane <= position, end - cumulative, FAR)) * step)

    spot = iota(logs_ref.shape, 1)
    logs = jnp.zeros(logs_ref.shape, F32)
    for at, part in enumerate(part for end in ends for part in parts_of(end, 3)):
        logs = jnp.where(spot == at, part.astype(F32), logs)
    logs_ref[...] = logs


def tail_tiles(meta_ref, base, rows, out_ref):
    bounds, height, width = out_ref.shape
    row = iota((bounds * height, 1), 0)
    wanted = jnp.full(row.shape, -1, I32)
    for j in range(bounds):
        wanted = jnp.where(row // height == j, meta_ref[base + j] + row % 4, wanted)
    wanted = jnp.where(row % 4 < 3, wanted, -1)
    picker = (iota((bounds * height, rows.shape[0]), 1) == wanted).astype(BF)
    picked = jnp.dot(picker, rows, preferred_element_type=F32)
    out_ref[...] = picked.reshape(bounds, height, width)


def index_kernel(
    me_ref, bound_ref, owner_ref, parent_ref, len_ref, x_ref,
    meta_ref, tails_ref, last_ref, count_ref, start_ref, size_ref, tile_ref, *, n_ctx, n_state,
):
    me = me_ref[0]
    length = x_ref.shape[0]
    bounds = bound_ref.shape[0]
    branches = owner_ref.shape[0]

    def clear(o, _):
        count_ref[o] = 0
        count_ref[n_ctx + o] = 0
        return 0

    lax.fori_loop(0, n_ctx, clear, 0)

    def place(b, _):
        owner = owner_ref[b]
        rank = count_ref[owner]
        start = count_ref[n_ctx + owner]
        size = len_ref[b]
        count_ref[owner] = rank + 1
        count_ref[n_ctx + owner] = start + size
        at = owner * BR_PER + rank
        meta_ref[at] = parent_ref[b]
        start_ref[at] = start
        size_ref[at] = size
        return 0

    lax.fori_loop(0, branches, place, 0)
    blocks = [lax.div(bound_ref[j], length) for j in range(bounds)]
    at = branches
    for k in range(SLOTS):
        meta_ref[at + 3 * bounds + k] = -1
    for j in range(bounds):
        slot = jnp.int32(0)
        for i in range(j):
            slot = slot + (blocks[i] == blocks[j]).astype(I32)
        meta_ref[at + j] = blocks[j]
        meta_ref[at + bounds + j] = slot
        meta_ref[at + 2 * bounds + j] = bound_ref[j] - me * length - 2

        @pl.when((blocks[j] == me) & (slot < SLOTS))
        def _():
            meta_ref[at + 3 * bounds + slot] = bound_ref[j] - me * length

    for k in range(BR_PER):
        meta_ref[at + 3 * bounds + SLOTS + k] = start_ref[me * BR_PER + k]
        meta_ref[at + 3 * bounds + SLOTS + BR_PER + k] = size_ref[me * BR_PER + k]
    last_ref[...] = x_ref[length - HALO :, :]
    tail_tiles(meta_ref, at + 2 * bounds, x_ref[...], tile_ref)
    upper = iota((8, n_state), 0) < 4
    groups = x_ref.shape[1] // n_state
    for o in range(n_ctx):
        first, second = (meta_ref[o * BR_PER + k] for k in range(BR_PER))
        tiles = []
        for g in range(groups):
            lanes = slice(g * n_state, (g + 1) * n_state)
            tiles.append(jnp.where(upper, tile_ref[first, :, lanes], tile_ref[second, :, lanes]))
        tails_ref[o] = jnp.concatenate(tiles, axis=0).astype(BF)


def convolve(ext_ref, taps_ref, first, height):
    taps = taps_ref[...].astype(F32)
    count = taps.shape[0]
    total = taps[0:1] * ext_ref[first - count + 1 : first - count + 1 + height]
    for i in range(1, count):
        start = first - count + 1 + i
        total = total + taps[i : i + 1] * ext_ref[start : start + height]
    return silu(total).astype(BF)


def over_rows(weighted, b_rows):
    return lax.dot_general(weighted, b_rows, (((0,), (0,)), ((), ())), preferred_element_type=F32)


def prefix_later_kernel(
    meta_ref, bc_ref, taps_ref, weighted_ref, logs_ref, xtails_ref,
    part_ref, misc_ref, conv_ref, ext_ref, tile_ref, *, base, tail_base,
):
    _, length, channels = weighted_ref.shape
    width = taps_ref.shape[1]
    n_state = width // 2
    n_ctx, xrows, _ = xtails_ref.shape
    heads = logs_ref.shape[0]
    bc = bc_ref[:, :width]
    ext_ref[...] = bc.astype(F32)
    convolved = convolve(ext_ref, taps_ref, HALO, length - HALO)
    conv_ref[HALO:] = convolved
    part_ref[0] = over_rows(weighted_ref[0, HALO:, :], convolved[:, :n_state])
    for slot in range(SLOTS):

        @pl.when(meta_ref[base + slot] >= 0)
        def _():
            part_ref[1 + slot] = over_rows(weighted_ref[1 + slot, HALO:, :], convolved[:, :n_state])

    misc_ref[:, :xrows, :] = xtails_ref[...]
    tail_tiles(meta_ref, tail_base, bc, tile_ref)
    row = iota((8, n_state), 0)
    per_head = n_ctx // heads
    for o in range(n_ctx):
        first, second = (meta_ref[o * BR_PER + k] for k in range(BR_PER))
        tails = []
        for g in range(2):
            lanes = slice(g * n_state, (g + 1) * n_state)
            tails.append(jnp.where(row < 4, tile_ref[first, :, lanes], tile_ref[second, :, lanes]))
        h = o // per_head
        tails[0] = jnp.where(row == LOGS, logs_ref[h : h + 1], tails[0])
        misc_ref[o, xrows:, :] = jnp.concatenate(tails, axis=0).astype(BF)


def prefix_state_kernel(
    meta_ref, x_ref, halo_ref, xtaps_ref, bc_ref, taps_ref, first_ref, part_ref, misc_ref, conv_ref,
    sent_ref, b_ref, c_ref, xfirst_ref, ext_ref, edge_ref, *, base,
):
    channels = x_ref.shape[1]
    width = taps_ref.shape[1]
    n_state = width // 2
    n_ctx, misc, _ = misc_ref.shape
    rows = channels // n_ctx
    ext_ref[:HALO] = halo_ref[:, channels:].astype(F32)
    ext_ref[HALO:] = bc_ref[:HALO, :width].astype(F32)
    convolved = convolve(ext_ref, taps_ref, HALO, HALO)
    b_rows = convolved[:, :n_state]
    b_ref[:HALO] = b_rows
    b_ref[HALO:] = conv_ref[HALO:, :n_state]
    c_ref[:HALO] = convolved[:, n_state:]
    c_ref[HALO:] = conv_ref[HALO:, n_state:]
    edge_ref[:HALO] = halo_ref[:, :channels].astype(F32)
    edge_ref[HALO:] = x_ref[:HALO].astype(F32)
    xfirst = convolve(edge_ref, xtaps_ref, HALO, HALO)
    xfirst_ref[...] = xfirst

    def send(at):
        weighted = (xfirst.astype(F32) * first_ref[at]).astype(BF)
        state = part_ref[at] + over_rows(weighted, b_rows)
        start = misc + at * rows
        sent_ref[:, start : start + rows, :] = state.astype(BF).reshape(n_ctx, rows, n_state)

    sent_ref[:, :misc, :] = misc_ref[...]
    send(0)
    for slot in range(SLOTS):
        position = meta_ref[base + slot]
        start = misc + (1 + slot) * rows

        @pl.when(position >= 0)
        def _():
            send(1 + slot)

        @pl.when(position < 0)
        def _():
            sent_ref[:, start : start + rows, :] = jnp.zeros((n_ctx, rows, n_state), BF)


def prefix_mix_kernel(xc_ref, xfirst_ref, b_ref, c_ref, cum_ref, step_ref, skip_ref, z_ref, y_ref, scale_ref):
    length, channels = xc_ref.shape
    scores = lax.dot_general(
        c_ref[...], b_ref[...], (((1,), (1,)), ((), ())), preferred_element_type=F32
    )
    mask = iota((length, length), 1) <= iota((length, length), 0)
    values = jnp.concatenate([xfirst_ref[...], xc_ref[HALO:]], axis=0)
    cumulative = cum_ref[...]
    gate = silu(z_ref[...].astype(F32))
    scale_ref[...] = expand(jnp.exp(cumulative).T, channels // cumulative.shape[0]) * gate
    extra = values.astype(F32) * skip_ref[...]
    mixed_rows(values, scores, step_ref[...], cumulative, mask, y_ref, extra, gate)


def scan_kernel(meta_ref, got_ref, *rest, n_branch, bounds):
    extra_ref = rest[0] if len(rest) == 5 else None
    back_ref, entering_ref, bound_ref, log_ref = rest[-4:]
    n_ctx, sent_rows, n_state = got_ref.shape
    rows = entering_ref.shape[1]
    misc = sent_rows - (1 + SLOTS) * rows
    parts = got_ref[:, misc - 16 : misc, :].astype(F32)[:, LOGS, :]
    for v in range(1 + SLOTS):
        log = parts[:, 3 * v : 3 * v + 1] + parts[:, 3 * v + 1 : 3 * v + 2] + parts[:, 3 * v + 2 : 3 * v + 3]
        log_ref[v] = jnp.broadcast_to(log, (n_ctx, n_state))
    state = jnp.zeros((rows, n_state), F32)
    for i in range(n_ctx):
        entering_ref[i] = state
        back_ref[i, :rows, :] = state.astype(BF)
        if i < n_ctx - 1:
            local = got_ref[i, misc : misc + rows, :].astype(F32)
            state = jnp.exp(log_ref[0, i : i + 1]) * state + local
    for j in range(bounds):
        block = meta_ref[n_branch + j]
        slot = meta_ref[n_branch + bounds + j]
        log = log_ref[1, pl.ds(block, 1)]
        part = got_ref[block, misc + rows : misc + 2 * rows, :].astype(F32)
        for other in range(1, SLOTS):
            first = misc + (1 + other) * rows
            log = jnp.where(slot == other, log_ref[1 + other, pl.ds(block, 1)], log)
            part = jnp.where(slot == other, got_ref[block, first : first + rows, :].astype(F32), part)
        if extra_ref is not None:
            tail = extra_ref[block, (bounds - SLOTS) * rows :, :].astype(F32)
            for more in range(bounds - SLOTS):
                here = slot == SLOTS + more
                three = tail[3 * more : 3 * more + 1] + tail[3 * more + 1 : 3 * more + 2] + tail[3 * more + 2 : 3 * more + 3]
                log = jnp.where(here, three, log)
                part = jnp.where(here, extra_ref[block, more * rows : (more + 1) * rows, :].astype(F32), part)
        bound_ref[j] = jnp.exp(log) * entering_ref[block] + part
    for o in range(n_ctx):
        for k in range(BR_PER):
            first = (1 + k) * rows
            back_ref[o, first : first + rows, :] = bound_ref[meta_ref[o * BR_PER + k]].astype(BF)


def segments(meta_ref, base, shape, axis):
    row = iota(shape, axis)
    segment = jnp.full(shape, BR_PER, I32)
    offset = row
    for k in range(BR_PER):
        start, size = meta_ref[base + k], meta_ref[base + BR_PER + k]
        inside = (row >= start) & (row < start + size)
        segment = jnp.where(inside, k, segment)
        offset = jnp.where(inside, row - start, offset)
    return segment, offset


def branch_kernel(
    meta_ref, x_ref, bc_ref, got_ref, dt_ref, rate_ref, xtaps_ref, taps_ref, skip_ref, z_ref,
    y_ref, c_ref, scale_ref, ext_ref, *, base,
):
    length, channels = x_ref.shape
    n_ctx, _, n_state = got_ref.shape
    width = taps_ref.shape[1]
    ext_ref[:HALO] = jnp.zeros((HALO, channels + width), F32)
    ext_ref[HALO:, :channels] = x_ref[...].astype(F32)
    ext_ref[HALO:, channels:] = bc_ref[:, width:].astype(F32)
    groups = (channels + width) // n_state
    misc = got_ref[0, : 8 * groups, :].astype(F32)
    for i in range(1, n_ctx):
        misc = misc + got_ref[i, : 8 * groups, :].astype(F32)
    tails = jnp.concatenate([misc[8 * g : 8 * (g + 1)] for g in range(groups)], axis=1)
    unused = iota(tails.shape, 0) % 4 == LOGS
    tails = jnp.where(unused, 0.0, tails)
    tails = jnp.concatenate([tails, jnp.zeros_like(tails)], axis=0).astype(BF)
    taps = jnp.concatenate([xtaps_ref[...].astype(F32), taps_ref[...].astype(F32)], axis=1)
    count = taps.shape[0]
    tail = count - 1
    segment, offset = segments(meta_ref, base, (length, 1), 0)
    place = iota((length, 16), 1)
    total = None
    for i in range(count):
        shift = tail - i
        rows = ext_ref[HALO - shift : HALO - shift + length]
        if shift:
            ahead = (offset < shift) & (segment < BR_PER)
            picker = ahead & (place == segment * 4 + tail - shift + offset)
            early = jnp.dot(picker.astype(BF), tails, preferred_element_type=F32)
            rows = jnp.where(offset >= shift, rows, 0.0) + early
        term = taps[i : i + 1] * rows
        total = term if total is None else total + term
    convolved = silu(total).astype(BF)
    values = convolved[:, :channels]
    b_rows = convolved[:, channels : channels + n_state]
    c_rows = convolved[:, channels + n_state :]
    c_ref[...] = c_rows
    step, log_decay, cumulative = step_and_logs(dt_ref[...], rate_ref[...])
    across, _ = segments(meta_ref, base, (1, length), 1)
    lane = iota(cumulative.shape, 1)
    before = cumulative - log_decay
    seed = jnp.zeros_like(cumulative)
    for k in range(BR_PER):
        first = jnp.sum(jnp.where(lane == meta_ref[base + k], before, 0.0), axis=1, keepdims=True)
        seed = jnp.where(across == k, jnp.exp(jnp.where(across == k, cumulative - first, 0.0)), seed)
    gate = silu(z_ref[...].astype(F32))
    scale_ref[...] = expand(seed.T, channels // seed.shape[0]) * gate
    scores = lax.dot_general(c_rows, b_rows, (((1,), (1,)), ((), ())), preferred_element_type=F32)
    mask = (segment == across) & (segment < BR_PER)
    mask = mask & (iota((length, length), 1) <= iota((length, length), 0))
    extra = values.astype(F32) * skip_ref[...]
    mixed_rows(values, scores, step, cumulative, mask, y_ref, extra, gate)


def gate_kernel(
    meta_ref, y_ref, scale_ref, c_ref, by_ref, bscale_ref, bc_ref, back_ref,
    g_ref, bg_ref, sq_ref, *, base,
):
    length, channels = y_ref.shape
    n_ctx, _, n_state = back_ref.shape
    rows = channels // n_ctx

    def from_state(c_rows, which):
        state = back_ref[:, which * rows : (which + 1) * rows, :].reshape(channels, n_state)
        return lax.dot_general(c_rows, state, (((1,), (1,)), ((), ())), preferred_element_type=F32)

    def squares(gated):
        square = gated * gated
        total = square[:, :n_state]
        for at in range(n_state, channels, n_state):
            total = total + square[:, at : at + n_state]
        ones = jnp.ones((8, n_state), F32)
        return lax.dot_general(
            ones, total, (((1,), (1,)), ((), ())), precision=HIGH, preferred_element_type=F32
        )

    gated = y_ref[...] + scale_ref[...] * from_state(c_ref[...], 0)
    g_ref[...] = gated
    sums = squares(gated)
    segment, _ = segments(meta_ref, base, (length, 1), 0)
    c_rows = bc_ref[...]
    seeded = from_state(c_rows, BR_PER)
    for k in range(BR_PER - 1):
        seeded = jnp.where(segment == k, from_state(c_rows, 1 + k), seeded)
    gated = by_ref[...] + bscale_ref[...] * seeded
    bg_ref[...] = gated
    more = squares(gated)
    half = length // 2
    row = iota((8, half), 0)
    packed = jnp.where(
        row == 0,
        sums[:, :half],
        jnp.where(row == 1, sums[:, half:], jnp.where(row == 2, more[:, :half], more[:, half:])),
    )
    for i in range(sq_ref.shape[0]):
        sq_ref[i] = packed


def norm_kernel(meta_ref, sq_ref, g_ref, bg_ref, gain_ref, out_ref, bout_ref, *, base):
    length, channels = g_ref.shape
    n_tp = sq_ref.shape[0]
    total = sq_ref[0]
    for i in range(1, n_tp):
        total = total + sq_ref[i]
    factor = lax.rsqrt(total / (channels * n_tp) + EPSILON).T
    gain = gain_ref[...]
    half = length // 2
    segment, _ = segments(meta_ref, base, (length, 1), 0)
    for k in range(2):
        rows = slice(k * half, (k + 1) * half)
        out_ref[rows] = (g_ref[rows] * factor[:, k : k + 1] * gain).astype(BF)
        scaled = bg_ref[rows] * factor[:, 2 + k : 3 + k] * gain
        bout_ref[rows] = jnp.where(segment[rows] < BR_PER, scaled, 0.0).astype(BF)


def call(kernel, outs, scratch, args, smem=0, smem_out=False, grid=False):
    def where(scalar, shape):
        if grid and not scalar:
            return pl.BlockSpec(shape, lambda _, n=len(shape): (0,) * n)
        return pl.BlockSpec(memory_space=pltpu.SMEM if scalar else pltpu.VMEM)

    return pl.pallas_call(
        kernel,
        grid=(1,) if grid else (),
        in_specs=[where(i < smem, a.shape) for i, a in enumerate(args)],
        out_specs=[where(smem_out and i == 0, s) for i, (s, _) in enumerate(outs)],
        out_shape=[jax.ShapeDtypeStruct(s, t) for s, t in outs],
        scratch_shapes=[(pltpu.SMEM if len(s) == 1 else pltpu.VMEM)(s, t) for s, t in scratch],
        compiler_params=pltpu.CompilerParams(vmem_limit_bytes=24 * 2**20),
        cost_estimate=pl.CostEstimate(flops=2 * 10**9, bytes_accessed=4 * 10**6, transcendentals=10**6),
    )(*args)


def more_states(xc, b_rows, step, cumulative, positions, n_ctx):
    length, channels = xc.shape
    heads = step.shape[0]
    n_state = b_rows.shape[1]
    row = jnp.arange(length, dtype=I32)
    hit = row[None, None, :] == positions[:, None, None]
    ends = jnp.sum(jnp.where(hit, cumulative[None], 0.0), axis=2)
    inside = (row[None, :] <= positions[:, None])[:, None, :]
    weight = jnp.exp(jnp.where(inside, ends[:, :, None] - cumulative[None], FAR)) * step[None]
    values = xc.reshape(length, heads, -1).astype(F32)
    weighted = (jnp.transpose(weight, (0, 2, 1))[:, :, :, None] * values[None]).astype(BF)
    states = jnp.einsum("jshp,sn->jhpn", weighted, b_rows, preferred_element_type=F32).astype(BF)
    rows = channels // n_ctx
    count = positions.shape[0]
    states = jnp.transpose(states.reshape(count, n_ctx, rows, n_state), (1, 0, 2, 3))
    parts = []
    rest = ends
    for _ in range(3):
        part = lax.reduce_precision(rest, 8, 7)
        parts.append(part)
        rest = rest - part
    logs = jnp.stack(parts, axis=1).reshape(3 * count, heads).T
    logs = jnp.repeat(logs, n_ctx // heads, axis=0)
    logs = jnp.broadcast_to(logs[:, :, None], (n_ctx, 3 * count, n_state)).astype(BF)
    sent = jnp.concatenate([states.reshape(n_ctx, count * rows, n_state), logs], axis=1)
    return jnp.pad(sent, ((0, 0), (0, -sent.shape[1] % 16), (0, 0)))


def body(
    prefix_x, prefix_z, prefix_bc, prefix_dt, branch_x, branch_z, branch_bc, branch_dt,
    conv_x, conv_bc, decay_rate, skip, norm_gain, bound_pos, branch_owner, branch_parent, branch_len,
):
    n_ctx = lax.axis_size("ctx")
    n_tp = lax.axis_size("tp")
    me = lax.axis_index("ctx")
    length, channels = prefix_x.shape
    heads = decay_rate.shape[0]
    width = prefix_bc.shape[1]
    n_state = width // 2
    rows = channels // n_ctx
    bounds = bound_pos.shape[0]
    branches = branch_owner.shape[0]
    tail = conv_x.shape[0] - 1
    onward = [(i, i + 1) for i in range(n_ctx - 1)]

    own = jnp.concatenate([prefix_bc, branch_bc], axis=1)
    spread = jnp.broadcast_to(own[None], (n_tp, *own.shape))
    gathered = lax.all_to_all(spread, "tp", 0, 0, tiled=True).reshape(length, 2 * width)
    rates = decay_rate[:, None]
    skips = jnp.repeat(skip, channels // heads)[None]
    gain = norm_gain[None]
    order = jnp.arange(bounds, dtype=I32)
    block_of = bound_pos // length
    slot_of = jnp.sum(
        ((block_of[:, None] == block_of[None, :]) & (order[None, :] < order[:, None])).astype(I32), axis=1
    )

    at_tails = branches + 2 * bounds
    at_positions = at_tails + bounds
    at_mine = at_positions + SLOTS
    xrows = 8 * channels // n_state
    meta, xtails, last = call(
        functools.partial(index_kernel, n_ctx=n_ctx, n_state=n_state),
        [((at_mine + 2 * BR_PER,), I32), ((n_ctx, xrows, n_state), BF), ((HALO, channels), BF)],
        [((2 * n_ctx,), I32), ((branches,), I32), ((branches,), I32), ((bounds, 8, channels), F32)],
        [jnp.full((1,), me, I32), bound_pos, branch_owner, branch_parent, branch_len, prefix_x],
        smem=5,
        smem_out=True,
    )
    xc, cumulative, step, weighted, first, logs = call(
        functools.partial(prefix_x_kernel, base=at_positions),
        [
            ((length, channels), BF),
            ((heads, length), F32),
            ((heads, length), F32),
            ((1 + SLOTS, length, channels), BF),
            ((1 + SLOTS, HALO, channels), F32),
            ((heads, n_state), F32),
        ],
        [((HALO + length, channels), F32)],
        [meta, prefix_x, prefix_dt, rates, conv_x],
        smem=1,
    )
    gathered, weighted, last = lax.optimization_barrier((gathered, weighted, last))
    halo = lax.ppermute(
        jnp.concatenate([last, gathered[length - HALO :, :width]], axis=1), "ctx", onward
    )
    part, misc, convolved = call(
        functools.partial(prefix_later_kernel, base=at_positions, tail_base=at_tails),
        [
            ((1 + SLOTS, channels, n_state), F32),
            ((n_ctx, xrows + 16, n_state), BF),
            ((length, width), BF),
        ],
        [((length, width), F32), ((bounds, 8, width), F32)],
        [meta, gathered, conv_bc, weighted, logs, xtails],
        smem=1,
    )
    sent, b_rows, c_rows, xfirst = call(
        functools.partial(prefix_state_kernel, base=at_positions),
        [
            ((n_ctx, xrows + 16 + (1 + SLOTS) * rows, n_state), BF),
            ((length, n_state), BF),
            ((length, n_state), BF),
            ((HALO, channels), BF),
        ],
        [((2 * HALO, width), F32), ((2 * HALO, channels), F32)],
        [meta, prefix_x, halo, conv_x, gathered, conv_bc, first, part, misc, convolved],
        smem=1,
    )
    got = lax.all_to_all(sent, "ctx", 0, 0, tiled=True)
    y, scale = call(
        prefix_mix_kernel,
        [((length, channels), F32), ((length, channels), F32)],
        [],
        [xc, xfirst, b_rows, c_rows, cumulative, step, skips, prefix_z],
    )

    scan = functools.partial(scan_kernel, n_branch=branches, bounds=bounds)
    scan_out = [((n_ctx, (1 + BR_PER) * rows, n_state), BF)]
    scan_scratch = [
        ((n_ctx, rows, n_state), F32),
        ((bounds, rows, n_state), F32),
        ((1 + SLOTS, n_ctx, n_state), F32),
    ]

    def usual():
        return call(scan, scan_out, scan_scratch, [meta, got], smem=1, grid=True)[0]

    def crowded():
        here = (block_of == me)[None, :] & (slot_of[None, :] == order[SLOTS:, None])
        positions = jnp.sum(jnp.where(here, (bound_pos - block_of * length + 1)[None, :], 0), axis=1) - 1
        whole = jnp.concatenate([xfirst, xc[HALO:]], axis=0)
        extra = more_states(whole, b_rows, step, cumulative, positions, n_ctx)
        extra = lax.all_to_all(extra, "ctx", 0, 0, tiled=True)
        return call(scan, scan_out, scan_scratch, [meta, got, extra], smem=1)[0]

    back = lax.cond(jnp.max(slot_of) >= SLOTS, crowded, usual)
    back = lax.all_to_all(back, "ctx", 0, 0, tiled=True)

    branch_y, branch_c, branch_scale = call(
        functools.partial(branch_kernel, base=at_mine),
        [((length, channels), F32), ((length, n_state), BF), ((length, channels), F32)],
        [((HALO + length, channels + width), F32)],
        [meta, branch_x, gathered, got, branch_dt, rates, conv_x, conv_bc, skips, branch_z],
        smem=1,
    )
    gated, branch_gated, squares = call(
        functools.partial(gate_kernel, base=at_mine),
        [((length, channels), F32), ((length, channels), F32), ((n_tp, 8, length // 2), F32)],
        [],
        [meta, y, scale, c_rows, branch_y, branch_scale, branch_c, back],
        smem=1,
    )
    squares = lax.all_to_all(squares, "tp", 0, 0, tiled=True)
    return tuple(
        call(
            functools.partial(norm_kernel, base=at_mine),
            [((length, channels), BF), ((length, channels), BF)],
            [],
            [meta, squares, gated, branch_gated, gain],
            smem=1,
            grid=True,
        )
    )


def solution(mesh):
    both = P(("ctx", "tp"), None)
    in_specs = (
        P("ctx", "tp"), P("ctx", "tp"), both, P("tp", "ctx"),
        P("ctx", "tp"), P("ctx", "tp"), both, P("tp", "ctx"),
        P(None, "tp"), P(), P("tp"), P("tp"), P("tp"), P(), P(), P(), P(),
    )
    out_specs = (P("ctx", "tp"), P("ctx", "tp"))
    return jax.shard_map(body, mesh=mesh, in_specs=in_specs, out_specs=out_specs, check_vma=False)
```

```python
import functools

import jax
import jax.numpy as jnp
from jax import lax
from jax.experimental import pallas as pl
from jax.experimental.pallas import tpu as pltpu
from jax.sharding import PartitionSpec as P

BR_PER = 2
EPSILON = 1e-05
SLOTS = 2
LOGS = 3
HALO = 16
BF = jnp.bfloat16
F32 = jnp.float32
I32 = jnp.int32
HIGH = lax.Precision.HIGHEST
FAR = -1e30


def iota(shape, axis):
    return lax.broadcasted_iota(I32, shape, axis)


def parts_of(value, count):
    found = []
    for _ in range(count):
        part = value.astype(BF)
        found.append(part)
        value = value - part.astype(F32)
    return found


def expand(columns, head_size):
    rows, heads = columns.shape
    low = iota((rows, 2 * head_size), 1) < head_size
    pairs = [
        jnp.where(low, columns[:, h : h + 1], columns[:, h + 1 : h + 2]) for h in range(0, heads, 2)
    ]
    return jnp.concatenate(pairs, axis=1)


def step_and_logs(raw, rates):
    step = jnp.maximum(raw, 0.0) + jnp.log1p(jnp.exp(-jnp.abs(raw)))
    log_decay = -rates * step
    length = raw.shape[1]
    upper = (iota((length, length), 0) <= iota((length, length), 1)).astype(F32)
    cumulative = jnp.dot(log_decay, upper, precision=HIGH, preferred_element_type=F32)
    return step, log_decay, cumulative


def silu(value):
    return value * jax.nn.sigmoid(value)


def mixed_rows(values, scores, step, cumulative, mask, out_ref, extra, gate):
    length, channels = values.shape
    heads = step.shape[0]
    size = channels // heads
    columns = cumulative.T
    half = length // 2
    low = iota((half, 2 * size), 1) < size
    for first, width in ((0, half), (half, length)):
        rows = slice(first, first + half)
        kept = mask[rows, :width]
        score = scores[rows, :width]
        for h in range(0, heads, 2):
            lanes = slice(h * size, (h + 2) * size)
            sums = []
            for one in (h, h + 1):
                gap = columns[rows, one : one + 1] - cumulative[one : one + 1, :width]
                mixing = score * jnp.exp(jnp.where(kept, gap, FAR)) * step[one : one + 1, :width]
                sums.append(jnp.dot(mixing.astype(BF), values[:width, lanes], preferred_element_type=F32))
            out_ref[rows, lanes] = (jnp.where(low, sums[0], sums[1]) + extra[rows, lanes]) * gate[rows, lanes]


def prefix_x_kernel(
    meta_ref, x_ref, dt_ref, rate_ref, taps_ref,
    xc_ref, cum_ref, step_ref, weighted_ref, first_ref, logs_ref, ext_ref, *, base,
):
    length, channels = x_ref.shape
    heads = rate_ref.shape[0]
    ext_ref[:HALO] = jnp.zeros((HALO, channels), F32)
    ext_ref[HALO:] = x_ref[...].astype(F32)
    taps = taps_ref[...].astype(F32)
    count = taps.shape[0]
    total = taps[0:1] * ext_ref[HALO - count + 1 : HALO - count + 1 + length]
    for i in range(1, count):
        first = HALO - count + 1 + i
        total = total + taps[i : i + 1] * ext_ref[first : first + length]
    values = silu(total).astype(BF)
    xc_ref[...] = values
    step, _, cumulative = step_and_logs(dt_ref[...], rate_ref[...])
    cum_ref[...] = cumulative
    step_ref[...] = step
    lane = iota((heads, length), 1)

    def weigh(at, weight):
        wide = expand(weight.T, channels // heads)
        first_ref[at] = wide[:HALO]
        weighted_ref[at] = (xc_ref[...].astype(F32) * wide).astype(BF)

    ends = [cumulative[:, length - 1 :]]
    weigh(0, jnp.exp(ends[0] - cumulative) * step)
    for slot in range(SLOTS):
        position = meta_ref[base + slot]
        end = jnp.sum(jnp.where(lane == position, cumulative, 0.0), axis=1, keepdims=True)
        ends.append(end)

        @pl.when(position >= 0)
        def _():
            weigh(1 + slot, jnp.exp(jnp.where(lane <= position, end - cumulative, FAR)) * step)

    spot = iota(logs_ref.shape, 1)
    logs = jnp.zeros(logs_ref.shape, F32)
    for at, part in enumerate(part for end in ends for part in parts_of(end, 3)):
        logs = jnp.where(spot == at, part.astype(F32), logs)
    logs_ref[...] = logs


def tail_tiles(meta_ref, base, rows, out_ref):
    bounds, height, width = out_ref.shape
    row = iota((bounds * height, 1), 0)
    wanted = jnp.full(row.shape, -1, I32)
    for j in range(bounds):
        wanted = jnp.where(row // height == j, meta_ref[base + j] + row % 4, wanted)
    wanted = jnp.where(row % 4 < 3, wanted, -1)
    picker = (iota((bounds * height, rows.shape[0]), 1) == wanted).astype(BF)
    picked = jnp.dot(picker, rows, preferred_element_type=F32)
    out_ref[...] = picked.reshape(bounds, height, width)


def index_kernel(
    me_ref, bound_ref, owner_ref, parent_ref, len_ref, x_ref,
    meta_ref, tails_ref, last_ref, count_ref, start_ref, size_ref, tile_ref, *, n_ctx, n_state,
):
    me = me_ref[0]
    length = x_ref.shape[0]
    bounds = bound_ref.shape[0]
    branches = owner_ref.shape[0]

    def clear(o, _):
        count_ref[o] = 0
        count_ref[n_ctx + o] = 0
        return 0

    lax.fori_loop(0, n_ctx, clear, 0)

    def place(b, _):
        owner = owner_ref[b]
        rank = count_ref[owner]
        start = count_ref[n_ctx + owner]
        size = len_ref[b]
        count_ref[owner] = rank + 1
        count_ref[n_ctx + owner] = start + size
        at = owner * BR_PER + rank
        meta_ref[at] = parent_ref[b]
        start_ref[at] = start
        size_ref[at] = size
        return 0

    lax.fori_loop(0, branches, place, 0)
    blocks = [lax.div(bound_ref[j], length) for j in range(bounds)]
    at = branches
    for k in range(SLOTS):
        meta_ref[at + 3 * bounds + k] = -1
    for j in range(bounds):
        slot = jnp.int32(0)
        for i in range(j):
            slot = slot + (blocks[i] == blocks[j]).astype(I32)
        meta_ref[at + j] = blocks[j]
        meta_ref[at + bounds + j] = slot
        meta_ref[at + 2 * bounds + j] = bound_ref[j] - me * length - 2

        @pl.when((blocks[j] == me) & (slot < SLOTS))
        def _():
            meta_ref[at + 3 * bounds + slot] = bound_ref[j] - me * length

    for k in range(BR_PER):
        meta_ref[at + 3 * bounds + SLOTS + k] = start_ref[me * BR_PER + k]
        meta_ref[at + 3 * bounds + SLOTS + BR_PER + k] = size_ref[me * BR_PER + k]
    last_ref[...] = x_ref[length - HALO :, :]
    tail_tiles(meta_ref, at + 2 * bounds, x_ref[...], tile_ref)
    upper = iota((8, n_state), 0) < 4
    groups = x_ref.shape[1] // n_state
    for o in range(n_ctx):
        first, second = (meta_ref[o * BR_PER + k] for k in range(BR_PER))
        tiles = []
        for g in range(groups):
            lanes = slice(g * n_state, (g + 1) * n_state)
            tiles.append(jnp.where(upper, tile_ref[first, :, lanes], tile_ref[second, :, lanes]))
        tails_ref[o] = jnp.concatenate(tiles, axis=0).astype(BF)


def convolve(ext_ref, taps_ref, first, height):
    taps = taps_ref[...].astype(F32)
    count = taps.shape[0]
    total = taps[0:1] * ext_ref[first - count + 1 : first - count + 1 + height]
    for i in range(1, count):
        start = first - count + 1 + i
        total = total + taps[i : i + 1] * ext_ref[start : start + height]
    return silu(total).astype(BF)


def over_rows(weighted, b_rows):
    return lax.dot_general(weighted, b_rows, (((0,), (0,)), ((), ())), preferred_element_type=F32)


def prefix_later_kernel(
    meta_ref, bc_ref, taps_ref, weighted_ref, logs_ref, xtails_ref,
    part_ref, misc_ref, conv_ref, ext_ref, tile_ref, *, base, tail_base,
):
    _, length, channels = weighted_ref.shape
    width = taps_ref.shape[1]
    n_state = width // 2
    n_ctx, xrows, _ = xtails_ref.shape
    heads = logs_ref.shape[0]
    bc = bc_ref[:, :width]
    ext_ref[...] = bc.astype(F32)
    convolved = convolve(ext_ref, taps_ref, HALO, length - HALO)
    conv_ref[HALO:] = convolved
    part_ref[0] = over_rows(weighted_ref[0, HALO:, :], convolved[:, :n_state])
    for slot in range(SLOTS):

        @pl.when(meta_ref[base + slot] >= 0)
        def _():
            part_ref[1 + slot] = over_rows(weighted_ref[1 + slot, HALO:, :], convolved[:, :n_state])

    misc_ref[:, :xrows, :] = xtails_ref[...]
    tail_tiles(meta_ref, tail_base, bc, tile_ref)
    row = iota((8, n_state), 0)
    per_head = n_ctx // heads
    for o in range(n_ctx):
        first, second = (meta_ref[o * BR_PER + k] for k in range(BR_PER))
        tails = []
        for g in range(2):
            lanes = slice(g * n_state, (g + 1) * n_state)
            tails.append(jnp.where(row < 4, tile_ref[first, :, lanes], tile_ref[second, :, lanes]))
        h = o // per_head
        tails[0] = jnp.where(row == LOGS, logs_ref[h : h + 1], tails[0])
        misc_ref[o, xrows:, :] = jnp.concatenate(tails, axis=0).astype(BF)


def prefix_state_kernel(
    meta_ref, x_ref, halo_ref, xtaps_ref, bc_ref, taps_ref, first_ref, part_ref, misc_ref, conv_ref,
    sent_ref, b_ref, c_ref, xfirst_ref, ext_ref, edge_ref, *, base,
):
    channels = x_ref.shape[1]
    width = taps_ref.shape[1]
    n_state = width // 2
    n_ctx, misc, _ = misc_ref.shape
    rows = channels // n_ctx
    ext_ref[:HALO] = halo_ref[:, channels:].astype(F32)
    ext_ref[HALO:] = bc_ref[:HALO, :width].astype(F32)
    convolved = convolve(ext_ref, taps_ref, HALO, HALO)
    b_rows = convolved[:, :n_state]
    b_ref[:HALO] = b_rows
    b_ref[HALO:] = conv_ref[HALO:, :n_state]
    c_ref[:HALO] = convolved[:, n_state:]
    c_ref[HALO:] = conv_ref[HALO:, n_state:]
    edge_ref[:HALO] = halo_ref[:, :channels].astype(F32)
    edge_ref[HALO:] = x_ref[:HALO].astype(F32)
    xfirst = convolve(edge_ref, xtaps_ref, HALO, HALO)
    xfirst_ref[...] = xfirst

    def send(at):
        weighted = (xfirst.astype(F32) * first_ref[at]).astype(BF)
        state = part_ref[at] + over_rows(weighted, b_rows)
        start = misc + at * rows
        sent_ref[:, start : start + rows, :] = state.astype(BF).reshape(n_ctx, rows, n_state)

    sent_ref[:, :misc, :] = misc_ref[...]
    send(0)
    for slot in range(SLOTS):
        position = meta_ref[base + slot]
        start = misc + (1 + slot) * rows

        @pl.when(position >= 0)
        def _():
            send(1 + slot)

        @pl.when(position < 0)
        def _():
            sent_ref[:, start : start + rows, :] = jnp.zeros((n_ctx, rows, n_state), BF)


def prefix_mix_kernel(xc_ref, xfirst_ref, b_ref, c_ref, cum_ref, step_ref, skip_ref, z_ref, y_ref, scale_ref):
    length, channels = xc_ref.shape
    scores = lax.dot_general(
        c_ref[...], b_ref[...], (((1,), (1,)), ((), ())), preferred_element_type=F32
    )
    mask = iota((length, length), 1) <= iota((length, length), 0)
    values = jnp.concatenate([xfirst_ref[...], xc_ref[HALO:]], axis=0)
    cumulative = cum_ref[...]
    gate = silu(z_ref[...].astype(F32))
    scale_ref[...] = expand(jnp.exp(cumulative).T, channels // cumulative.shape[0]) * gate
    extra = values.astype(F32) * skip_ref[...]
    mixed_rows(values, scores, step_ref[...], cumulative, mask, y_ref, extra, gate)


def scan_kernel(meta_ref, got_ref, *rest, n_branch, bounds):
    extra_ref = rest[0] if len(rest) == 5 else None
    back_ref, entering_ref, bound_ref, decay_ref = rest[-4:]
    n_ctx, sent_rows, n_state = got_ref.shape
    rows = entering_ref.shape[1]
    misc = sent_rows - (1 + SLOTS) * rows
    parts = got_ref[:, misc - 16 : misc, :].astype(F32)[:, LOGS, :]
    for v in range(1 + SLOTS):
        log = parts[:, 3 * v : 3 * v + 1] + parts[:, 3 * v + 1 : 3 * v + 2] + parts[:, 3 * v + 2 : 3 * v + 3]
        decay_ref[v] = jnp.broadcast_to(jnp.exp(log), (n_ctx, n_state))
    state = jnp.zeros((rows, n_state), F32)
    for i in range(n_ctx):
        entering_ref[i] = state
        back_ref[i, :rows, :] = state.astype(BF)
        if i < n_ctx - 1:
            local = got_ref[i, misc : misc + rows, :].astype(F32)
            state = decay_ref[0, i : i + 1] * state + local
    for j in range(bounds):
        block = meta_ref[n_branch + j]
        slot = meta_ref[n_branch + bounds + j]
        log = decay_ref[1, pl.ds(block, 1)]
        part = got_ref[block, misc + rows : misc + 2 * rows, :].astype(F32)
        for other in range(1, SLOTS):
            first = misc + (1 + other) * rows
            log = jnp.where(slot == other, decay_ref[1 + other, pl.ds(block, 1)], log)
            part = jnp.where(slot == other, got_ref[block, first : first + rows, :].astype(F32), part)
        if extra_ref is not None:
            tail = extra_ref[block, (bounds - SLOTS) * rows :, :].astype(F32)
            for more in range(bounds - SLOTS):
                here = slot == SLOTS + more
                three = tail[3 * more : 3 * more + 1] + tail[3 * more + 1 : 3 * more + 2] + tail[3 * more + 2 : 3 * more + 3]
                log = jnp.where(here, jnp.exp(three), log)
                part = jnp.where(here, extra_ref[block, more * rows : (more + 1) * rows, :].astype(F32), part)
        bound_ref[j] = log * entering_ref[block] + part
    for o in range(n_ctx):
        for k in range(BR_PER):
            first = (1 + k) * rows
            back_ref[o, first : first + rows, :] = bound_ref[meta_ref[o * BR_PER + k]].astype(BF)


def segments(meta_ref, base, shape, axis):
    row = iota(shape, axis)
    segment = jnp.full(shape, BR_PER, I32)
    offset = row
    for k in range(BR_PER):
        start, size = meta_ref[base + k], meta_ref[base + BR_PER + k]
        inside = (row >= start) & (row < start + size)
        segment = jnp.where(inside, k, segment)
        offset = jnp.where(inside, row - start, offset)
    return segment, offset


def branch_kernel(
    meta_ref, x_ref, bc_ref, got_ref, dt_ref, rate_ref, xtaps_ref, taps_ref, skip_ref, z_ref,
    y_ref, c_ref, scale_ref, ext_ref, *, base,
):
    length, channels = x_ref.shape
    n_ctx, _, n_state = got_ref.shape
    width = taps_ref.shape[1]
    ext_ref[:HALO] = jnp.zeros((HALO, channels + width), F32)
    ext_ref[HALO:, :channels] = x_ref[...].astype(F32)
    ext_ref[HALO:, channels:] = bc_ref[:, width:].astype(F32)
    groups = (channels + width) // n_state
    misc = got_ref[0, : 8 * groups, :].astype(F32)
    for i in range(1, n_ctx):
        misc = misc + got_ref[i, : 8 * groups, :].astype(F32)
    tails = jnp.concatenate([misc[8 * g : 8 * (g + 1)] for g in range(groups)], axis=1)
    unused = iota(tails.shape, 0) % 4 == LOGS
    tails = jnp.where(unused, 0.0, tails)
    tails = jnp.concatenate([tails, jnp.zeros_like(tails)], axis=0).astype(BF)
    taps = jnp.concatenate([xtaps_ref[...].astype(F32), taps_ref[...].astype(F32)], axis=1)
    count = taps.shape[0]
    tail = count - 1
    segment, offset = segments(meta_ref, base, (length, 1), 0)
    place = iota((length, 16), 1)
    total = None
    for i in range(count):
        shift = tail - i
        rows = ext_ref[HALO - shift : HALO - shift + length]
        if shift:
            ahead = (offset < shift) & (segment < BR_PER)
            picker = ahead & (place == segment * 4 + tail - shift + offset)
            early = jnp.dot(picker.astype(BF), tails, preferred_element_type=F32)
            rows = jnp.where(offset >= shift, rows, 0.0) + early
        term = taps[i : i + 1] * rows
        total = term if total is None else total + term
    convolved = silu(total).astype(BF)
    values = convolved[:, :channels]
    b_rows = convolved[:, channels : channels + n_state]
    c_rows = convolved[:, channels + n_state :]
    c_ref[...] = c_rows
    step, log_decay, cumulative = step_and_logs(dt_ref[...], rate_ref[...])
    across, _ = segments(meta_ref, base, (1, length), 1)
    lane = iota(cumulative.shape, 1)
    before = cumulative - log_decay
    seed = jnp.zeros_like(cumulative)
    for k in range(BR_PER):
        first = jnp.sum(jnp.where(lane == meta_ref[base + k], before, 0.0), axis=1, keepdims=True)
        seed = jnp.where(across == k, jnp.exp(jnp.where(across == k, cumulative - first, 0.0)), seed)
    gate = silu(z_ref[...].astype(F32))
    scale_ref[...] = expand(seed.T, channels // seed.shape[0]) * gate
    scores = lax.dot_general(c_rows, b_rows, (((1,), (1,)), ((), ())), preferred_element_type=F32)
    mask = (segment == across) & (segment < BR_PER)
    mask = mask & (iota((length, length), 1) <= iota((length, length), 0))
    extra = values.astype(F32) * skip_ref[...]
    mixed_rows(values, scores, step, cumulative, mask, y_ref, extra, gate)


def gate_kernel(
    meta_ref, y_ref, scale_ref, c_ref, by_ref, bscale_ref, bc_ref, back_ref,
    g_ref, bg_ref, sq_ref, *, base,
):
    length, channels = y_ref.shape
    n_ctx, _, n_state = back_ref.shape
    rows = channels // n_ctx

    def from_state(c_rows, which):
        state = back_ref[:, which * rows : (which + 1) * rows, :].reshape(channels, n_state)
        return lax.dot_general(c_rows, state, (((1,), (1,)), ((), ())), preferred_element_type=F32)

    def squares(gated):
        square = gated * gated
        total = square[:, :n_state]
        for at in range(n_state, channels, n_state):
            total = total + square[:, at : at + n_state]
        ones = jnp.ones((8, n_state), F32)
        return lax.dot_general(
            ones, total, (((1,), (1,)), ((), ())), precision=HIGH, preferred_element_type=F32
        )

    gated = y_ref[...] + scale_ref[...] * from_state(c_ref[...], 0)
    g_ref[...] = gated
    sums = squares(gated)
    segment, _ = segments(meta_ref, base, (length, 1), 0)
    c_rows = bc_ref[...]
    seeded = from_state(c_rows, BR_PER)
    for k in range(BR_PER - 1):
        seeded = jnp.where(segment == k, from_state(c_rows, 1 + k), seeded)
    gated = by_ref[...] + bscale_ref[...] * seeded
    bg_ref[...] = gated
    more = squares(gated)
    half = length // 2
    row = iota((8, half), 0)
    packed = jnp.where(
        row == 0,
        sums[:, :half],
        jnp.where(row == 1, sums[:, half:], jnp.where(row == 2, more[:, :half], more[:, half:])),
    )
    for i in range(sq_ref.shape[0]):
        sq_ref[i] = packed


def norm_kernel(meta_ref, sq_ref, g_ref, bg_ref, gain_ref, out_ref, bout_ref, *, base):
    length, channels = g_ref.shape
    n_tp = sq_ref.shape[0]
    total = sq_ref[0]
    for i in range(1, n_tp):
        total = total + sq_ref[i]
    factor = lax.rsqrt(total / (channels * n_tp) + EPSILON).T
    gain = gain_ref[...]
    half = length // 2
    segment, _ = segments(meta_ref, base, (length, 1), 0)
    for k in range(2):
        rows = slice(k * half, (k + 1) * half)
        out_ref[rows] = (g_ref[rows] * factor[:, k : k + 1] * gain).astype(BF)
        scaled = bg_ref[rows] * factor[:, 2 + k : 3 + k] * gain
        bout_ref[rows] = jnp.where(segment[rows] < BR_PER, scaled, 0.0).astype(BF)


def call(kernel, outs, scratch, args, smem=0, smem_out=False, grid=False):
    def where(scalar, shape):
        if grid and not scalar:
            return pl.BlockSpec(shape, lambda _, n=len(shape): (0,) * n)
        return pl.BlockSpec(memory_space=pltpu.SMEM if scalar else pltpu.VMEM)

    return pl.pallas_call(
        kernel,
        grid=(1,) if grid else (),
        in_specs=[where(i < smem, a.shape) for i, a in enumerate(args)],
        out_specs=[where(smem_out and i == 0, s) for i, (s, _) in enumerate(outs)],
        out_shape=[jax.ShapeDtypeStruct(s, t) for s, t in outs],
        scratch_shapes=[(pltpu.SMEM if len(s) == 1 else pltpu.VMEM)(s, t) for s, t in scratch],
        compiler_params=pltpu.CompilerParams(vmem_limit_bytes=24 * 2**20),
        cost_estimate=pl.CostEstimate(flops=2 * 10**9, bytes_accessed=4 * 10**6, transcendentals=10**6),
    )(*args)


def more_states(xc, b_rows, step, cumulative, positions, n_ctx):
    length, channels = xc.shape
    heads = step.shape[0]
    n_state = b_rows.shape[1]
    row = jnp.arange(length, dtype=I32)
    hit = row[None, None, :] == positions[:, None, None]
    ends = jnp.sum(jnp.where(hit, cumulative[None], 0.0), axis=2)
    inside = (row[None, :] <= positions[:, None])[:, None, :]
    weight = jnp.exp(jnp.where(inside, ends[:, :, None] - cumulative[None], FAR)) * step[None]
    values = xc.reshape(length, heads, -1).astype(F32)
    weighted = (jnp.transpose(weight, (0, 2, 1))[:, :, :, None] * values[None]).astype(BF)
    states = jnp.einsum("jshp,sn->jhpn", weighted, b_rows, preferred_element_type=F32).astype(BF)
    rows = channels // n_ctx
    count = positions.shape[0]
    states = jnp.transpose(states.reshape(count, n_ctx, rows, n_state), (1, 0, 2, 3))
    parts = []
    rest = ends
    for _ in range(3):
        part = lax.reduce_precision(rest, 8, 7)
        parts.append(part)
        rest = rest - part
    logs = jnp.stack(parts, axis=1).reshape(3 * count, heads).T
    logs = jnp.repeat(logs, n_ctx // heads, axis=0)
    logs = jnp.broadcast_to(logs[:, :, None], (n_ctx, 3 * count, n_state)).astype(BF)
    sent = jnp.concatenate([states.reshape(n_ctx, count * rows, n_state), logs], axis=1)
    return jnp.pad(sent, ((0, 0), (0, -sent.shape[1] % 16), (0, 0)))


def body(
    prefix_x, prefix_z, prefix_bc, prefix_dt, branch_x, branch_z, branch_bc, branch_dt,
    conv_x, conv_bc, decay_rate, skip, norm_gain, bound_pos, branch_owner, branch_parent, branch_len,
):
    n_ctx = lax.axis_size("ctx")
    n_tp = lax.axis_size("tp")
    me = lax.axis_index("ctx")
    length, channels = prefix_x.shape
    heads = decay_rate.shape[0]
    width = prefix_bc.shape[1]
    n_state = width // 2
    rows = channels // n_ctx
    bounds = bound_pos.shape[0]
    branches = branch_owner.shape[0]
    tail = conv_x.shape[0] - 1
    onward = [(i, i + 1) for i in range(n_ctx - 1)]

    own = jnp.concatenate([prefix_bc, branch_bc], axis=1)
    spread = jnp.broadcast_to(own[None], (n_tp, *own.shape))
    gathered = lax.all_to_all(spread, "tp", 0, 0, tiled=True).reshape(length, 2 * width)
    rates = decay_rate[:, None]
    skips = jnp.repeat(skip, channels // heads)[None]
    gain = norm_gain[None]
    order = jnp.arange(bounds, dtype=I32)
    block_of = bound_pos // length
    slot_of = jnp.sum(
        ((block_of[:, None] == block_of[None, :]) & (order[None, :] < order[:, None])).astype(I32), axis=1
    )

    at_tails = branches + 2 * bounds
    at_positions = at_tails + bounds
    at_mine = at_positions + SLOTS
    xrows = 8 * channels // n_state
    meta, xtails, last = call(
        functools.partial(index_kernel, n_ctx=n_ctx, n_state=n_state),
        [((at_mine + 2 * BR_PER,), I32), ((n_ctx, xrows, n_state), BF), ((HALO, channels), BF)],
        [((2 * n_ctx,), I32), ((branches,), I32), ((branches,), I32), ((bounds, 8, channels), F32)],
        [jnp.full((1,), me, I32), bound_pos, branch_owner, branch_parent, branch_len, prefix_x],
        smem=5,
        smem_out=True,
    )
    xc, cumulative, step, weighted, first, logs = call(
        functools.partial(prefix_x_kernel, base=at_positions),
        [
            ((length, channels), BF),
            ((heads, length), F32),
            ((heads, length), F32),
            ((1 + SLOTS, length, channels), BF),
            ((1 + SLOTS, HALO, channels), F32),
            ((heads, n_state), F32),
        ],
        [((HALO + length, channels), F32)],
        [meta, prefix_x, prefix_dt, rates, conv_x],
        smem=1,
    )
    gathered, weighted, last = lax.optimization_barrier((gathered, weighted, last))
    halo = lax.ppermute(
        jnp.concatenate([last, gathered[length - HALO :, :width]], axis=1), "ctx", onward
    )
    part, misc, convolved = call(
        functools.partial(prefix_later_kernel, base=at_positions, tail_base=at_tails),
        [
            ((1 + SLOTS, channels, n_state), F32),
            ((n_ctx, xrows + 16, n_state), BF),
            ((length, width), BF),
        ],
        [((length, width), F32), ((bounds, 8, width), F32)],
        [meta, gathered, conv_bc, weighted, logs, xtails],
        smem=1,
    )
    sent, b_rows, c_rows, xfirst = call(
        functools.partial(prefix_state_kernel, base=at_positions),
        [
            ((n_ctx, xrows + 16 + (1 + SLOTS) * rows, n_state), BF),
            ((length, n_state), BF),
            ((length, n_state), BF),
            ((HALO, channels), BF),
        ],
        [((2 * HALO, width), F32), ((2 * HALO, channels), F32)],
        [meta, prefix_x, halo, conv_x, gathered, conv_bc, first, part, misc, convolved],
        smem=1,
    )
    got = lax.all_to_all(sent, "ctx", 0, 0, tiled=True)
    y, scale = call(
        prefix_mix_kernel,
        [((length, channels), F32), ((length, channels), F32)],
        [],
        [xc, xfirst, b_rows, c_rows, cumulative, step, skips, prefix_z],
    )

    scan = functools.partial(scan_kernel, n_branch=branches, bounds=bounds)
    scan_out = [((n_ctx, (1 + BR_PER) * rows, n_state), BF)]
    scan_scratch = [
        ((n_ctx, rows, n_state), F32),
        ((bounds, rows, n_state), F32),
        ((1 + SLOTS, n_ctx, n_state), F32),
    ]

    def usual():
        return call(scan, scan_out, scan_scratch, [meta, got], smem=1, grid=True)[0]

    def crowded():
        here = (block_of == me)[None, :] & (slot_of[None, :] == order[SLOTS:, None])
        positions = jnp.sum(jnp.where(here, (bound_pos - block_of * length + 1)[None, :], 0), axis=1) - 1
        whole = jnp.concatenate([xfirst, xc[HALO:]], axis=0)
        extra = more_states(whole, b_rows, step, cumulative, positions, n_ctx)
        extra = lax.all_to_all(extra, "ctx", 0, 0, tiled=True)
        return call(scan, scan_out, scan_scratch, [meta, got, extra], smem=1)[0]

    back = lax.cond(jnp.max(slot_of) >= SLOTS, crowded, usual)
    back = lax.all_to_all(back, "ctx", 0, 0, tiled=True)

    branch_y, branch_c, branch_scale = call(
        functools.partial(branch_kernel, base=at_mine),
        [((length, channels), F32), ((length, n_state), BF), ((length, channels), F32)],
        [((HALO + length, channels + width), F32)],
        [meta, branch_x, gathered, got, branch_dt, rates, conv_x, conv_bc, skips, branch_z],
        smem=1,
    )
    gated, branch_gated, squares = call(
        functools.partial(gate_kernel, base=at_mine),
        [((length, channels), F32), ((length, channels), F32), ((n_tp, 8, length // 2), F32)],
        [],
        [meta, y, scale, c_rows, branch_y, branch_scale, branch_c, back],
        smem=1,
    )
    squares = lax.all_to_all(squares, "tp", 0, 0, tiled=True)
    return tuple(
        call(
            functools.partial(norm_kernel, base=at_mine),
            [((length, channels), BF), ((length, channels), BF)],
            [],
            [meta, squares, gated, branch_gated, gain],
            smem=1,
            grid=True,
        )
    )


def solution(mesh):
    both = P(("ctx", "tp"), None)
    in_specs = (
        P("ctx", "tp"), P("ctx", "tp"), both, P("tp", "ctx"),
        P("ctx", "tp"), P("ctx", "tp"), both, P("tp", "ctx"),
        P(None, "tp"), P(), P("tp"), P("tp"), P("tp"), P(), P(), P(), P(),
    )
    out_specs = (P("ctx", "tp"), P("ctx", "tp"))
    return jax.shard_map(body, mesh=mesh, in_specs=in_specs, out_specs=out_specs, check_vma=False)
```
